32 devices in a mesh: dp: 16 (over z, y, x), tp: 2 (over core).
Axes of the slice: x: 2, y: 2, z: 4, core: 2. Of those that a mesh axis runs over, the one named last changes fastest.
Arguments:
- inputs: bfloat16 [16384, 768], P('dp'), may hold values from -6 to 6
- cotangent: bfloat16 [16384, 768], P(('dp', 'tp')), may hold values from -6 to 6
- seq_lengths: int32 [16, 2], P('dp'), may hold values from 0 to 1024, as said below
- timesteps: int32 [16, 2], P('dp'), may hold values from 0 to 1999
- time_w1: float32 [128, 768], P(None, ('dp', 'tp')), may hold values from -0.5 to 0.5
- time_b1: float32 [768], P(('dp', 'tp')), may hold values from -3 to 3
- time_w2: float32 [768, 768], P(('dp', 'tp')), may hold values from -0.21875 to 0.21875
- time_b2: float32 [768], P(('dp', 'tp')), may hold values from -3 to 3
- w_query: float32 [768, 768], P('dp', 'tp'), may hold values from -0.21875 to 0.21875
- b_query: float32 [768], P('tp'), may hold values from -3 to 3
- w_key: float32 [768, 768], P('dp', 'tp'), may hold values from -0.21875 to 0.21875
- w_value: float32 [768, 768], P('dp', 'tp'), may hold values from -0.21875 to 0.21875
- b_value: float32 [768], P('tp'), may hold values from -3 to 3
- w_out: float32 [768, 768], P('tp', 'dp'), may hold values from -2.5 to 2.5
- b_out: float32 [768], P(('dp', 'tp')), may hold values from -3 to 3
- norm1_gain: float32 [768], P(('dp', 'tp')), may hold values from 0.5 to 1.5
- norm1_bias: float32 [768], P(('dp', 'tp')), may hold values from -3 to 3
- w_up: float32 [768, 3072], P('dp', 'tp'), may hold values from -0.21875 to 0.21875
- b_up: float32 [3072], P('tp'), may hold values from -3 to 3
- w_down: float32 [3072, 768], P('tp', 'dp'), may hold values from -0.109375 to 0.109375
- b_down: float32 [768], P(('dp', 'tp')), may hold values from -3 to 3
- norm2_gain: float32 [768], P(('dp', 'tp')), may hold values from 0.5 to 1.5
- norm2_bias: float32 [768], P(('dp', 'tp')), may hold values from -3 to 3
Outputs:
- outputs: bfloat16 [16384, 768], P(('dp', 'tp'))
- input_grad: float32 [16384, 768], P('dp')
- grad_time_w1: float32 [128, 768], P(None, ('dp', 'tp'))
- grad_time_b1: float32 [768], P(('dp', 'tp'))
- grad_time_w2: float32 [768, 768], P(('dp', 'tp'))
- grad_time_b2: float32 [768], P(('dp', 'tp'))
- grad_w_query: float32 [768, 768], P('dp', 'tp')
- grad_b_query: float32 [768], P('tp')
- grad_w_key: float32 [768, 768], P('dp', 'tp')
- grad_w_value: float32 [768, 768], P('dp', 'tp')
- grad_b_value: float32 [768], P('tp')
- grad_w_out: float32 [768, 768], P('tp', 'dp')
- grad_b_out: float32 [768], P(('dp', 'tp'))
- grad_norm1_gain: float32 [768], P(('dp', 'tp'))
- grad_norm1_bias: float32 [768], P(('dp', 'tp'))
- grad_w_up: float32 [768, 3072], P('dp', 'tp')
- grad_b_up: float32 [3072], P('tp')
- grad_w_down: float32 [3072, 768], P('tp', 'dp')
- grad_b_down: float32 [768], P(('dp', 'tp'))
- grad_norm2_gain: float32 [768], P(('dp', 'tp'))
- grad_norm2_bias: float32 [768], P(('dp', 'tp'))
The draws below stay inside these ranges and needn't reach their ends.
Inputs may be any that keep to these rules, and one draw needn't show every extreme that they name: Group g's first sequence fills rows 0 to seq_lengths[g,0] - 1 and its second the next seq_lengths[g,1] rows; the remaining rows of the group are padding. Either the second length is 0 and the first exceeds 1024 / 2, or both lie between 256 and 512 with a sum over 512. Some group holds one sequence of exactly 1024.
All inputs are finite; a program needn't handle non-finite values.
Results may differ from the reference program's by a relative error of at most 0.025.
The reference program's roundings to bfloat16 on the way count: a program that leaves them out, or rounds other values in their place, can miss the bound.
Values may be sent and summed in bfloat16 or wider, within the bound.
A program may use at most 128 MiB of HBM per device.

```python
import math
import jax
import jax.numpy as jnp
from jax import lax

D = 768
H = 12
HD = 64
FF = 3072
TE = 128
SEQ_LEN = 1024
TOKENS = 16384
N_DP = 16


def draw_seq_lengths(key, part):
    key = jax.random.fold_in(key, 7)
    quarter = SEQ_LEN // 4
    key_kind, key_long, key_first, key_second, key_pick = jax.random.split(key, 5)
    is_long = jax.random.randint(key_kind, (N_DP,), 0, 2)
    long_len = jax.random.randint(key_long, (N_DP,), 2 * quarter + 1, 4 * quarter + 1)
    first_short = jax.random.randint(key_first, (N_DP,), quarter + 1, 2 * quarter + 1)
    second_short = jax.random.randint(key_second, (N_DP,), quarter, 2 * quarter + 1)
    chosen = jax.random.randint(key_pick, (), 0, N_DP)
    forced = jnp.arange(N_DP) == chosen
    is_long = jnp.where(forced, 1, is_long)
    long_len = jnp.where(forced, 4 * quarter, long_len)
    first_len = jnp.where(is_long == 1, long_len, first_short)
    second_len = jnp.where(is_long == 1, 0, second_short)
    return jnp.stack([first_len, second_len], axis=1).astype(jnp.int32)


def place_ends(values, stream_key, low, top_value):
    index_at = [jax.random.randint(jax.random.fold_in(stream_key, axis), (), 0, length) for axis, length in enumerate(values.shape)]
    widest = values.shape.index(max(values.shape))
    neighbour = index_at[:widest] + [(index_at[widest] + 1) % values.shape[widest]] + index_at[widest + 1:]
    return values.at[tuple(index_at)].set(low).at[tuple(neighbour)].set(top_value)


def shard_levels(own_key, extent, cuts, low, high):
    loudness = 1.0
    for dim, blocks in cuts:
        heights = jax.random.uniform(jax.random.fold_in(jax.random.fold_in(own_key, 6), dim), (blocks,), jnp.float32, low / len(cuts), high / len(cuts))
        loudness = loudness * jnp.repeat(jnp.exp(heights), extent[dim] // blocks).reshape((-1,) + (1,) * (len(extent) - 1 - dim))
    return loudness


def scatter_about(own_key, shape, scale, bound, pieces=(), kind=jnp.bfloat16):
    entries = scale * jax.random.normal(own_key, shape, jnp.float32)
    if pieces:
        entries = entries * shard_levels(own_key, shape, pieces, -0.22, 0.18)
    return jnp.clip(entries, -bound, bound).astype(kind)


def setup_inputs(seed: int = 0) -> dict:
    key_list = jax.random.split(jax.random.key(seed), 24)
    inputs = scatter_about(key_list[0], (TOKENS, D), 1.0, 6.0, ((0, 16),))
    cotangent = scatter_about(key_list[1], (TOKENS, D), 1.0, 6.0, ((0, 32),))
    seq_lengths = draw_seq_lengths(jax.random.fold_in(key_list[23], 71), 0)
    timesteps = place_ends(jax.random.randint(key_list[3], (N_DP, 2), 0, 2000), jax.random.fold_in(key_list[3], 1), 0, 1999).astype(jnp.int32)
    time_w1 = scatter_about(key_list[4], (TE, D), TE ** -0.5, 0.5, ((1, 32),), jnp.float32)
    time_b1 = scatter_about(key_list[5], (D,), 0.5, 3.0, ((0, 32),), jnp.float32)
    time_w2 = scatter_about(key_list[6], (D, D), D ** -0.5, 0.21875, ((0, 32),), jnp.float32)
    time_b2 = scatter_about(key_list[7], (D,), 0.5, 3.0, ((0, 32),), jnp.float32)
    w_query = scatter_about(key_list[8], (D, D), D ** -0.5, 0.21875, ((0, 16), (1, 2)), jnp.float32)
    b_query = scatter_about(key_list[9], (D,), 0.5, 3.0, ((0, 2),), jnp.float32)
    w_key = scatter_about(key_list[10], (D, D), D ** -0.5, 0.21875, ((0, 16), (1, 2)), jnp.float32)
    w_value = scatter_about(key_list[11], (D, D), D ** -0.5, 0.21875, ((0, 16), (1, 2)), jnp.float32)
    b_value = scatter_about(key_list[12], (D,), 0.5, 3.0, ((0, 2),), jnp.float32)
    w_out = scatter_about(key_list[13], (D, D), (max(1, 8 * D // SEQ_LEN)) ** -0.5, 2.5, ((0, 2), (1, 16)), jnp.float32)
    b_out = scatter_about(key_list[14], (D,), 0.5, 3.0, ((0, 32),), jnp.float32)
    norm1_gain = jnp.clip(1.0 + 0.1 * jax.random.normal(key_list[15], (D,), jnp.float32), 0.5, 1.5)
    norm1_bias = scatter_about(key_list[16], (D,), 0.5, 3.0, ((0, 32),), jnp.float32)
    w_up = scatter_about(key_list[17], (D, FF), D ** -0.5, 0.21875, ((0, 16), (1, 2)), jnp.float32)
    b_up = scatter_about(key_list[18], (FF,), 0.5, 3.0, ((0, 2),), jnp.float32)
    w_down = scatter_about(key_list[19], (FF, D), FF ** -0.5, 0.109375, ((0, 2), (1, 16)), jnp.float32)
    b_down = scatter_about(key_list[20], (D,), 0.5, 3.0, ((0, 32),), jnp.float32)
    norm2_gain = jnp.clip(1.0 + 0.1 * jax.random.normal(key_list[21], (D,), jnp.float32), 0.5, 1.5)
    norm2_bias = scatter_about(key_list[22], (D,), 0.5, 3.0, ((0, 32),), jnp.float32)
    return dict(inputs=inputs, cotangent=cotangent, seq_lengths=seq_lengths, timesteps=timesteps, time_w1=time_w1, time_b1=time_b1, time_w2=time_w2, time_b2=time_b2, w_query=w_query, b_query=b_query, w_key=w_key, w_value=w_value, b_value=b_value, w_out=w_out, b_out=b_out, norm1_gain=norm1_gain, norm1_bias=norm1_bias, w_up=w_up, b_up=b_up, w_down=w_down, b_down=b_down, norm2_gain=norm2_gain, norm2_bias=norm2_bias)


@jax.custom_vjp
def low(v):
    return lax.optimization_barrier(v.astype(jnp.bfloat16)).astype(jnp.float32)

@jax.custom_vjp
def low_back(v):
    return v

def low_keep(v):
    return (low(v), None)

def low_pass(kept, grad):
    return (grad,)

def back_keep(v):
    return (v, None)

def back_low(kept, grad):
    return (low(grad),)
low.defvjp(low_keep, low_pass)
low_back.defvjp(back_keep, back_low)
highest = lax.Precision.HIGHEST
epsilon = 1e-05

def matmul(left_side, right_side):
    return jnp.dot(left_side, right_side, precision=highest, preferred_element_type=jnp.float32)

def time_features(time_steps, feature_width):
    half_width = feature_width // 2
    frequency = jnp.exp(-math.log(10000.0) * jnp.arange(half_width, dtype=jnp.float32) / half_width)
    angles = time_steps.astype(jnp.float32)[:, None] * frequency[None, :]
    return jnp.concatenate([jnp.cos(angles), jnp.sin(angles)], axis=1)

def segment_ids(lengths, row_count):
    row_index = jnp.arange(row_count, dtype=jnp.int32)
    inner = jnp.where(row_index < lengths[0] + lengths[1], 1, 2)
    return jnp.where(row_index < lengths[0], 0, inner).astype(jnp.int32)

def layer_norm(summed, gain_row, shift_row):
    centered = summed - lax.optimization_barrier(jnp.mean(summed, axis=-1, keepdims=True))
    variance = lax.optimization_barrier(jnp.mean(centered * centered, axis=-1, keepdims=True))
    return centered * lax.rsqrt(variance + epsilon) * gain_row + shift_row

def attention(query_rows, key_rows, value_rows, segment):
    rows_total = query_rows.shape[0]
    block_rows = min(512, rows_total)
    factor = 1.0 / math.sqrt(HD)
    query_heads = query_rows.reshape(rows_total // block_rows, block_rows, H, HD)
    key_heads = key_rows.reshape(rows_total, H, HD)
    value_heads = value_rows.reshape(rows_total, H, HD)
    seg_blocks = segment.reshape(rows_total // block_rows, block_rows)

    def one_block(item):
        query_blk, seg_blk = item
        scores = low_back(jnp.einsum('qhd,khd->hqk', query_blk, key_heads, precision=highest) * factor)
        allowed = seg_blk[:, None] == segment[None, :]
        scores = jnp.where(allowed[None], scores, -1e+30)
        row_max = lax.optimization_barrier(jnp.max(scores, axis=-1, keepdims=True))
        exp_scores = jnp.exp(scores - row_max)
        prob_weights = low(exp_scores / lax.optimization_barrier(jnp.sum(exp_scores, axis=-1, keepdims=True)))
        return jnp.einsum('hqk,khd->qhd', prob_weights, value_heads, precision=highest)
    mixed_heads = lax.map(jax.checkpoint(one_block), (query_heads, seg_blocks))
    return mixed_heads.reshape(rows_total, H * HD)

def layer_forward(params, inputs_f, segment, time_steps):
    time_w1, time_b1, time_w2, time_b2, w_query, b_query, w_key, w_value, b_value, w_out, b_out, norm1_gain, norm1_bias, w_up, b_up, w_down, b_down, norm2_gain, norm2_bias = params
    features = low(time_features(time_steps, TE))
    time_hidden = low(jax.nn.silu(matmul(features, low(time_w1)) + time_b1))
    time_embed = matmul(time_hidden, low(time_w2)) + time_b2
    picker = (segment[:, None] == jnp.arange(2, dtype=jnp.int32)[None, :]).astype(jnp.float32)
    base_rows = inputs_f + matmul(picker, time_embed)
    base_low = low(base_rows)
    query_rows = low(low_back(matmul(base_low, low(w_query)) + b_query))
    key_rows = low(low_back(matmul(base_low, low(w_key))))
    value_rows = low(low_back(matmul(base_low, low(w_value)) + b_value))
    mixed_rows = low(low_back(attention(query_rows, key_rows, value_rows, segment)))
    attn_out = low_back(matmul(mixed_rows, low(w_out))) + b_out
    first_norm = layer_norm(base_rows + attn_out, norm1_gain, norm1_bias)
    up_pre = low_back(matmul(low(first_norm), low(w_up))) + b_up
    up_act = low(jax.nn.gelu(up_pre))
    ffn_out = low_back(matmul(up_act, low(w_down))) + b_down
    return layer_norm(first_norm + ffn_out, norm2_gain, norm2_bias)

def reference(inputs, cotangent, seq_lengths, timesteps, time_w1, time_b1, time_w2, time_b2, w_query, b_query, w_key, w_value, b_value, w_out, b_out, norm1_gain, norm1_bias, w_up, b_up, w_down, b_down, norm2_gain, norm2_bias):
    params = (time_w1.astype(jnp.float32), time_b1.astype(jnp.float32), time_w2.astype(jnp.float32), time_b2.astype(jnp.float32), w_query.astype(jnp.float32), b_query.astype(jnp.float32), w_key.astype(jnp.float32), w_value.astype(jnp.float32), b_value.astype(jnp.float32), w_out.astype(jnp.float32), b_out.astype(jnp.float32), norm1_gain.astype(jnp.float32), norm1_bias.astype(jnp.float32), w_up.astype(jnp.float32), b_up.astype(jnp.float32), w_down.astype(jnp.float32), b_down.astype(jnp.float32), norm2_gain.astype(jnp.float32), norm2_bias.astype(jnp.float32))
    group_inputs = inputs.astype(jnp.float32).reshape(N_DP, SEQ_LEN, D)
    group_cot = cotangent.astype(jnp.float32).reshape(N_DP, SEQ_LEN, D)

    def one_group(totals, item):
        inputs_grp, cot_grp, lengths, time_steps = item
        segment = segment_ids(lengths, SEQ_LEN)
        valid = (segment < 2).astype(jnp.float32)

        def forward(prm, inputs_f):
            return layer_forward(prm, inputs_f, segment, time_steps)
        result, pullback = jax.vjp(forward, params, inputs_grp)
        grad_params, grad_inputs = pullback(cot_grp * valid[:, None])
        totals = jax.tree.map(lambda left_side, right_side: left_side + right_side, totals, grad_params)
        return (totals, (result.astype(jnp.bfloat16), grad_inputs))
    zeros_init = jax.tree.map(jnp.zeros_like, params)
    totals, (result_rows, grad_rows) = lax.scan(one_group, zeros_init, (group_inputs, group_cot, seq_lengths, timesteps))
    return (result_rows.reshape(TOKENS, D), grad_rows.reshape(TOKENS, D), totals[0], totals[1], totals[2], totals[3], totals[4], totals[5], totals[6], totals[7], totals[8], totals[9], totals[10], totals[11], totals[12], totals[13], totals[14], totals[15], totals[16], totals[17], totals[18])
```

```python
import functools
import math

import jax
import jax.numpy as jnp
from jax import lax
from jax.experimental import pallas as pl
from jax.experimental.pallas import tpu as pltpu
from jax.sharding import PartitionSpec as P

HD = 64
TE = 128
SUPER = 16

epsilon = 1e-05
highest = lax.Precision.HIGHEST
f32 = jnp.float32
bf16 = jnp.bfloat16


class Place:
    def __init__(self, sub):
        self.sub = sub
        index = lax.axis_index("dp")
        self.low = lax.rem(index, sub)
        self.place = lax.div(index, sub)
        self.z = lax.div(self.place, 4)
        self.p = lax.rem(self.place, 4)
        self.r = self.ring(self.p)

    @staticmethod
    def ring(v):
        half = lax.div(v, 2)
        return 2 * half + lax.rem(lax.rem(v, 2) + half, 2)

    def spot(self, dz, dr):
        z = lax.rem(self.z + dz + 4, 4)
        p = self.ring(lax.rem(self.r + dr + 4, 4))
        return z * 4 + p

    def device(self, dz, dr):
        return {"dp": self.spot(dz, dr) * self.sub + self.low}

    def other(self):
        return {"tp": 1 - lax.axis_index("tp")}

    def rows(self, dz, dr, count):
        return pl.ds(pl.multiple_of(self.spot(dz, dr) * count, 16), count)

    def enter(self):
        barrier = pltpu.get_barrier_semaphore()
        for peer in (
            [self.device(d, 0) for d in (1, 2, 3)]
            + [self.device(0, d) for d in (1, 2, 3)]
            + [self.other()]
        ):
            pl.semaphore_signal(barrier, inc=1, device_id=peer, device_id_type=pl.DeviceIdType.MESH)
        pl.semaphore_wait(barrier, 7)


def remote(src, dst, send, recv, device):
    return pltpu.make_async_remote_copy(
        src_ref=src,
        dst_ref=dst,
        send_sem=send,
        recv_sem=recv,
        device_id=device,
        device_id_type=pl.DeviceIdType.MESH,
    )


class Gather:
    def __init__(self, place, shard, full, send, recv, g):
        rows = shard.shape[0]
        at = lambda dz, dr: full.at[place.rows(dz, dr, rows), :]
        self.place, self.shard, self.full, self.count = place, shard, full, rows
        self.to_planes = [
            remote(shard, at(0, 0), send.at[g, d - 1], recv.at[g, d - 1], place.device(d, 0))
            for d in (1, 2, 3)
        ]
        self.around = []
        self.relay = []
        for d in range(4):
            source = shard if d == 0 else at(-d, 0)
            self.around.append(
                [
                    remote(
                        source,
                        at(-d, 0),
                        send.at[g, 3 + 2 * d + k],
                        recv.at[g, 3 + 2 * d + k],
                        place.device(0, 1 - 2 * k),
                    )
                    for k in (0, 1)
                ]
            )
            k = d // 2
            self.relay.append(
                remote(
                    at(-d, 2 * k - 1),
                    at(-d, 2 * k - 1),
                    send.at[g, 11 + d],
                    recv.at[g, 11 + d],
                    place.device(0, 1 - 2 * k),
                )
            )

    def begin(self):
        for copy in self.to_planes:
            copy.start()
        for copy in self.around[0]:
            copy.start()
        self.full[self.place.rows(0, 0, self.count), :] = self.shard[...]

    def turn(self, d):
        if d:
            self.to_planes[d - 1].wait_recv()
            for copy in self.around[d]:
                copy.start()

    def pass_on(self, d):
        k = d // 2
        self.around[d][k].wait_recv()
        self.relay[d].start()

    def finish(self):
        for d in range(4):
            self.around[d][1 - d // 2].wait_recv()
            self.relay[d].wait_recv()

    def drain(self):
        for copy in self.to_planes + [c for pair in self.around for c in pair] + self.relay:
            copy.wait_send()


class Reduce:
    def __init__(self, place, grads, total, first, second, third, joined, across, send, recv, g):
        rows = total.shape[0]
        at = lambda dz, dr: grads.at[place.rows(dz, dr, rows), :]
        self.place, self.grads, self.total, self.rows = place, grads, total, rows
        self.first, self.second, self.third, self.joined, self.across = first, second, third, joined, across
        self.far, self.near, self.up = [], [], []
        for d in range(4):
            k = d // 2
            self.far.append(
                remote(
                    at(d, 2), first.at[d], send.at[g, d], recv.at[g, d], place.device(0, 1 - 2 * k)
                )
            )
            pair = []
            for j in (0, 1):
                source = joined.at[d] if j == k else at(d, 1 - 2 * j)
                pair.append(
                    remote(
                        source,
                        second.at[j * 4 + d],
                        send.at[g, 4 + 2 * d + j],
                        recv.at[g, 4 + 2 * d + j],
                        place.device(0, 1 - 2 * j),
                    )
                )
            self.near.append(pair)
        for d in (1, 2, 3):
            self.up.append(
                remote(
                    across.at[d - 1],
                    third.at[d - 1],
                    send.at[g, 11 + d],
                    recv.at[g, 11 + d],
                    place.device(d, 0),
                )
            )

    def block(self, dz, dr):
        return self.grads[self.place.rows(dz, dr, self.rows), :].astype(f32)

    def begin(self):
        for d in range(4):
            self.far[d].start()
        for d in range(4):
            self.near[d][1 - d // 2].start()

    def join(self, d):
        k = d // 2
        self.far[d].wait_recv()
        self.joined[d] = (self.first[d].astype(f32) + self.block(d, 1 - 2 * k)).astype(bf16)
        self.near[d][k].start()

    def cross(self, d):
        for j in (0, 1):
            self.near[d][j].wait_recv()
        summed = self.block(d, 0) + self.second[d].astype(f32) + self.second[4 + d].astype(f32)
        if d:
            self.across[d - 1] = summed.astype(bf16)
            self.up[d - 1].start()
        else:
            self.total[...] = summed

    def finish(self):
        for copy in self.up:
            copy.wait_recv()
        self.total[...] += (
            self.third[0].astype(f32) + self.third[1].astype(f32) + self.third[2].astype(f32)
        )

    def drain(self):
        for copy in self.far + [c for pair in self.near for c in pair] + self.up:
            copy.wait_send()


class Spread:
    def __init__(self, place, along, sources, slots, send, recv, base):
        if along == "tp":
            self.copies = [remote(sources[0], slots, send.at[base], recv.at[base], place.other())]
            return
        self.copies = [
            remote(
                sources[d - 1],
                slots.at[d - 1],
                send.at[base + d - 1],
                recv.at[base + d - 1],
                place.device(d, 0) if along == "z" else place.device(0, d),
            )
            for d in (1, 2, 3)
        ]

    def start(self):
        for copy in self.copies:
            copy.start()

    def wait(self):
        for copy in self.copies:
            copy.wait_recv()

    def drain(self):
        for copy in self.copies:
            copy.wait_send()


def gather_kernel(
    sub,
    w0, w1, w2, w3, feats, vectors, tw1, tb1, tw2,
    f0, f1, f2, f3, all_feats, embed, shared,
    feat_z, feat_sum, feat_in, part, part_in, part_sum, part_z, part_zsum, part_tp,
    send, recv, small_send, small_recv,
):
    place = Place(sub)
    place.enter()
    seqs = feats.shape[0]
    spread_z = Spread(place, "z", [feats] * 3, feat_z, small_send, small_recv, 0)
    spread_z.start()
    gathers = [
        Gather(place, shard, full, send, recv, g)
        for g, (shard, full) in enumerate(((w0, f0), (w1, f1), (w2, f2), (w3, f3)))
    ]
    for one in gathers:
        one.begin()
    spread_z.wait()
    feat_sum[...] = feats[...] + feat_z[0] + feat_z[1] + feat_z[2]
    spread_r = Spread(place, "r", [feat_sum] * 3, feat_in, small_send, small_recv, 3)
    spread_r.start()
    all_feats[0] = feat_sum[...]
    spread_r.wait()
    for d in (1, 2, 3):
        all_feats[d] = feat_in[d - 1]
    every = all_feats[...].reshape(4 * seqs, TE)
    before = (
        jnp.dot(every.astype(bf16), tw1[...].astype(bf16), preferred_element_type=f32) + tb1[...]
    )
    hidden = jax.nn.silu(before).astype(bf16)
    share = jnp.dot(hidden, tw2[...].astype(bf16), preferred_element_type=f32)
    for d in range(4):
        part[d, :seqs, :] = share[d * seqs : (d + 1) * seqs, :]
        part[d, seqs:, :] = vectors[...]
    back = Spread(
        place, "r", [part.at[3], part.at[2], part.at[1]], part_in, small_send, small_recv, 6
    )
    back.start()
    back.wait()
    part_sum[...] = part[0] + part_in[0] + part_in[1] + part_in[2]
    over_z = Spread(place, "z", [part_sum] * 3, part_z, small_send, small_recv, 9)
    over_z.start()
    over_z.wait()
    part_zsum[...] = part_sum[...] + part_z[0] + part_z[1] + part_z[2]
    pair = Spread(place, "tp", [part_zsum], part_tp, small_send, small_recv, 12)
    pair.start()
    pair.wait()
    both = part_zsum[...] + part_tp[...]
    shared[...] = both[seqs:]
    embed[...] = both[:seqs] + shared[0:1, :]
    for one in gathers:
        for d in (1, 2, 3):
            one.turn(d)
        for d in range(4):
            one.pass_on(d)
    for one in gathers:
        one.finish()
    for one in gathers:
        one.drain()
    for one in (spread_z, spread_r, back, over_z, pair):
        one.drain()


def reduce_kernel(
    sub,
    g0, g1, g2, g3, sums,
    t0, t1, t2, t3, all_sums, all_embed,
    *rest,
):
    buffers, (pair_in, pair_sum, z_in, z_sum, r_in, send, recv, small_send, small_recv) = rest[:20], rest[20:]
    place = Place(sub)
    place.enter()
    reduces = [
        Reduce(place, grads, total, *buffers[5 * g : 5 * g + 5], send, recv, g)
        for g, (grads, total) in enumerate(((g0, t0), (g1, t1), (g2, t2), (g3, t3)))
    ]
    pair = Spread(place, "tp", [sums], pair_in, small_send, small_recv, 0)
    pair.start()
    for one in reduces:
        one.begin()
    pair.wait()
    other = pair_in[...]
    row = lax.broadcasted_iota(jnp.int32, other.shape, 0)
    pair_sum[...] = sums[...] + jnp.where((row >= 8) & (row < 16), 0.0, other)
    over_z = Spread(place, "z", [pair_sum] * 3, z_in, small_send, small_recv, 1)
    over_z.start()
    over_z.wait()
    z_sum[...] = pair_sum[...] + z_in[0] + z_in[1] + z_in[2]
    over_r = Spread(place, "r", [z_sum] * 3, r_in, small_send, small_recv, 4)
    over_r.start()
    over_r.wait()
    all_sums[...] = z_sum[:16] + r_in[0, :16] + r_in[1, :16] + r_in[2, :16]
    all_embed[0] = z_sum[16:]
    for d in (1, 2, 3):
        all_embed[d] = r_in[d - 1, 16:]
    for one in reduces:
        for d in range(4):
            one.join(d)
    for one in reduces:
        for d in (1, 2, 3, 0):
            one.cross(d)
    for one in reduces:
        one.finish()
    for one in reduces:
        one.drain()
    for one in (pair, over_z, over_r):
        one.drain()


def vmem(count):
    return [pl.BlockSpec(memory_space=pltpu.VMEM)] * count


def call_gather(sub, shards, feats, vectors, tw1, tb1, tw2):
    seqs = feats.shape[0]
    width = vectors.shape[1]
    full = [jax.ShapeDtypeStruct((s.shape[0] * SUPER, s.shape[1]), bf16) for s in shards]
    small = seqs + 8
    return pl.pallas_call(
        functools.partial(gather_kernel, sub),
        out_shape=full
        + [
            jax.ShapeDtypeStruct((4, seqs, TE), f32),
            jax.ShapeDtypeStruct((seqs, width), f32),
            jax.ShapeDtypeStruct((8, width), f32),
        ],
        in_specs=vmem(9),
        out_specs=vmem(7),
        scratch_shapes=[
            pltpu.VMEM((3, seqs, TE), f32),
            pltpu.VMEM((seqs, TE), f32),
            pltpu.VMEM((3, seqs, TE), f32),
            pltpu.VMEM((4, small, width), f32),
            pltpu.VMEM((3, small, width), f32),
            pltpu.VMEM((small, width), f32),
            pltpu.VMEM((3, small, width), f32),
            pltpu.VMEM((small, width), f32),
            pltpu.VMEM((small, width), f32),
            pltpu.SemaphoreType.DMA((4, 15)),
            pltpu.SemaphoreType.DMA((4, 15)),
            pltpu.SemaphoreType.DMA((13,)),
            pltpu.SemaphoreType.DMA((13,)),
        ],
        compiler_params=pltpu.CompilerParams(
            collective_id=0, has_side_effects=True, vmem_limit_bytes=40 * 1024 * 1024
        ),
        name="gather_weights",
    )(*shards, feats, vectors, tw1, tb1, tw2)


def call_reduce(sub, grads, sums):
    rows = grads[0].shape[0] // SUPER
    width = sums.shape[1]
    seqs = sums.shape[0] - 16
    buffers = []
    for one in grads:
        for count in (4, 8, 3, 4, 3):
            buffers.append(pltpu.VMEM((count, rows, one.shape[1]), bf16))
    tall = sums.shape[0]
    return pl.pallas_call(
        functools.partial(reduce_kernel, sub),
        out_shape=[jax.ShapeDtypeStruct((rows, one.shape[1]), f32) for one in grads]
        + [
            jax.ShapeDtypeStruct((16, width), f32),
            jax.ShapeDtypeStruct((4, seqs, width), f32),
        ],
        in_specs=vmem(5),
        out_specs=vmem(6),
        scratch_shapes=buffers
        + [
            pltpu.VMEM((tall, width), f32),
            pltpu.VMEM((tall, width), f32),
            pltpu.VMEM((3, tall, width), f32),
            pltpu.VMEM((tall, width), f32),
            pltpu.VMEM((3, tall, width), f32),
            pltpu.SemaphoreType.DMA((4, 15)),
            pltpu.SemaphoreType.DMA((4, 15)),
            pltpu.SemaphoreType.DMA((7,)),
            pltpu.SemaphoreType.DMA((7,)),
        ],
        compiler_params=pltpu.CompilerParams(
            collective_id=1, has_side_effects=True, vmem_limit_bytes=48 * 1024 * 1024
        ),
        name="reduce_gradients",
    )(*grads, sums)


def time_features(time_steps, feature_width):
    half_width = feature_width // 2
    frequency = jnp.exp(-math.log(10000.0) * jnp.arange(half_width, dtype=f32) / half_width)
    angles = time_steps.astype(f32)[:, None] * frequency[None, :]
    return jnp.concatenate([jnp.cos(angles), jnp.sin(angles)], axis=1)


def segment_ids(lengths, row_count):
    row_index = jnp.arange(row_count, dtype=jnp.int32)
    inner = jnp.where(row_index < lengths[0] + lengths[1], 1, 2)
    return jnp.where(row_index < lengths[0], 0, inner).astype(jnp.int32)


def contract_rows(left_side, right_side, precision_mode=None):
    return lax.dot_general(
        left_side,
        right_side,
        (((0,), (0,)), ((), ())),
        precision=precision_mode,
        preferred_element_type=jnp.float32,
    )


def contract_cols(left_side, right_side, precision_mode=None):
    return lax.dot_general(
        left_side,
        right_side,
        (((1,), (1,)), ((), ())),
        precision=precision_mode,
        preferred_element_type=jnp.float32,
    )


def norm_forward(summed, gain_row, shift_row):
    centered = summed - jnp.mean(summed, axis=-1, keepdims=True)
    inv_std = lax.rsqrt(jnp.mean(centered * centered, axis=-1, keepdims=True) + epsilon)
    normed = centered * inv_std
    return (normed * gain_row + shift_row, normed, inv_std)


def norm_backward(grad_rows, normed, inv_std, gain_row):
    scaled = grad_rows * gain_row
    inner = (
        scaled
        - jnp.mean(scaled, axis=-1, keepdims=True)
        - normed * jnp.mean(scaled * normed, axis=-1, keepdims=True)
    )
    return (inner * inv_std, jnp.sum(grad_rows * normed, axis=0), jnp.sum(grad_rows, axis=0))


def block_scores(query_blk, key_heads, seg_blk, segment, factor):
    raw_scores = (
        jnp.einsum("qhd,khd->hqk", query_blk, key_heads, preferred_element_type=jnp.float32)
        * factor
    )
    allowed = seg_blk[:, None] == segment[None, :]
    return jnp.where(allowed[None], raw_scores, -1e30)


def attention_forward(query_rows, key_rows, value_rows, segment, block_rows):
    rows_total = query_rows.shape[0]
    head_count = query_rows.shape[1] // HD
    factor = 1.0 / math.sqrt(HD)
    key_heads = key_rows.reshape(rows_total, head_count, HD)
    value_heads = value_rows.reshape(rows_total, head_count, HD)
    query_blocks = query_rows.reshape(rows_total // block_rows, block_rows, head_count, HD)
    seg_blocks = segment.reshape(rows_total // block_rows, block_rows)

    def one_block(item):
        query_blk, seg_blk = item
        scores = block_scores(query_blk, key_heads, seg_blk, segment, factor)
        row_max = jnp.max(scores, axis=-1, keepdims=True)
        exp_scores = jnp.exp(scores - row_max)
        row_total = jnp.sum(exp_scores, axis=-1, keepdims=True)
        prob_low = (exp_scores / row_total).astype(jnp.bfloat16)
        mixed_blk = jnp.einsum(
            "hqk,khd->qhd", prob_low, value_heads, preferred_element_type=jnp.float32
        )
        log_total = (row_max + jnp.log(row_total))[..., 0]
        return (mixed_blk.reshape(block_rows, head_count * HD).astype(jnp.bfloat16), log_total)

    mixed_blocks, log_totals = lax.map(one_block, (query_blocks, seg_blocks))
    return (mixed_blocks.reshape(rows_total, head_count * HD), log_totals)


def attention_backward(
    query_rows, key_rows, value_rows, grad_mixed, log_totals, segment, block_rows
):
    rows_total = query_rows.shape[0]
    head_count = query_rows.shape[1] // HD
    factor = 1.0 / math.sqrt(HD)
    block_count = rows_total // block_rows
    key_heads = key_rows.reshape(rows_total, head_count, HD)
    value_heads = value_rows.reshape(rows_total, head_count, HD)
    query_blocks = query_rows.reshape(block_count, block_rows, head_count, HD)
    grad_blocks = grad_mixed.reshape(block_count, block_rows, head_count, HD)
    seg_blocks = segment.reshape(block_count, block_rows)

    def one_block(carry, item):
        grad_key_acc, grad_value_acc = carry
        query_blk, grad_blk, seg_blk, log_blk = item
        scores = block_scores(query_blk, key_heads, seg_blk, segment, factor)
        probs_full = jnp.exp(scores - log_blk[..., None])
        prob_low = probs_full.astype(jnp.bfloat16)
        grad_value_acc = grad_value_acc + jnp.einsum(
            "hqk,qhd->khd", prob_low, grad_blk, preferred_element_type=jnp.float32
        )
        grad_probs = jnp.einsum(
            "qhd,khd->hqk", grad_blk, value_heads, preferred_element_type=jnp.float32
        )
        row_inner = jnp.sum(grad_probs * probs_full, axis=-1, keepdims=True)
        grad_scores = (probs_full * (grad_probs - row_inner)).astype(jnp.bfloat16)
        grad_query_blk = (
            jnp.einsum("hqk,khd->qhd", grad_scores, key_heads, preferred_element_type=jnp.float32)
            * factor
        )
        grad_key_acc = (
            grad_key_acc
            + jnp.einsum("hqk,qhd->khd", grad_scores, query_blk, preferred_element_type=jnp.float32)
            * factor
        )
        return ((grad_key_acc, grad_value_acc), grad_query_blk.reshape(block_rows, head_count * HD))

    zeros_heads = jnp.zeros((rows_total, head_count, HD), jnp.float32)
    (grad_key_acc, grad_value_acc), grad_query_blocks = lax.scan(
        one_block, (zeros_heads, zeros_heads), (query_blocks, grad_blocks, seg_blocks, log_totals)
    )
    return (
        grad_query_blocks.reshape(rows_total, head_count * HD),
        grad_key_acc.reshape(rows_total, head_count * HD),
        grad_value_acc.reshape(rows_total, head_count * HD),
    )


def on_device(
    inputs, cotangent, seq_lengths, timesteps, time_w1, time_b1, time_w2, time_b2,
    w_query, b_query, w_key, w_value, b_value, w_out, b_out, norm1_gain, norm1_bias,
    w_up, b_up, w_down, b_down, norm2_gain, norm2_bias,
):
    dp = lax.axis_size("dp")
    sub = dp // SUPER
    low = [[q * sub + l for l in range(sub)] for q in range(SUPER)]
    dp_index = lax.axis_index("dp")
    tp_index = lax.axis_index("tp")
    seq_rows, width = inputs.shape
    own_rows = seq_rows // lax.axis_size("tp")
    row_start = tp_index * own_rows
    block_rows = min(512, seq_rows)
    head_width = w_query.shape[1]

    def near_gather(value, axis):
        if sub == 1:
            return value
        return lax.all_gather(value, "dp", axis=axis, tiled=True, axis_index_groups=low)

    def near_sum(value):
        if sub == 1:
            return value
        return lax.psum(value, "dp", axis_index_groups=low)

    def near_scatter(value):
        if sub == 1:
            return value
        return lax.psum_scatter(
            value, "dp", scatter_dimension=0, tiled=True, axis_index_groups=low
        )

    z = dp_index // (4 * sub)
    pair_row = (z * sub + dp_index % sub) * 2
    seqs = 8 * sub
    features = time_features(timesteps[0], TE).astype(bf16)
    placed_feats = lax.dynamic_update_slice(
        jnp.zeros((seqs, TE), f32), features.astype(f32), (pair_row, 0)
    )
    own_slice = width // (dp * lax.axis_size("tp"))
    slice_start = (dp_index * lax.axis_size("tp") + tp_index) * own_slice
    stacked = jnp.stack(
        [time_b2, b_out, norm1_gain, norm1_bias, b_down, norm2_gain, norm2_bias, jnp.zeros_like(b_out)]
    )
    vectors = lax.dynamic_update_slice(jnp.zeros((8, width), f32), stacked, (0, slice_start))
    shards = [
        near_gather(one, 0)
        for one in (
            jnp.concatenate([w_query, w_key, w_value], axis=1).astype(bf16),
            w_out.T.astype(bf16),
            w_up.astype(bf16),
            w_down.T.astype(bf16),
        )
    ]
    wqkv, wout_t, wup, wdown_t, all_feats, embed, shared = call_gather(
        sub,
        shards,
        near_sum(placed_feats),
        near_sum(vectors),
        near_gather(time_w1, 1),
        near_gather(time_b1, 0)[None, :],
        near_gather(time_w2, 0),
    )
    bout_full, gain_one, shift_one, bdown_full, gain_two, shift_two = [shared[i] for i in range(1, 7)]
    time_embed = lax.dynamic_slice(embed, (pair_row, 0), (2, width))

    lengths = seq_lengths[0]
    segment = segment_ids(lengths, seq_rows)
    inner_embed = jnp.where((segment == 1)[:, None], time_embed[1][None, :], 0.0)
    added = jnp.where((segment == 0)[:, None], time_embed[0][None, :], inner_embed)
    base_rows = inputs.astype(f32) + added
    base_low = base_rows.astype(bf16)
    projected = jnp.dot(base_low, wqkv, preferred_element_type=f32)
    query_rows = (projected[:, :head_width] + b_query).astype(bf16)
    key_rows = projected[:, head_width : 2 * head_width].astype(bf16)
    value_rows = (projected[:, 2 * head_width :] + b_value).astype(bf16)
    mixed_low, log_totals = attention_forward(query_rows, key_rows, value_rows, segment, block_rows)
    attn_own = (
        lax.psum_scatter(
            contract_cols(mixed_low, wout_t).astype(bf16), "tp", scatter_dimension=0, tiled=True
        ).astype(f32)
        + bout_full
    )
    base_own = lax.dynamic_slice_in_dim(base_rows, row_start, own_rows, 0)
    first_out, normed_one, inv_one = norm_forward(base_own + attn_own, gain_one, shift_one)
    first_all = lax.all_gather(first_out.astype(bf16), "tp", axis=0, tiled=True)
    up_pre = jnp.dot(first_all, wup, preferred_element_type=f32) + b_up
    gelu_value, gelu_pull = jax.vjp(jax.nn.gelu, up_pre)
    up_act = gelu_value.astype(bf16)
    ffn_own = (
        lax.psum_scatter(
            contract_cols(up_act, wdown_t).astype(bf16), "tp", scatter_dimension=0, tiled=True
        ).astype(f32)
        + bdown_full
    )
    outputs_own, normed_two, inv_two = norm_forward(first_out + ffn_own, gain_two, shift_two)
    seg_own = lax.dynamic_slice_in_dim(segment, row_start, own_rows, 0)
    valid_own = (seg_own < 2).astype(f32)
    grad_y = cotangent.astype(f32) * valid_own[:, None]
    grad_second, grad_gain_two, grad_shift_two = norm_backward(grad_y, normed_two, inv_two, gain_two)
    grad_b_down = jnp.sum(grad_second, axis=0)
    grad_down_all = lax.all_gather(grad_second.astype(bf16), "tp", axis=0, tiled=True)
    grad_w_down = contract_rows(grad_down_all, up_act)
    grad_act = jnp.dot(grad_down_all, wdown_t, preferred_element_type=f32)
    grad_up_pre = gelu_pull(grad_act)[0]
    grad_b_up = jnp.sum(grad_up_pre, axis=0)
    grad_up_low = grad_up_pre.astype(bf16)
    grad_w_up = contract_rows(first_all, grad_up_low)
    grad_first = grad_second + lax.psum_scatter(
        contract_cols(grad_up_low, wup).astype(bf16), "tp", scatter_dimension=0, tiled=True
    ).astype(f32)
    grad_r1, grad_gain_one, grad_shift_one = norm_backward(grad_first, normed_one, inv_one, gain_one)
    grad_b_out = jnp.sum(grad_r1, axis=0)
    grad_attn_all = lax.all_gather(grad_r1.astype(bf16), "tp", axis=0, tiled=True)
    grad_w_out = contract_rows(grad_attn_all, mixed_low)
    grad_mixed = jnp.dot(grad_attn_all, wout_t, preferred_element_type=f32).astype(bf16)
    grad_query, grad_keys, grad_values = attention_backward(
        query_rows, key_rows, value_rows, grad_mixed, log_totals, segment, block_rows
    )
    grad_qkv = jnp.concatenate(
        [grad_query.astype(bf16), grad_keys.astype(bf16), grad_values.astype(bf16)], axis=1
    )
    grad_qkv_sums = jnp.sum(grad_qkv.astype(f32), axis=0)
    grad_b_query = grad_qkv_sums[:head_width]
    grad_b_value = grad_qkv_sums[2 * head_width :]
    grad_qkv_w = contract_rows(base_low, grad_qkv)
    input_term = contract_cols(grad_qkv, wqkv)
    own_part = lax.dynamic_slice_in_dim(input_term, row_start, own_rows, 0) + grad_r1
    input_term = lax.dynamic_update_slice_in_dim(input_term, own_part, row_start, 0)
    grad_inputs = lax.psum(input_term.astype(bf16), "tp").astype(f32)
    grad_own = lax.dynamic_slice_in_dim(grad_inputs, row_start, own_rows, 0)
    picker_own = (seg_own[:, None] == jnp.arange(2, dtype=jnp.int32)[None, :]).astype(f32)
    grad_embed = contract_rows(picker_own, grad_own, highest)

    placed_embed = lax.dynamic_update_slice(jnp.zeros((seqs, width), f32), grad_embed, (pair_row, 0))
    zero_row = jnp.zeros((width,), f32)
    sums = jnp.concatenate(
        [
            jnp.stack(
                [grad_b_out, grad_gain_one, grad_shift_one, grad_b_down, grad_gain_two, grad_shift_two]
                + [zero_row] * 2
            ),
            jnp.concatenate([grad_b_query, grad_b_value]).reshape(-1, width),
            grad_b_up.reshape(-1, width),
        ],
        axis=0,
    )
    local_rows = sums.shape[0]
    sums = jnp.concatenate([sums, jnp.zeros((16 - local_rows, width), f32), placed_embed], axis=0)
    red_qkv, red_out, red_up, red_down, all_sums, all_embed = call_reduce(
        sub,
        [grad_qkv_w.astype(bf16), grad_w_out.astype(bf16), grad_w_up.astype(bf16), grad_w_down.astype(bf16)],
        sums,
    )
    all_sums, all_embed = near_sum((all_sums, all_embed))
    red_qkv, red_out, red_up, red_down = [
        near_scatter(one) for one in (red_qkv, red_out, red_up, red_down)
    ]
    own_vectors = lax.dynamic_slice(all_sums, (0, slice_start), (8, own_slice))
    tp_vectors = all_sums[8:16].reshape(-1)
    every_feat = all_feats.reshape(-1, TE)
    every_embed = all_embed.reshape(-1, width)
    time_pre = (
        jnp.dot(every_feat.astype(bf16), time_w1.astype(bf16), preferred_element_type=f32) + time_b1
    )
    silu_value, silu_pull = jax.vjp(jax.nn.silu, time_pre)
    time_hidden = silu_value.astype(bf16).astype(f32)
    red_tw2 = contract_rows(time_hidden, every_embed, highest)
    grad_hidden = contract_cols(every_embed, time_w2.astype(bf16).astype(f32), highest)
    grad_time_pre = silu_pull(grad_hidden)[0]
    red_tb1 = jnp.sum(grad_time_pre, axis=0)
    red_tw1 = contract_rows(every_feat, grad_time_pre, highest)
    red_tb2 = lax.dynamic_slice(jnp.sum(every_embed, axis=0), (slice_start,), (own_slice,))
    hidden_width = b_up.shape[0]
    return (
        outputs_own.astype(bf16),
        grad_inputs,
        red_tw1,
        red_tb1,
        red_tw2,
        red_tb2,
        red_qkv[:, :head_width],
        tp_vectors[:head_width],
        red_qkv[:, head_width : 2 * head_width],
        red_qkv[:, 2 * head_width :],
        tp_vectors[head_width : 2 * head_width],
        red_out.T,
        own_vectors[0],
        own_vectors[1],
        own_vectors[2],
        red_up,
        tp_vectors[2 * head_width : 2 * head_width + hidden_width],
        red_down.T,
        own_vectors[3],
        own_vectors[4],
        own_vectors[5],
    )


def solution(mesh):
    placed = (
        P("dp", None),
        P(("dp", "tp"), None),
        P("dp", None),
        P("dp", None),
        P(None, ("dp", "tp")),
        P(("dp", "tp")),
        P(("dp", "tp"), None),
        P(("dp", "tp")),
        P("dp", "tp"),
        P("tp"),
        P("dp", "tp"),
        P("dp", "tp"),
        P("tp"),
        P("tp", "dp"),
        P(("dp", "tp")),
        P(("dp", "tp")),
        P(("dp", "tp")),
        P("dp", "tp"),
        P("tp"),
        P("tp", "dp"),
        P(("dp", "tp")),
        P(("dp", "tp")),
        P(("dp", "tp")),
    )
    return jax.shard_map(
        on_device,
        mesh=mesh,
        in_specs=placed,
        out_specs=(
            P(("dp", "tp"), None),
            P("dp", None),
            P(None, ("dp", "tp")),
            P(("dp", "tp")),
            P(("dp", "tp"), None),
            P(("dp", "tp")),
            P("dp", "tp"),
            P("tp"),
            P("dp", "tp"),
            P("dp", "tp"),
            P("tp"),
            P("tp", "dp"),
            P(("dp", "tp")),
            P(("dp", "tp")),
            P(("dp", "tp")),
            P("dp", "tp"),
            P("tp"),
            P("tp", "dp"),
            P(("dp", "tp")),
            P(("dp", "tp")),
            P(("dp", "tp")),
        ),
        check_vma=False,
    )
```

```python
import functools
import math
import types

import jax
import jax.numpy as jnp
from jax import lax
from jax.experimental import pallas as pl
from jax.experimental.pallas import tpu as pltpu
from jax.sharding import PartitionSpec as P

HD = 64
TE = 128
SUPER = 16

epsilon = 1e-05
highest = lax.Precision.HIGHEST
f32 = jnp.float32
bf16 = jnp.bfloat16


class Place:
    def __init__(self, sub):
        self.sub = sub
        index = lax.axis_index("dp")
        self.low = lax.rem(index, sub)
        self.place = lax.div(index, sub)
        self.z = lax.div(self.place, 4)
        self.p = lax.rem(self.place, 4)
        self.r = self.ring(self.p)

    @staticmethod
    def ring(v):
        half = lax.div(v, 2)
        return 2 * half + lax.rem(lax.rem(v, 2) + half, 2)

    def spot(self, dz, dr):
        z = lax.rem(self.z + dz + 4, 4)
        p = self.ring(lax.rem(self.r + dr + 4, 4))
        return z * 4 + p

    def device(self, dz, dr):
        return {"dp": self.spot(dz, dr) * self.sub + self.low}

    def other(self):
        return {"tp": 1 - lax.axis_index("tp")}

    def rows(self, dz, dr, count):
        return pl.ds(pl.multiple_of(self.spot(dz, dr) * count, 16), count)

    def enter(self):
        barrier = pltpu.get_barrier_semaphore()
        for peer in (
            [self.device(d, 0) for d in (1, 2, 3)]
            + [self.device(0, d) for d in (1, 2, 3)]
            + [self.other()]
        ):
            pl.semaphore_signal(barrier, inc=1, device_id=peer, device_id_type=pl.DeviceIdType.MESH)
        pl.semaphore_wait(barrier, 7)


def remote(src, dst, send, recv, device):
    return pltpu.make_async_remote_copy(
        src_ref=src,
        dst_ref=dst,
        send_sem=send,
        recv_sem=recv,
        device_id=device,
        device_id_type=pl.DeviceIdType.MESH,
    )


def many(k, name, g):
    return getattr(k, name + str(g))


class Gather:
    def __init__(self, place, shard, full, send, recv, g):
        rows = shard.shape[0]
        at = lambda dz, dr: full.at[place.rows(dz, dr, rows), :]
        self.place, self.shard, self.full, self.count = place, shard, full, rows
        self.to_planes = [
            remote(shard, at(0, 0), send.at[g, d - 1], recv.at[g, d - 1], place.device(d, 0))
            for d in (1, 2, 3)
        ]
        self.around = []
        self.relay = []
        for d in range(4):
            source = shard if d == 0 else at(-d, 0)
            self.around.append(
                [
                    remote(
                        source,
                        at(-d, 0),
                        send.at[g, 3 + 2 * d + k],
                        recv.at[g, 3 + 2 * d + k],
                        place.device(0, 1 - 2 * k),
                    )
                    for k in (0, 1)
                ]
            )
            k = d // 2
            self.relay.append(
                remote(
                    at(-d, 2 * k - 1),
                    at(-d, 2 * k - 1),
                    send.at[g, 11 + d],
                    recv.at[g, 11 + d],
                    place.device(0, 1 - 2 * k),
                )
            )

    def begin(self):
        for copy in self.to_planes:
            copy.start()
        for copy in self.around[0]:
            copy.start()
        self.full[self.place.rows(0, 0, self.count), :] = self.shard[...]

    def turn(self):
        for d in (1, 2, 3):
            self.to_planes[d - 1].wait_recv()
            for copy in self.around[d]:
                copy.start()

    def pass_on(self):
        for d in range(4):
            self.around[d][d // 2].wait_recv()
            self.relay[d].start()

    def finish(self):
        for d in range(4):
            self.around[d][1 - d // 2].wait_recv()
            self.relay[d].wait_recv()

    def drain(self):
        for copy in self.to_planes + [c for pair in self.around for c in pair] + self.relay:
            copy.wait_send()


class Reduce:
    def __init__(self, place, grads, total, first, second, third, send, recv, g):
        rows = total.shape[0]
        at = lambda dz, dr: grads.at[place.rows(dz, dr, rows), :]
        self.place, self.grads, self.total, self.rows = place, grads, total, rows
        self.first, self.second, self.third = first, second, third
        self.far, self.near, self.up = [], [], []
        for d in range(4):
            k = d // 2
            self.far.append(
                remote(
                    at(d, 2), first.at[d], send.at[g, d], recv.at[g, d], place.device(0, 1 - 2 * k)
                )
            )
            self.near.append(
                [
                    remote(
                        at(d, 1 - 2 * j),
                        second.at[j * 4 + d],
                        send.at[g, 4 + 2 * d + j],
                        recv.at[g, 4 + 2 * d + j],
                        place.device(0, 1 - 2 * j),
                    )
                    for j in (0, 1)
                ]
            )
        for d in (1, 2, 3):
            self.up.append(
                remote(
                    at(d, 0),
                    third.at[d - 1],
                    send.at[g, 11 + d],
                    recv.at[g, 11 + d],
                    place.device(d, 0),
                )
            )

    def begin(self):
        for d in range(4):
            self.far[d].start()
        for d in range(4):
            self.near[d][1 - d // 2].start()

    def join(self):
        for d in range(4):
            k = d // 2
            self.far[d].wait_recv()
            rows = self.place.rows(d, 1 - 2 * k, self.rows)
            self.grads[rows, :] = (self.grads[rows, :].astype(f32) + self.first[d].astype(f32)).astype(bf16)
            self.near[d][k].start()

    def cross(self):
        for d in (1, 2, 3, 0):
            for j in (0, 1):
                self.near[d][j].wait_recv()
            rows = self.place.rows(d, 0, self.rows)
            summed = (
                self.grads[rows, :].astype(f32)
                + self.second[d].astype(f32)
                + self.second[4 + d].astype(f32)
            )
            if d:
                self.grads[rows, :] = summed.astype(bf16)
                self.up[d - 1].start()
            else:
                self.total[...] = summed

    def finish(self):
        for copy in self.up:
            copy.wait_recv()
        self.total[...] += (
            self.third[0].astype(f32) + self.third[1].astype(f32) + self.third[2].astype(f32)
        )

    def drain(self):
        for copy in self.far + [c for pair in self.near for c in pair] + self.up:
            copy.wait_send()


class Spread:
    def __init__(self, place, along, sources, slots, send, recv, base):
        rows = slice(0, sources[0].shape[0])
        if along == "tp":
            self.copies = [
                remote(sources[0], slots.at[rows], send.at[base], recv.at[base], place.other())
            ]
            return
        self.copies = [
            remote(
                sources[d - 1],
                slots.at[d - 1, rows],
                send.at[base + d - 1],
                recv.at[base + d - 1],
                place.device(d, 0) if along == "z" else place.device(0, d),
            )
            for d in (1, 2, 3)
        ]

    def start(self):
        for copy in self.copies:
            copy.start()

    def wait(self):
        for copy in self.copies:
            copy.wait_recv()

    def drain(self):
        for copy in self.copies:
            copy.wait_send()


def mul(a, b):
    return lax.dot_general(a, b, (((1,), (0,)), ((), ())), preferred_element_type=f32)


def mul_t(a, b):
    return lax.dot_general(a, b, (((1,), (1,)), ((), ())), preferred_element_type=f32)


def fold(x):
    return jnp.sum(x.reshape(x.shape[0] // 8, 8, x.shape[1]), axis=0)


def mean(x):
    return jnp.mean(x, axis=-1, keepdims=True)


PAIR = 2 * HD
TOP = math.sqrt(2.0 / math.pi)


def layer_kernel(sub, names, *refs):
    k = types.SimpleNamespace(**dict(zip(names, refs, strict=True)))
    place = Place(sub)
    side = lax.axis_index("tp")
    x_ref = k.x
    total_rows, width = x_ref.shape
    half = total_rows // 2
    tp_send, tp_recv = k.tp_send, k.tp_recv
    seqs = k.feats.shape[0]
    pairs = k.mixed.shape[1] // PAIR
    hidden_width = k.bup.shape[1]
    own0 = pl.multiple_of(side * half, half)
    far0 = pl.multiple_of((1 - side) * half, half)
    first_len = k.lengths[0, 0]
    both_len = first_len + k.lengths[0, 1]

    def segment(start, count):
        row = lax.broadcasted_iota(jnp.int32, (count, 1), 0) + start
        return jnp.where(row < first_len, 0, jnp.where(row < both_len, 1, 2))

    def swap(n, src, dst):
        return remote(src, dst, tp_send.at[n], tp_recv.at[n], place.other())

    place.enter()
    small_send, small_recv = k.small_send, k.small_recv
    spread_z = Spread(place, "z", [k.feats] * 3, k.feat_z, small_send, small_recv, 0)
    spread_z.start()
    gathers = [
        Gather(place, many(k, "w", g), many(k, "full", g), k.g_send, k.g_recv, g) for g in range(4)
    ]
    gathers[0].begin()
    spread_z.wait()
    k.feat_sum[...] = k.feats[...] + k.feat_z[0] + k.feat_z[1] + k.feat_z[2]
    spread_r = Spread(place, "r", [k.feat_sum] * 3, k.feat_in, small_send, small_recv, 3)
    spread_r.start()
    k.all_feats[0] = k.feat_sum[...]
    spread_r.wait()
    for d in (1, 2, 3):
        k.all_feats[d] = k.feat_in[d - 1]
    every = k.all_feats[...].reshape(4 * seqs, TE)
    before = mul(every.astype(bf16), k.tw1[...].astype(bf16)) + k.tb1[...]
    hidden = jax.nn.silu(before).astype(bf16)
    share = mul(hidden, k.tw2[...].astype(bf16))
    part = k.part
    for d in range(4):
        part[d, :seqs, :] = share[d * seqs : (d + 1) * seqs, :]
        part[d, seqs : seqs + 8, :] = k.vectors[...]
    top = slice(0, seqs + 8)
    back = Spread(
        place, "r", [part.at[n, top] for n in (3, 2, 1)], k.part_in, small_send, small_recv, 6
    )
    back.start()
    back.wait()
    in_plane = k.part_in
    k.part_sum[top] = part[0, top] + in_plane[0, top] + in_plane[1, top] + in_plane[2, top]
    over_z = Spread(place, "z", [k.part_sum.at[top]] * 3, k.part_z, small_send, small_recv, 9)
    over_z.start()
    gathers[0].turn()
    gathers[1].begin()
    gathers[2].begin()
    over_z.wait()
    from_z = k.part_z
    k.part_zsum[top] = k.part_sum[top] + from_z[0, top] + from_z[1, top] + from_z[2, top]
    pair = Spread(place, "tp", [k.part_zsum.at[top]], k.part_tp, small_send, small_recv, 12)
    pair.start()
    pair.wait()
    both = k.part_zsum[top] + k.part_tp[top]
    shared = k.shared
    shared[...] = both[seqs:]
    embed = both[:seqs] + shared[0:1, :]
    at_row = (place.z * sub + place.low) * 2
    seq_row = lax.broadcasted_iota(jnp.int32, (seqs, 1), 0)
    for s in (0, 1):
        k.embed[s : s + 1, :] = jnp.sum(
            jnp.where(seq_row == at_row + s, embed, 0.0), axis=0, keepdims=True
        )

    for one in (spread_z, spread_r, back, over_z, pair):
        one.drain()

    def vector(n):
        return shared[n : n + 1, :]

    def base_of(start, count):
        seg = segment(start, count)
        added = jnp.where(
            seg == 0, k.embed[0:1, :], jnp.where(seg == 1, k.embed[1:2, :], 0.0)
        )
        return x_ref[pl.ds(start, count), :].astype(f32) + added

    @pl.loop(0, total_rows // 128)
    def _(i):
        start = pl.multiple_of(i * 128, 128)
        k.base[pl.ds(start, 128), :] = base_of(start, 128).astype(bf16)
        seg = segment(start, 128)
        lane = lax.rem(lax.broadcasted_iota(jnp.int32, (1, PAIR), 1), HD)
        k.mask_k[pl.ds(start, 128), :] = jnp.where(lane == seg, 1.0, 0.0).astype(bf16)
        k.mask_q[pl.ds(start, 128), :] = jnp.where((lane < 3) & (lane != seg), -1e30, 0.0).astype(
            bf16
        )

    def transpose(source, dest):
        @pl.loop(0, width // 128)
        def _(i):
            cut = pl.ds(pl.multiple_of(i * 128, 128), 128)
            dest[cut, :] = source[:, cut].T

    transpose(k.base, k.base_t)
    gathers[0].pass_on()
    gathers[0].finish()

    lane = lax.broadcasted_iota(jnp.int32, (1, PAIR), 1)
    lower = lane < HD
    scale = jnp.where(lax.broadcasted_iota(jnp.int32, (1, 3 * PAIR), 1) < PAIR, HD**-0.5, 1.0)
    qkv = k.qkv
    rows_at_once = 256

    def cut_of(j, part_index):
        return slice((3 * j + part_index) * PAIR, (3 * j + part_index + 1) * PAIR)

    def projection(j):
        cols = slice(3 * j * PAIR, 3 * (j + 1) * PAIR)

        @pl.loop(0, total_rows // 512)
        def _(i):
            rows = pl.ds(pl.multiple_of(i * 512, 512), 512)
            got = (mul(k.base[rows, :], k.full0[:, cols]) + k.bqkv[:, cols]) * scale
            qkv[rows, cols] = got.astype(bf16)

    def in_head(h):
        return lower if h == 0 else jnp.logical_not(lower)

    def with_mask(value, mask, h):
        return jnp.where(in_head(h), value.astype(f32), mask.astype(f32)).astype(bf16)

    def attend(j):
        for h in (0, 1):
            k.keys[h] = with_mask(qkv[:, cut_of(j, 1)], k.mask_k[...], h)

        @pl.loop(0, total_rows // rows_at_once)
        def _(i):
            rows = pl.ds(pl.multiple_of(i * rows_at_once, rows_at_once), rows_at_once)
            outs, logs = [], []
            for h in (0, 1):
                query = with_mask(qkv[rows, cut_of(j, 0)], k.mask_q[rows, :], h)
                scores = mul_t(query, k.keys[h])
                top = jnp.max(scores, axis=-1, keepdims=True)
                weight = jnp.exp(scores - top)
                total = jnp.sum(weight, axis=-1, keepdims=True)
                outs.append(mul(weight.astype(bf16), qkv[:, cut_of(j, 2)]) / total)
                logs.append(top + jnp.log(total))
            k.mixed[rows, j * PAIR : (j + 1) * PAIR] = jnp.where(lower, outs[0], outs[1]).astype(bf16)
            k.lse[rows, :] = jnp.where(lower, logs[0], logs[1])

        flipped = k.lse[...].T
        k.lse_t[j, 0:1, :] = flipped[0:1, :]
        k.lse_t[j, 1:2, :] = flipped[HD : HD + 1, :]

    projection(0)
    gathers[1].turn()
    gathers[2].turn()
    gathers[3].begin()
    projection(1)
    projection(2)
    attend(0)
    gathers[1].pass_on()
    gathers[2].pass_on()
    attend(1)
    gathers[3].turn()
    attend(2)
    for j in range(3, pairs):
        attend(j)
    gathers[1].finish()
    gathers[3].pass_on()

    block = 256

    @pl.loop(0, half // block)
    def _(i):
        rows = pl.ds(pl.multiple_of(far0 + i * block, block), block)
        k.half_send[pl.ds(pl.multiple_of(i * block, block), block), :] = mul_t(
            k.mixed[rows, :], k.full1[...]
        ).astype(bf16)

    swap_a = swap(0, k.half_send, k.half_recv)
    swap_a.start()
    first_own, normed_one, inv_one = k.first_own, k.normed_one, k.inv_one

    @pl.loop(0, half // block)
    def _(i):
        here = pl.ds(pl.multiple_of(i * block, block), block)
        start = pl.multiple_of(own0 + i * block, block)
        first_own[here, :] = (
            base_of(start, block) + vector(1) + mul_t(k.mixed[pl.ds(start, block), :], k.full1[...])
        )

    swap_a.wait_recv()
    small = 128

    @pl.loop(0, half // small)
    def _(i):
        here = pl.ds(pl.multiple_of(i * small, small), small)
        summed = first_own[here, :] + k.half_recv[here, :].astype(f32)
        centered = summed - mean(summed)
        inv = lax.rsqrt(mean(centered * centered) + epsilon)
        normed = centered * inv
        first = normed * vector(2) + vector(3)
        first_own[here, :] = first
        normed_one[here, :] = normed
        inv_one[here, :] = jnp.broadcast_to(inv, (small, 128))
        k.first[pl.ds(pl.multiple_of(own0 + i * small, small), small), :] = first.astype(bf16)

    own = pl.ds(own0, half)
    far = pl.ds(far0, half)
    swap_b = swap(1, k.first.at[own, :], k.first.at[own, :])
    swap_b.start()
    gathers[2].finish()
    chunk = 512
    blocks = hidden_width // chunk

    def rise(start):
        rows = pl.ds(start, half)

        @pl.loop(0, blocks)
        def _(i):
            cols = pl.ds(pl.multiple_of(i * chunk, chunk), chunk)
            up = mul(k.first[rows, :], k.full2[:, cols]) + k.bup[:, cols]
            square = up * up
            inner = up * (TOP + (TOP * 0.044715) * square)
            gate = 0.5 + 0.5 * jnp.tanh(inner)
            act = up * gate
            slope = gate + act * (1.0 - gate) * (2.0 * TOP + (6.0 * TOP * 0.044715) * square)
            k.act[rows, cols] = act.astype(bf16)
            k.slope[rows, cols] = slope.astype(bf16)

    rise(own0)
    swap_a.wait_send()
    swap_b.wait_recv()
    rise(far0)
    transpose(k.first, k.first_t)
    gathers[3].finish()

    @pl.loop(0, half // block)
    def _(i):
        rows = pl.ds(pl.multiple_of(far0 + i * block, block), block)
        k.half_send[pl.ds(pl.multiple_of(i * block, block), block), :] = mul_t(
            k.act[rows, :], k.full3[...]
        ).astype(bf16)

    swap_c = swap(2, k.half_send, k.half_recv)
    swap_c.start()
    own_sum = first_own

    @pl.loop(0, half // block)
    def _(i):
        here = pl.ds(pl.multiple_of(i * block, block), block)
        rows = pl.ds(pl.multiple_of(own0 + i * block, block), block)
        own_sum[here, :] = mul_t(k.act[rows, :], k.full3[...]) + first_own[here, :] + vector(4)

    swap_c.wait_recv()
    swap_b.wait_send()
    acc = k.acc
    acc[...] = jnp.zeros_like(acc)

    @pl.loop(0, half // small)
    def _(i):
        here = pl.ds(pl.multiple_of(i * small, small), small)
        summed = own_sum[here, :] + k.half_recv[here, :].astype(f32)
        centered = summed - mean(summed)
        inv = lax.rsqrt(mean(centered * centered) + epsilon)
        normed = centered * inv
        k.out[here, :] = (normed * vector(5) + vector(6)).astype(bf16)
        start = pl.multiple_of(own0 + i * small, small)
        grad = jnp.where(segment(start, small) < 2, k.cot[here, :].astype(f32), 0.0)
        scaled = grad * vector(5)
        second = inv * (scaled - mean(scaled) - normed * mean(scaled * normed))
        own_sum[here, :] = second
        k.base[pl.ds(start, small), :] = second.astype(bf16)
        acc[0] += fold(grad * normed)
        acc[1] += fold(grad)
        acc[2] += fold(second)

    swap_d = swap(3, k.base.at[own, :], k.base.at[own, :])
    swap_d.start()
    acc_up = k.acc_up
    acc_up[...] = jnp.zeros_like(acc_up)

    def fall(start):
        rows = pl.ds(start, half)

        @pl.loop(0, blocks)
        def _(i):
            cols = pl.ds(pl.multiple_of(i * chunk, chunk), chunk)
            grad = mul(k.base[rows, :], k.full3[:, cols]) * k.slope[rows, cols].astype(f32)
            k.slope[rows, cols] = grad.astype(bf16)
            acc_up[:, cols] += fold(grad)

    reduces = [
        Reduce(
            place, many(k, "grad", g), many(k, "total", g), many(k, "near", g), many(k, "ring", g), many(k, "high", g),
            k.r_send, k.r_recv, g,
        )
        for g in range(3 + pairs)
    ]

    def weight_grad(g, left_t, right, first_col, count, step):
        @pl.loop(0, count // step)
        def _(i):
            cols = pl.ds(pl.multiple_of(i * step, step), step)
            source = pl.ds(pl.multiple_of(first_col + i * step, 128), step)
            many(k, "grad", g)[:, cols] = mul(left_t[...], right[:, source]).astype(bf16)

    fall(own0)
    swap_c.wait_send()
    swap_d.wait_recv()
    transpose(k.base, k.grad_t)
    weight_grad(0, k.grad_t, k.act, 0, hidden_width, chunk)
    reduces[0].begin()
    fall(far0)

    @pl.loop(0, half // block)
    def _(i):
        rows = pl.ds(pl.multiple_of(far0 + i * block, block), block)
        k.half_send[pl.ds(pl.multiple_of(i * block, block), block), :] = mul_t(
            k.slope[rows, :], k.full2[...]
        ).astype(bf16)

    swap_e = swap(4, k.half_send, k.half_recv)
    swap_e.start()

    @pl.loop(0, half // block)
    def _(i):
        here = pl.ds(pl.multiple_of(i * block, block), block)
        rows = pl.ds(pl.multiple_of(own0 + i * block, block), block)
        own_sum[here, :] += mul_t(k.slope[rows, :], k.full2[...])

    swap_e.wait_recv()

    @pl.loop(0, half // small)
    def _(i):
        here = pl.ds(pl.multiple_of(i * small, small), small)
        grad = own_sum[here, :] + k.half_recv[here, :].astype(f32)
        normed = normed_one[here, :]
        scaled = grad * vector(2)
        r1 = inv_one[here, 0:1] * (scaled - mean(scaled) - normed * mean(scaled * normed))
        k.first[pl.ds(pl.multiple_of(own0 + i * small, small), small), :] = r1.astype(bf16)
        acc[3] += fold(grad * normed)
        acc[4] += fold(grad)
        acc[5] += fold(r1)

    swap_f = swap(5, k.first.at[own, :], k.first.at[own, :])
    swap_f.start()
    weight_grad(1, k.first_t, k.slope, 0, hidden_width, chunk)
    reduces[1].begin()
    reduces[0].join()
    swap_f.wait_recv()

    @pl.loop(0, total_rows // 512)
    def _(i):
        rows = pl.ds(pl.multiple_of(i * 512, 512), 512)
        k.grad_mixed[rows, :] = mul(k.first[rows, :], k.full1[...]).astype(bf16)

    transpose(k.first, k.grad_t)
    weight_grad(2, k.grad_t, k.mixed, 0, pairs * PAIR, pairs * PAIR)
    reduces[2].begin()

    grad_qkv = k.grad_qkv
    acc_qkv = k.acc_qkv

    def attend_back(j):
        mixed_cut = slice(j * PAIR, (j + 1) * PAIR)
        for h in (0, 1):
            k.keys[h] = with_mask(qkv[:, cut_of(j, 0)], k.mask_q[...], h)
        product = k.grad_mixed[:, mixed_cut].astype(f32) * k.mixed[:, mixed_cut].astype(f32)
        flipped = product.T
        k.inner[0:1, :] = jnp.sum(flipped[:HD], axis=0, keepdims=True)
        k.inner[1:2, :] = jnp.sum(flipped[HD:], axis=0, keepdims=True)
        k.keys_t[...] = qkv[:, cut_of(j, 1)].T
        k.query_t[...] = jnp.zeros_like(k.query_t)

        @pl.loop(0, total_rows // rows_at_once)
        def _(i):
            start = pl.multiple_of(i * rows_at_once, rows_at_once)
            rows = pl.ds(start, rows_at_once)
            grads_v, grads_k, query_t = [], [], []
            for h in (0, 1):
                key = with_mask(qkv[rows, cut_of(j, 1)], k.mask_k[rows, :], h)
                prob = jnp.exp(mul_t(key, k.keys[h]) - k.lse_t[j, h : h + 1, :])
                value = jnp.where(in_head(h), qkv[rows, cut_of(j, 2)].astype(f32), 0.0).astype(bf16)
                grad_prob = mul_t(value, k.grad_mixed[:, mixed_cut])
                grad_score = (prob * (grad_prob - k.inner[h : h + 1, :])).astype(bf16)
                grads_v.append(mul(prob.astype(bf16), k.grad_mixed[:, mixed_cut]))
                grads_k.append(mul(grad_score, qkv[:, cut_of(j, 0)]))
                query_t.append(mul(k.keys_t[h * HD : (h + 1) * HD, rows], grad_score))
            grad_k = jnp.where(lower, grads_k[0], grads_k[1]).astype(bf16)
            grad_v = jnp.where(lower, grads_v[0], grads_v[1]).astype(bf16)
            grad_qkv[rows, cut_of(j, 1)] = grad_k
            grad_qkv[rows, cut_of(j, 2)] = grad_v
            k.query_t[...] += jnp.concatenate(query_t, axis=0)

        grad_qkv[:, cut_of(j, 0)] = (k.query_t[...].T * HD**-0.5).astype(bf16)
        cols = slice(3 * j * PAIR, 3 * (j + 1) * PAIR)
        acc_qkv[:, cols] = fold(grad_qkv[:, cols].astype(f32))
        weight_grad(3 + j, k.base_t, grad_qkv, 3 * j * PAIR, 3 * PAIR, 3 * PAIR)
        reduces[3 + j].begin()

    attend_back(0)
    reduces[0].cross()
    reduces[1].join()
    attend_back(1)
    reduces[2].join()
    reduces[1].cross()
    reduces[2].cross()
    for j in range(2, pairs):
        attend_back(j)
        reduces[1 + j].join()

    in_send, in_recv = k.act.at[:, :width], k.act.at[:, width : 2 * width]

    @pl.loop(0, total_rows // block)
    def _(i):
        rows = pl.ds(pl.multiple_of(i * block, block), block)
        in_send[rows, :] = mul_t(grad_qkv[rows, :], k.full0[...]).astype(bf16)

    swap_g = swap(6, in_send, in_recv)
    swap_g.start()
    for g in range(3, 2 + pairs):
        if g > 3:
            reduces[g].join()
    reduces[0].finish()
    reduces[3].cross()
    swap_g.wait_recv()
    ge = k.acc_ge
    ge[...] = jnp.zeros_like(ge)

    @pl.loop(0, total_rows // small)
    def _(i):
        start = pl.multiple_of(i * small, small)
        rows = pl.ds(start, small)
        grad = (in_send[rows, :].astype(f32) + in_recv[rows, :].astype(f32)) + k.first[rows, :].astype(f32)
        k.grad_in[rows, :] = grad
        seg = segment(start, small)
        ge[0] += fold(jnp.where(seg == 0, grad, 0.0))
        ge[1] += fold(jnp.where(seg == 1, grad, 0.0))

    def row_of(x):
        return jnp.sum(x, axis=0, keepdims=True)

    sums = k.part.at[0]
    sums[...] = jnp.zeros_like(sums)
    for row, n in enumerate((5, 3, 4, 2, 0, 1)):
        sums[row : row + 1, :] = row_of(acc[n])
    up_row = row_of(acc_up[...])
    for n in range(hidden_width // width):
        sums[8 + n : 9 + n, :] = up_row[:, n * width : (n + 1) * width]
    qkv_row = row_of(acc_qkv[...])
    at = 8 + hidden_width // width
    sums[at : at + 1, :] = qkv_row[:, :width]
    sums[at + 1 : at + 2, : qkv_row.shape[1] - width] = qkv_row[:, width:]
    sums[16:, :] = jnp.where(
        seq_row == at_row, row_of(ge[0]), jnp.where(seq_row == at_row + 1, row_of(ge[1]), 0.0)
    )
    pair_sums = Spread(place, "tp", [sums], k.part_tp, small_send, small_recv, 13)
    pair_sums.start()
    reduces[2 + pairs].join()
    pair_sums.wait()
    row = lax.broadcasted_iota(jnp.int32, sums.shape, 0)
    k.part_sum[...] = sums[...] + jnp.where(row < 8, k.part_tp[...], 0.0)
    sums_z = Spread(place, "z", [k.part_sum] * 3, k.part_z, small_send, small_recv, 14)
    sums_z.start()
    for g in range(4, 2 + pairs):
        reduces[g].cross()
    sums_z.wait()
    k.part_zsum[...] = k.part_sum[...] + k.part_z[0] + k.part_z[1] + k.part_z[2]
    sums_r = Spread(place, "r", [k.part_zsum] * 3, k.part_in, small_send, small_recv, 17)
    sums_r.start()
    for g in range(1, 3):
        reduces[g].finish()
    sums_r.wait()
    k.all_sums[...] = (
        k.part_zsum[:16] + k.part_in[0, :16] + k.part_in[1, :16] + k.part_in[2, :16]
    )
    k.all_embed[0] = k.part_zsum[16:]
    for d in (1, 2, 3):
        k.all_embed[d] = k.part_in[d - 1, 16:]
    reduces[2 + pairs].cross()
    for g in range(3, 3 + pairs):
        reduces[g].finish()
    for one in (
        gathers
        + reduces
        + [pair_sums, sums_z, sums_r]
    ):
        one.drain()
    for copy in (swap_d, swap_e, swap_f, swap_g):
        copy.wait_send()


def call_layer(sub, operands):
    rows, width = operands["x"].shape
    half = rows // 2
    heads = operands["w1"].shape[1]
    hidden = operands["bup"].shape[1]
    pairs = heads // PAIR
    seqs = operands["feats"].shape[0]
    mine = operands["w0"].shape[0]
    tall = seqs + 16
    columns = [hidden, hidden, heads] + [3 * PAIR] * pairs
    shape = jax.ShapeDtypeStruct
    results = dict(
        out=shape((half, width), bf16),
        grad_in=shape((rows, width), f32),
        all_feats=shape((4, seqs, TE), f32),
        all_sums=shape((16, width), f32),
        all_embed=shape((4, seqs, width), f32),
    )
    for g, wide in enumerate(columns):
        results["total" + str(g)] = shape((mine, wide), f32)
    vm = pltpu.VMEM
    sem = pltpu.SemaphoreType.DMA
    scratch = dict(
        full0=vm((width, 3 * heads), bf16),
        full1=vm((width, heads), bf16),
        full2=vm((width, hidden), bf16),
        full3=vm((width, hidden), bf16),
        feat_z=vm((3, seqs, TE), f32),
        feat_sum=vm((seqs, TE), f32),
        feat_in=vm((3, seqs, TE), f32),
        part=vm((4, tall, width), f32),
        part_in=vm((3, tall, width), f32),
        part_sum=vm((tall, width), f32),
        part_z=vm((3, tall, width), f32),
        part_zsum=vm((tall, width), f32),
        part_tp=vm((tall, width), f32),
        shared=vm((8, width), f32),
        embed=vm((8, width), f32),
        base=vm((rows, width), bf16),
        base_t=vm((width, rows), bf16),
        mask_q=vm((rows, PAIR), bf16),
        mask_k=vm((rows, PAIR), bf16),
        keys=vm((2, rows, PAIR), bf16),
        qkv=vm((rows, 3 * heads), bf16),
        mixed=vm((rows, heads), bf16),
        lse=vm((rows, PAIR), f32),
        lse_t=vm((pairs, 8, rows), f32),
        half_send=vm((half, width), bf16),
        half_recv=vm((half, width), bf16),
        first_own=vm((half, width), f32),
        normed_one=vm((half, width), f32),
        inv_one=vm((half, 128), f32),
        first=vm((rows, width), bf16),
        first_t=vm((width, rows), bf16),
        act=vm((rows, hidden), bf16),
        slope=vm((rows, hidden), bf16),
        acc=vm((6, 8, width), f32),
        acc_up=vm((8, hidden), f32),
        acc_qkv=vm((8, 3 * heads), f32),
        acc_ge=vm((2, 8, width), f32),
        grad_t=vm((width, rows), bf16),
        grad_mixed=vm((rows, heads), bf16),
        inner=vm((8, rows), f32),
        keys_t=vm((PAIR, rows), bf16),
        query_t=vm((PAIR, rows), f32),
        grad_qkv=vm((rows, 3 * heads), bf16),
        g_send=sem((4, 15)),
        g_recv=sem((4, 15)),
        r_send=sem((3 + pairs, 15)),
        r_recv=sem((3 + pairs, 15)),
        small_send=sem((20,)),
        small_recv=sem((20,)),
        tp_send=sem((7,)),
        tp_recv=sem((7,)),
    )
    for g, wide in enumerate(columns):
        scratch["grad" + str(g)] = vm((width, wide), bf16)
        scratch["near" + str(g)] = vm((4, mine, wide), bf16)
        scratch["ring" + str(g)] = vm((8, mine, wide), bf16)
        scratch["high" + str(g)] = vm((3, mine, wide), bf16)
    names = [*operands, *results, *scratch]
    in_specs = [
        pl.BlockSpec(memory_space=pltpu.SMEM if n == "lengths" else pltpu.VMEM) for n in operands
    ]
    got = pl.pallas_call(
        functools.partial(layer_kernel, sub, names),
        out_shape=list(results.values()),
        in_specs=in_specs,
        out_specs=vmem(len(results)),
        scratch_shapes=list(scratch.values()),
        compiler_params=pltpu.CompilerParams(
            collective_id=0, has_side_effects=True, vmem_limit_bytes=63_000 * 1024
        ),
        name="layer",
    )(*operands.values())
    return types.SimpleNamespace(**dict(zip(results, got, strict=True)))


def vmem(count):
    return [pl.BlockSpec(memory_space=pltpu.VMEM)] * count


def time_features(time_steps, feature_width):
    half_width = feature_width // 2
    frequency = jnp.exp(-math.log(10000.0) * jnp.arange(half_width, dtype=f32) / half_width)
    angles = time_steps.astype(f32)[:, None] * frequency[None, :]
    return jnp.concatenate([jnp.cos(angles), jnp.sin(angles)], axis=1)


def contract_rows(left_side, right_side, precision_mode=None):
    return lax.dot_general(
        left_side,
        right_side,
        (((0,), (0,)), ((), ())),
        precision=precision_mode,
        preferred_element_type=jnp.float32,
    )


def contract_cols(left_side, right_side, precision_mode=None):
    return lax.dot_general(
        left_side,
        right_side,
        (((1,), (1,)), ((), ())),
        precision=precision_mode,
        preferred_element_type=jnp.float32,
    )


def on_device(
    inputs, cotangent, seq_lengths, timesteps, time_w1, time_b1, time_w2, time_b2,
    w_query, b_query, w_key, w_value, b_value, w_out, b_out, norm1_gain, norm1_bias,
    w_up, b_up, w_down, b_down, norm2_gain, norm2_bias,
):
    dp = lax.axis_size("dp")
    sub = dp // SUPER
    low = [[q * sub + l for l in range(sub)] for q in range(SUPER)]
    dp_index = lax.axis_index("dp")
    tp_index = lax.axis_index("tp")
    seq_rows, width = inputs.shape
    head_width = w_query.shape[1]

    def near_gather(value, axis):
        if sub == 1:
            return value
        return lax.all_gather(value, "dp", axis=axis, tiled=True, axis_index_groups=low)

    def near_sum(value):
        if sub == 1:
            return value
        return lax.psum(value, "dp", axis_index_groups=low)

    def near_scatter(value):
        if sub == 1:
            return value
        return lax.psum_scatter(
            value, "dp", scatter_dimension=0, tiled=True, axis_index_groups=low
        )

    z = dp_index // (4 * sub)
    pair_row = (z * sub + dp_index % sub) * 2
    seqs = 8 * sub
    features = time_features(timesteps[0], TE).astype(bf16)
    placed_feats = lax.dynamic_update_slice(
        jnp.zeros((seqs, TE), f32), features.astype(f32), (pair_row, 0)
    )
    own_slice = width // (dp * lax.axis_size("tp"))
    slice_start = (dp_index * lax.axis_size("tp") + tp_index) * own_slice
    stacked = jnp.stack(
        [time_b2, b_out, norm1_gain, norm1_bias, b_down, norm2_gain, norm2_bias, jnp.zeros_like(b_out)]
    )
    vectors = lax.dynamic_update_slice(jnp.zeros((8, width), f32), stacked, (0, slice_start))
    pairs = head_width // PAIR
    hidden_width = b_up.shape[0]

    def by_pairs(parts):
        cut = [part.reshape(-1, pairs, 1, PAIR) for part in parts]
        return jnp.concatenate(cut, axis=2).reshape(-1, 3 * head_width)

    operands = dict(
        lengths=seq_lengths,
        x=inputs,
        cot=cotangent,
        w0=near_gather(by_pairs([w_query, w_key, w_value]).astype(bf16), 0),
        w1=near_gather(w_out.T.astype(bf16), 0),
        w2=near_gather(w_up.astype(bf16), 0),
        w3=near_gather(w_down.T.astype(bf16), 0),
        bqkv=by_pairs([b_query, jnp.zeros_like(b_query), b_value]),
        bup=b_up[None, :],
        feats=near_sum(placed_feats),
        vectors=near_sum(vectors),
        tw1=near_gather(time_w1, 1),
        tb1=near_gather(time_b1, 0)[None, :],
        tw2=near_gather(time_w2, 0),
    )
    got = call_layer(sub, operands)
    all_feats = got.all_feats
    all_sums, all_embed = near_sum((got.all_sums, got.all_embed))
    red_down, red_up, red_out = [near_scatter(many(got, "total", g)) for g in range(3)]
    red_pairs = [near_scatter(many(got, "total", 3 + j)) for j in range(pairs)]

    def of_pairs(part):
        return jnp.concatenate([one[:, part * PAIR : (part + 1) * PAIR] for one in red_pairs], axis=1)

    own_vectors = lax.dynamic_slice(all_sums, (0, slice_start), (8, own_slice))
    tp_vectors = all_sums[8:16].reshape(-1)
    qkv_sums = tp_vectors[hidden_width : hidden_width + 3 * head_width].reshape(pairs, 3, PAIR)
    every_feat = all_feats.reshape(-1, TE)
    every_embed = all_embed.reshape(-1, width)
    time_pre = (
        jnp.dot(every_feat.astype(bf16), time_w1.astype(bf16), preferred_element_type=f32) + time_b1
    )
    silu_value, silu_pull = jax.vjp(jax.nn.silu, time_pre)
    time_hidden = silu_value.astype(bf16).astype(f32)
    red_tw2 = contract_rows(time_hidden, every_embed, highest)
    grad_hidden = contract_cols(every_embed, time_w2.astype(bf16).astype(f32), highest)
    grad_time_pre = silu_pull(grad_hidden)[0]
    red_tb1 = jnp.sum(grad_time_pre, axis=0)
    red_tw1 = contract_rows(every_feat, grad_time_pre, highest)
    red_tb2 = lax.dynamic_slice(jnp.sum(every_embed, axis=0), (slice_start,), (own_slice,))
    return (
        got.out,
        got.grad_in,
        red_tw1,
        red_tb1,
        red_tw2,
        red_tb2,
        of_pairs(0),
        qkv_sums[:, 0].reshape(-1),
        of_pairs(1),
        of_pairs(2),
        qkv_sums[:, 2].reshape(-1),
        red_out.T,
        own_vectors[0],
        own_vectors[1],
        own_vectors[2],
        red_up,
        tp_vectors[:hidden_width],
        red_down.T,
        own_vectors[3],
        own_vectors[4],
        own_vectors[5],
    )


def solution(mesh):
    placed = (
        P("dp", None),
        P(("dp", "tp"), None),
        P("dp", None),
        P("dp", None),
        P(None, ("dp", "tp")),
        P(("dp", "tp")),
        P(("dp", "tp"), None),
        P(("dp", "tp")),
        P("dp", "tp"),
        P("tp"),
        P("dp", "tp"),
        P("dp", "tp"),
        P("tp"),
        P("tp", "dp"),
        P(("dp", "tp")),
        P(("dp", "tp")),
        P(("dp", "tp")),
        P("dp", "tp"),
        P("tp"),
        P("tp", "dp"),
        P(("dp", "tp")),
        P(("dp", "tp")),
        P(("dp", "tp")),
    )
    return jax.shard_map(
        on_device,
        mesh=mesh,
        in_specs=placed,
        out_specs=(
            P(("dp", "tp"), None),
            P("dp", None),
            P(None, ("dp", "tp")),
            P(("dp", "tp")),
            P(("dp", "tp"), None),
            P(("dp", "tp")),
            P("dp", "tp"),
            P("tp"),
            P("dp", "tp"),
            P("dp", "tp"),
            P("tp"),
            P("tp", "dp"),
            P(("dp", "tp")),
            P(("dp", "tp")),
            P(("dp", "tp")),
            P("dp", "tp"),
            P("tp"),
            P("tp", "dp"),
            P(("dp", "tp")),
            P(("dp", "tp")),
            P(("dp", "tp")),
        ),
        check_vma=False,
    )
```

```python
import functools
import math
import types

import jax
import jax.numpy as jnp
from jax import lax
from jax.experimental import pallas as pl
from jax.experimental.pallas import tpu as pltpu
from jax.sharding import PartitionSpec as P

HD = 64
TE = 128
SUPER = 16

epsilon = 1e-05
highest = lax.Precision.HIGHEST
f32 = jnp.float32
bf16 = jnp.bfloat16


class Place:
    def __init__(self, sub):
        self.sub = sub
        index = lax.axis_index("dp")
        self.low = lax.rem(index, sub)
        self.place = lax.div(index, sub)
        self.z = lax.div(self.place, 4)
        self.p = lax.rem(self.place, 4)
        self.r = self.ring(self.p)
        self.outer = (self.z == 0) | (self.z == 3)
        self.inner = (self.z == 1) | (self.z == 2)

    @staticmethod
    def ring(v):
        half = lax.div(v, 2)
        return 2 * half + lax.rem(lax.rem(v, 2) + half, 2)

    def spot(self, dz, dr):
        z = lax.rem(self.z + dz + 4, 4)
        p = self.ring(lax.rem(self.r + dr + 4, 4))
        return z * 4 + p

    def device(self, dz, dr):
        return {"dp": self.spot(dz, dr) * self.sub + self.low}

    def beside(self, step):
        plane = lax.rem(self.z + step + 4, 4)
        return {"dp": (plane * 4 + self.p) * self.sub + self.low}

    def other(self):
        return {"tp": 1 - lax.axis_index("tp")}

    def rows(self, dz, dr, count):
        return pl.ds(pl.multiple_of(self.spot(dz, dr) * count, 16), count)

    def enter(self):
        barrier = pltpu.get_barrier_semaphore()
        for peer in (
            [self.device(d, 0) for d in (1, 2, 3)]
            + [self.device(0, d) for d in (1, 2, 3)]
            + [self.other()]
        ):
            pl.semaphore_signal(barrier, inc=1, device_id=peer, device_id_type=pl.DeviceIdType.MESH)
        pl.semaphore_wait(barrier, 7)


def remote(src, dst, send, recv, device):
    return pltpu.make_async_remote_copy(
        src_ref=src,
        dst_ref=dst,
        send_sem=send,
        recv_sem=recv,
        device_id=device,
        device_id_type=pl.DeviceIdType.MESH,
    )


def many(k, name, g):
    return getattr(k, name + str(g))


class Gather:
    def __init__(self, place, shard, full, cols, send, recv, g):
        rows = shard.shape[0]
        at = lambda dz, dr: full.at[place.rows(dz, dr, rows), cols]
        self.place, self.shard, self.full, self.count = place, shard, full, rows
        self.cols = cols
        shard = shard.at[:, cols]
        self.to_planes = [
            remote(shard, at(0, 0), send.at[g, d - 1], recv.at[g, d - 1], place.device(d, 0))
            for d in (1, 2, 3)
        ]
        self.around = []
        self.relay = []
        for d in range(4):
            source = shard if d == 0 else at(-d, 0)
            self.around.append(
                [
                    remote(
                        source,
                        at(-d, 0),
                        send.at[g, 3 + 2 * d + k],
                        recv.at[g, 3 + 2 * d + k],
                        place.device(0, 1 - 2 * k),
                    )
                    for k in (0, 1)
                ]
            )
            k = d // 2
            self.relay.append(
                remote(
                    at(-d, 2 * k - 1),
                    at(-d, 2 * k - 1),
                    send.at[g, 11 + d],
                    recv.at[g, 11 + d],
                    place.device(0, 1 - 2 * k),
                )
            )

    def begin(self):
        for copy in self.to_planes:
            copy.start()
        self.full[self.place.rows(0, 0, self.count), self.cols] = self.shard[:, self.cols]

    def own(self):
        for copy in self.around[0]:
            copy.start()

    def turn(self, *which):
        for d in which or (1, 2, 3):
            self.to_planes[d - 1].wait_recv()
            for copy in self.around[d]:
                copy.start()

    def pass_on(self, *which):
        for d in which or (0, 1, 2, 3):
            self.around[d][d // 2].wait_recv()
            self.relay[d].start()

    def finish(self):
        for d in range(4):
            self.around[d][1 - d // 2].wait_recv()
            self.relay[d].wait_recv()

    def drain(self):
        for copy in self.to_planes + [c for pair in self.around for c in pair] + self.relay:
            copy.wait_send()


def halves(cols):
    middle = (cols.start + cols.stop) // 2
    return slice(cols.start, middle), slice(middle, cols.stop)


class Climb:
    def __init__(self, place, shard, full, cols, send, recv, g):
        rows = shard.shape[0]
        self.place, self.shard, self.full, self.count, self.cols = place, shard, full, rows, cols
        z = place.z
        at = lambda dr, part: full.at[place.rows(0, dr, rows), part]
        slab = lambda plane: full.at[pl.ds(pl.multiple_of(plane * 4 * rows, 16), 4 * rows), cols]
        self.around = [
            remote(shard.at[:, cols], at(0, cols), send.at[g, n], recv.at[g, n], place.device(0, 1 - 2 * n))
            for n in (0, 1)
        ]
        self.relay = [
            remote(at(2 * n - 1, part), at(2 * n - 1, part), send.at[g, 2 + n], recv.at[g, 2 + n], place.device(0, 1 - 2 * n))
            for n, part in enumerate(halves(cols))
        ]
        self.up, self.down = [
            remote(slab(z), slab(z), send.at[g, 4 + n], recv.at[g, 4 + z], place.beside(1 - 2 * n))
            for n in (0, 1)
        ]
        self.heard = []
        table = [
            jnp.where(z == 0, 1, z - 1),
            jnp.where(z == 3, 1, jnp.where(z == 2, 3, 2)),
            jnp.where(z < 2, 3, 0),
        ]
        for n, plane in enumerate(table):
            self.heard.append(
                remote(
                    slab(plane), slab(plane), send.at[g, 6 + n], recv.at[g, 4 + plane],
                    place.beside(jnp.where(plane < z, 1, -1)),
                )
            )

    def begin(self):
        for copy in self.around:
            copy.start()
        self.full[self.place.rows(0, 0, self.count), self.cols] = self.shard[:, self.cols]

    def pass_on(self):
        for n in (0, 1):
            self.around[n].wait_recv()
            self.relay[n].start()

    def rise(self):
        for n in (0, 1):
            self.relay[n].wait_recv()
        pl.when(self.place.z < 3)(self.up.start)
        pl.when(self.place.z > 0)(self.down.start)

    def hear(self, n):
        self.heard[n].wait_recv()
        pl.when(self.place.inner)(self.heard[n].start)

    def drain(self):
        for copy in self.around + self.relay:
            copy.wait_send()
        pl.when(self.place.z < 3)(self.up.wait_send)
        pl.when(self.place.z > 0)(self.down.wait_send)
        for copy in self.heard:
            pl.when(self.place.inner)(copy.wait_send)


class Reduce:
    def __init__(self, place, grads, total, cols, first, second, third, send, recv, g):
        rows = total.shape[0]
        at = lambda dz, dr: grads.at[place.rows(dz, dr, rows), cols]
        self.place, self.grads, self.total, self.rows, self.cols = place, grads, total, rows, cols
        self.first, self.second, self.third = first, second, third
        self.far, self.near, self.up = [], [], []
        for d in range(4):
            k = d // 2
            self.far.append(
                remote(
                    at(d, 2), first.at[d], send.at[g, d], recv.at[g, d], place.device(0, 1 - 2 * k)
                )
            )
            self.near.append(
                [
                    remote(
                        at(d, 1 - 2 * j),
                        second.at[j * 4 + d],
                        send.at[g, 4 + 2 * d + j],
                        recv.at[g, 4 + 2 * d + j],
                        place.device(0, 1 - 2 * j),
                    )
                    for j in (0, 1)
                ]
            )
        for d in (1, 2, 3):
            self.up.append(
                remote(
                    at(d, 0),
                    third.at[d - 1],
                    send.at[g, 11 + d],
                    recv.at[g, 11 + d],
                    place.device(d, 0),
                )
            )

    def begin(self):
        for d in range(4):
            self.far[d].start()
        for d in range(4):
            self.near[d][1 - d // 2].start()

    def join(self):
        for d in range(4):
            k = d // 2
            self.far[d].wait_recv()
            here = self.place.rows(d, 1 - 2 * k, self.rows), self.cols
            self.grads[here] = (self.grads[here].astype(f32) + self.first[d].astype(f32)).astype(bf16)
            self.near[d][k].start()

    def cross(self):
        for d in (1, 2, 3, 0):
            for j in (0, 1):
                self.near[d][j].wait_recv()
            here = self.place.rows(d, 0, self.rows), self.cols
            summed = (
                self.grads[here].astype(f32)
                + self.second[d].astype(f32)
                + self.second[4 + d].astype(f32)
            )
            if d:
                self.grads[here] = summed.astype(bf16)
                self.up[d - 1].start()
            else:
                self.total[:, self.cols] = summed

    def finish(self):
        for copy in self.up:
            copy.wait_recv()
        self.total[:, self.cols] += (
            self.third[0].astype(f32) + self.third[1].astype(f32) + self.third[2].astype(f32)
        )

    def drain(self):
        for copy in self.far + [c for pair in self.near for c in pair] + self.up:
            copy.wait_send()


class Descend:
    def __init__(self, place, grads, total, cols, deep, far, near, send, recv, g):
        rows = total.shape[0]
        self.place, self.grads, self.total, self.rows, self.cols = place, grads, total, rows, cols
        self.deep, self.far, self.near = deep, far, near
        lower = place.z < 2
        inward = jnp.where(lower, 1, -1)
        plane = lambda c: jnp.where(lower, c, 3 - c)
        self.slab = lambda c: (pl.ds(pl.multiple_of(plane(c) * 4 * rows, 16), 4 * rows), cols)
        part = halves(cols)
        self.part = part
        self.here = lambda dr, n: (place.rows(0, dr, rows), part[n])
        self.slot = [slice(p.start - cols.start, p.stop - cols.start) for p in part]

        def copy(source, dest, n, m, to):
            return remote(grads.at[source], dest, send.at[g, n], recv.at[g, m], to)

        ahead = place.beside(inward)
        self.enter = [copy(self.slab(3 - n), deep.at[n], n, n, ahead) for n in range(3)]
        self.between = [copy(self.slab(3 - n), deep.at[3 + n], 3 + n, 3 + n, ahead) for n in (0, 1)]
        self.leave = copy(self.slab(0), deep.at[0], 5, 5, place.beside(-inward))
        side = [place.device(0, 1), place.device(0, -1)]
        self.away = [
            copy(self.here(2, n), far.at[:, self.slot[n]], 6 + n, 6 + n, side[n]) for n in (0, 1)
        ]
        self.plain = [
            copy(self.here(1 - 2 * n, 1 - n), near.at[n, :, self.slot[1 - n]], 8 + n, 8 + n, side[n])
            for n in (0, 1)
        ]
        self.joined = [
            copy(self.here(1 - 2 * n, n), near.at[n, :, self.slot[n]], 10 + n, 10 + n, side[n])
            for n in (0, 1)
        ]

    def add(self, here, *terms):
        total = self.grads[here].astype(f32)
        for term in terms:
            total += term.astype(f32)
        self.grads[here] = total.astype(bf16)

    def begin(self):
        @pl.when(self.place.outer)
        def _():
            for copy in self.enter:
                copy.start()

    def pass_in(self):
        @pl.when(self.place.inner)
        def _():
            for n in (0, 1):
                self.enter[n].wait_recv()
                self.add(self.slab(3 - n), self.deep[n])
                self.between[n].start()

    def pass_out(self):
        @pl.when(self.place.inner)
        def _():
            self.between[0].wait_recv()
            self.add(self.slab(0), self.deep[3])
            self.leave.start()

    def arrive(self):
        @pl.when(self.place.inner)
        def _():
            self.enter[2].wait_recv()
            self.between[1].wait_recv()
            self.add(self.slab(1), self.deep[2], self.deep[4])

        @pl.when(self.place.outer)
        def _():
            self.leave.wait_recv()
            self.add(self.slab(0), self.deep[0])

        for copy in self.away + self.plain:
            copy.start()

    def join(self):
        for n in (0, 1):
            self.away[n].wait_recv()
            self.add(self.here(1 - 2 * n, n), self.far[:, self.slot[n]])
            self.joined[n].start()

    def finish(self):
        for copy in self.plain + self.joined:
            copy.wait_recv()
        own = self.place.rows(0, 0, self.rows), self.cols
        self.total[:, self.cols] = (
            self.grads[own].astype(f32) + self.near[0].astype(f32) + self.near[1].astype(f32)
        )

    def drain(self):
        for copy in self.away + self.plain + self.joined:
            copy.wait_send()

        @pl.when(self.place.outer)
        def _():
            for copy in self.enter:
                copy.wait_send()

        @pl.when(self.place.inner)
        def _():
            for copy in self.between + [self.leave]:
                copy.wait_send()


class Spread:
    def __init__(self, place, along, sources, slots, send, recv, base):
        rows = slice(0, sources[0].shape[0])
        if along == "tp":
            self.copies = [
                remote(sources[0], slots.at[rows], send.at[base], recv.at[base], place.other())
            ]
            return
        self.copies = [
            remote(
                sources[d - 1],
                slots.at[d - 1, rows],
                send.at[base + d - 1],
                recv.at[base + d - 1],
                place.device(d, 0) if along == "z" else place.device(0, d),
            )
            for d in (1, 2, 3)
        ]

    def start(self):
        for copy in self.copies:
            copy.start()

    def wait(self):
        for copy in self.copies:
            copy.wait_recv()

    def drain(self):
        for copy in self.copies:
            copy.wait_send()


def mul(a, b):
    return lax.dot_general(a, b, (((1,), (0,)), ((), ())), preferred_element_type=f32)


def mul_t(a, b):
    return lax.dot_general(a, b, (((1,), (1,)), ((), ())), preferred_element_type=f32)


def fold(x):
    return jnp.sum(x.reshape(x.shape[0] // 8, 8, x.shape[1]), axis=0)


def mean(x):
    return jnp.mean(x, axis=-1, keepdims=True)


def exact(a, b, i, j):
    return lax.dot_general(
        a, b, (((i,), (j,)), ((), ())), precision=highest, preferred_element_type=f32
    )


def chosen(place, count, width):
    own = count // place.sub
    entry = lax.broadcasted_iota(jnp.int32, (count, width), 0)
    column = lax.broadcasted_iota(jnp.int32, (count, width), 1)
    low = lax.div(entry, own)
    home = (place.place * place.sub + low) * lax.axis_size("tp") + lax.axis_index("tp")
    return jnp.where(column == home * own + lax.rem(entry, own), 1.0, 0.0)


PAIR = 2 * HD
TOP = math.sqrt(2.0 / math.pi)


def layer_kernel(sub, names, *refs):
    k = types.SimpleNamespace(**dict(zip(names, refs, strict=True)))
    place = Place(sub)
    side = lax.axis_index("tp")
    x_ref = k.rows_in
    total_rows, width = x_ref.shape
    half = total_rows // 2
    tp_send, tp_recv = k.tp_send, k.tp_recv
    per = k.steps.shape[1]
    seqs = k.feats.shape[0]
    pairs = k.mixed.shape[1] // PAIR
    hidden_width = k.bup.shape[1]
    own0 = pl.multiple_of(side * half, half)
    far0 = pl.multiple_of((1 - side) * half, half)
    first_len = k.lengths[0, 0]
    both_len = first_len + k.lengths[0, 1]

    def segment(start, count):
        row = lax.broadcasted_iota(jnp.int32, (count, 1), 0) + start
        return jnp.where(row < first_len, 0, jnp.where(row < both_len, 1, 2))

    def swap(n, src, dst):
        return remote(src, dst, tp_send.at[n], tp_recv.at[n], place.other())

    def cut_of(j, part_index):
        return slice((3 * j + part_index) * PAIR, (3 * j + part_index + 1) * PAIR)

    def pair_of(j):
        return slice(j * PAIR, (j + 1) * PAIR)

    bring_x = pltpu.make_async_copy(k.x, x_ref, k.local.at[0])
    bring_cot = pltpu.make_async_copy(k.cot, k.cot_in, k.local.at[1])
    bring_x.start()
    bring_cot.start()
    for j in range(pairs):
        for n, source in enumerate((k.wq, k.wk, k.wv)):
            k.w0[:, cut_of(j, n)] = source[:, pair_of(j)].astype(bf16)
        k.bqkv[:, cut_of(j, 0)] = k.bq[pair_of(j)].reshape(1, PAIR)
        k.bqkv[:, cut_of(j, 1)] = jnp.zeros((1, PAIR), f32)
        k.bqkv[:, cut_of(j, 2)] = k.bv[pair_of(j)].reshape(1, PAIR)
    k.bup[...] = k.bu[...].reshape(1, hidden_width)
    k.w1[...] = k.wo[...].astype(bf16)
    k.w2[...] = k.wu[...].astype(bf16)
    k.w3[...] = k.wd[...].astype(bf16)
    at_row = (place.z * sub + place.low) * 2
    seq_row = lax.broadcasted_iota(jnp.int32, (seqs, 1), 0)
    step = jnp.zeros((seqs, 1), f32)
    for n in range(per):
        step = jnp.where(seq_row == place.z * per + n, k.steps[0, n].astype(f32), step)
    column = lax.broadcasted_iota(jnp.int32, (1, TE), 1)
    number = jnp.where(column < TE // 2, column, column - TE // 2).astype(f32)
    angle = step * jnp.exp(-math.log(10000.0) * number / (TE // 2))
    wave = jnp.where(column < TE // 2, jnp.cos(angle), jnp.sin(angle)).astype(bf16).astype(f32)
    mine = (seq_row >= place.z * per) & (seq_row < (place.z + 1) * per)
    k.feats[...] = jnp.where(mine, wave, 0.0)
    given = (k.v0, k.v1, k.v2, k.v3, k.v4, k.v5, k.v6)
    count = k.v0.shape[1]
    for n, source in enumerate(given):
        k.given[n : n + 1, :] = source[...]
    k.given[7:8, :] = jnp.zeros((1, count), f32)
    vectors = exact(k.given[...], chosen(place, count, width), 1, 0)

    place.enter()
    small_send, small_recv = k.small_send, k.small_recv
    spread_z = Spread(place, "z", [k.feats] * 3, k.feat_z, small_send, small_recv, 0)
    spread_z.start()
    low_half, high_half = halves(slice(0, hidden_width))
    gather_a, gather_b, gather_c, gather_d = [
        Gather(place, shard, full, part, k.g_send, k.g_recv, g)
        for g, (shard, full, part) in enumerate(
            (
                (k.w0, k.full0, slice(0, k.w0.shape[1])),
                (k.w1, k.full1, slice(0, k.w1.shape[1])),
                (k.w2, k.full2, slice(0, hidden_width)),
                (k.w3, k.full3, low_half),
            )
        )
    ]
    climb = Climb(place, k.w3, k.full3, high_half, k.g_send, k.g_recv, 4)
    gather_a.begin()
    gather_a.own()
    spread_z.wait()
    k.feat_sum[...] = k.feats[...] + k.feat_z[0] + k.feat_z[1] + k.feat_z[2]
    spread_r = Spread(place, "r", [k.feat_sum] * 3, k.feat_in, small_send, small_recv, 3)
    spread_r.start()
    climb.begin()
    gather_b.own()
    k.all_feats[0] = k.feat_sum[...]

    @pl.loop(0, total_rows // 128)
    def _(i):
        start = pl.multiple_of(i * 128, 128)
        seg = segment(start, 128)
        lane = lax.rem(lax.broadcasted_iota(jnp.int32, (1, PAIR), 1), HD)
        k.mask_k[pl.ds(start, 128), :] = jnp.where(lane == seg, 1.0, 0.0).astype(bf16)
        k.mask_q[pl.ds(start, 128), :] = jnp.where((lane < 3) & (lane != seg), -1e30, 0.0).astype(
            bf16
        )

    spread_r.wait()
    for d in (1, 2, 3):
        k.all_feats[d] = k.feat_in[d - 1]
    every = k.all_feats[...].reshape(4 * seqs, TE)
    before = mul_t(every.astype(bf16), k.tw1t[...].astype(bf16)) + k.tb1[...]
    hidden = jax.nn.silu(before).astype(bf16)
    share = mul(hidden, k.tw2[...].astype(bf16))
    part = k.part
    for d in range(4):
        part[d, :seqs, :] = share[d * seqs : (d + 1) * seqs, :]
        part[d, seqs : seqs + 8, :] = vectors
    top = slice(0, seqs + 8)
    back = Spread(
        place, "r", [part.at[n, top] for n in (3, 2, 1)], k.part_in, small_send, small_recv, 6
    )
    back.start()
    gather_c.own()
    gather_b.begin()
    gather_a.turn()
    back.wait()
    in_plane = k.part_in
    k.part_sum[top] = part[0, top] + in_plane[0, top] + in_plane[1, top] + in_plane[2, top]
    over_z = Spread(place, "z", [k.part_sum.at[top]] * 3, k.part_z, small_send, small_recv, 9)
    over_z.start()
    gather_c.begin()
    gather_d.begin()
    gather_d.own()
    climb.pass_on()
    gather_a.pass_on(0)
    bring_x.wait()
    over_z.wait()
    from_z = k.part_z
    k.part_zsum[top] = k.part_sum[top] + from_z[0, top] + from_z[1, top] + from_z[2, top]
    pair = Spread(place, "tp", [k.part_zsum.at[top]], k.part_tp, small_send, small_recv, 12)
    pair.start()
    gather_b.turn()
    pair.wait()
    both = k.part_zsum[top] + k.part_tp[top]
    shared = k.shared
    shared[...] = both[seqs:]
    embed = both[:seqs] + shared[0:1, :]
    for s in (0, 1):
        k.embed[s : s + 1, :] = jnp.sum(
            jnp.where(seq_row == at_row + s, embed, 0.0), axis=0, keepdims=True
        )
    for one in (spread_z, spread_r, back, over_z, pair):
        one.drain()

    def vector(n):
        return shared[n : n + 1, :]

    def base_of(start, count):
        seg = segment(start, count)
        added = jnp.where(
            seg == 0, k.embed[0:1, :], jnp.where(seg == 1, k.embed[1:2, :], 0.0)
        )
        return x_ref[pl.ds(start, count), :].astype(f32) + added

    @pl.loop(0, total_rows // 128)
    def _(i):
        start = pl.multiple_of(i * 128, 128)
        k.base[pl.ds(start, 128), :] = base_of(start, 128).astype(bf16)

    def transpose(source, dest):
        @pl.loop(0, width // 128)
        def _(i):
            cut = pl.ds(pl.multiple_of(i * 128, 128), 128)
            dest[cut, :] = source[:, cut].T

    transpose(k.base, k.base_t)
    gather_a.pass_on(1, 2, 3)
    climb.rise()
    gather_a.finish()

    lane = lax.broadcasted_iota(jnp.int32, (1, PAIR), 1)
    lower = lane < HD
    scale = jnp.where(lax.broadcasted_iota(jnp.int32, (1, 3 * PAIR), 1) < PAIR, HD**-0.5, 1.0)
    qkv = k.qkv
    rows_at_once = 256

    def projection(j):
        cols = slice(3 * j * PAIR, 3 * (j + 1) * PAIR)

        @pl.loop(0, total_rows // 512)
        def _(i):
            rows = pl.ds(pl.multiple_of(i * 512, 512), 512)
            got = (mul(k.base[rows, :], k.full0[:, cols]) + k.bqkv[:, cols]) * scale
            qkv[rows, cols] = got.astype(bf16)

    def in_head(h):
        return lower if h == 0 else jnp.logical_not(lower)

    def with_mask(value, mask, h):
        return jnp.where(in_head(h), value.astype(f32), mask.astype(f32)).astype(bf16)

    def attend(j):
        for h in (0, 1):
            k.keys[h] = with_mask(qkv[:, cut_of(j, 1)], k.mask_k[...], h)

        @pl.loop(0, total_rows // rows_at_once)
        def _(i):
            rows = pl.ds(pl.multiple_of(i * rows_at_once, rows_at_once), rows_at_once)
            outs, logs = [], []
            for h in (0, 1):
                query = with_mask(qkv[rows, cut_of(j, 0)], k.mask_q[rows, :], h)
                scores = mul_t(query, k.keys[h])
                top = jnp.max(scores, axis=-1, keepdims=True)
                weight = jnp.exp(scores - top)
                total = jnp.sum(weight, axis=-1, keepdims=True)
                outs.append(mul(weight.astype(bf16), qkv[:, cut_of(j, 2)]) / total)
                logs.append(top + jnp.log(total))
            k.mixed[rows, j * PAIR : (j + 1) * PAIR] = jnp.where(lower, outs[0], outs[1]).astype(bf16)
            k.lse[rows, :] = jnp.where(lower, logs[0], logs[1])

        flipped = k.lse[...].T
        k.lse_t[j, 0:1, :] = flipped[0:1, :]
        k.lse_t[j, 1:2, :] = flipped[HD : HD + 1, :]

    projection(0)
    gather_c.turn()
    gather_b.pass_on()
    for j in range(1, pairs):
        projection(j)
    attend(0)
    gather_d.turn()
    gather_c.pass_on(0, 1)
    attend(1)
    gather_c.pass_on(2, 3)
    climb.hear(0)
    gather_d.pass_on()
    for j in range(2, pairs):
        attend(j)
    gather_b.finish()

    block = 256

    @pl.loop(0, half // block)
    def _(i):
        rows = pl.ds(pl.multiple_of(far0 + i * block, block), block)
        k.half_send[pl.ds(pl.multiple_of(i * block, block), block), :] = mul_t(
            k.mixed[rows, :], k.full1[...]
        ).astype(bf16)

    swap_a = swap(0, k.half_send, k.half_recv)
    swap_a.start()
    first_own, normed_one, inv_one = k.first_own, k.normed_one, k.inv_one

    @pl.loop(0, half // block)
    def _(i):
        here = pl.ds(pl.multiple_of(i * block, block), block)
        start = pl.multiple_of(own0 + i * block, block)
        first_own[here, :] = (
            base_of(start, block) + vector(1) + mul_t(k.mixed[pl.ds(start, block), :], k.full1[...])
        )

    climb.hear(1)
    swap_a.wait_recv()
    small = 128

    @pl.loop(0, half // small)
    def _(i):
        here = pl.ds(pl.multiple_of(i * small, small), small)
        summed = first_own[here, :] + k.half_recv[here, :].astype(f32)
        centered = summed - mean(summed)
        inv = lax.rsqrt(mean(centered * centered) + epsilon)
        normed = centered * inv
        first = normed * vector(2) + vector(3)
        first_own[here, :] = first
        normed_one[here, :] = normed
        inv_one[here, :] = jnp.broadcast_to(inv, (small, 128))
        k.first[pl.ds(pl.multiple_of(own0 + i * small, small), small), :] = first.astype(bf16)

    own = pl.ds(own0, half)
    far = pl.ds(far0, half)
    swap_b = swap(1, k.first.at[own, :], k.first.at[own, :])
    swap_b.start()
    gather_c.finish()
    chunk = 512
    blocks = hidden_width // chunk

    def rise(start):
        rows = pl.ds(start, half)

        @pl.loop(0, blocks)
        def _(i):
            cols = pl.ds(pl.multiple_of(i * chunk, chunk), chunk)
            up = mul(k.first[rows, :], k.full2[:, cols]) + k.bup[:, cols]
            square = up * up
            inner = up * (TOP + (TOP * 0.044715) * square)
            gate = 0.5 + 0.5 * jnp.tanh(inner)
            act = up * gate
            slope = gate + act * (1.0 - gate) * (2.0 * TOP + (6.0 * TOP * 0.044715) * square)
            k.act[rows, cols] = act.astype(bf16)
            k.slope[rows, cols] = slope.astype(bf16)

    rise(own0)
    swap_a.wait_send()
    swap_b.wait_recv()
    rise(far0)
    transpose(k.first, k.first_t)
    gather_d.finish()
    climb.hear(2)
    bring_cot.wait()

    @pl.loop(0, half // block)
    def _(i):
        rows = pl.ds(pl.multiple_of(far0 + i * block, block), block)
        k.half_send[pl.ds(pl.multiple_of(i * block, block), block), :] = mul_t(
            k.act[rows, :], k.full3[...]
        ).astype(bf16)

    swap_c = swap(2, k.half_send, k.half_recv)
    swap_c.start()
    own_sum = first_own

    @pl.loop(0, half // block)
    def _(i):
        here = pl.ds(pl.multiple_of(i * block, block), block)
        rows = pl.ds(pl.multiple_of(own0 + i * block, block), block)
        own_sum[here, :] = mul_t(k.act[rows, :], k.full3[...]) + first_own[here, :] + vector(4)

    swap_c.wait_recv()
    swap_b.wait_send()
    acc = k.acc
    acc[...] = jnp.zeros_like(acc)

    @pl.loop(0, half // small)
    def _(i):
        here = pl.ds(pl.multiple_of(i * small, small), small)
        summed = own_sum[here, :] + k.half_recv[here, :].astype(f32)
        centered = summed - mean(summed)
        inv = lax.rsqrt(mean(centered * centered) + epsilon)
        normed = centered * inv
        k.out_stage[here, :] = (normed * vector(5) + vector(6)).astype(bf16)
        start = pl.multiple_of(own0 + i * small, small)
        grad = jnp.where(segment(start, small) < 2, k.cot_in[here, :].astype(f32), 0.0)
        scaled = grad * vector(5)
        second = inv * (scaled - mean(scaled) - normed * mean(scaled * normed))
        own_sum[here, :] = second
        k.base[pl.ds(start, small), :] = second.astype(bf16)
        acc[0] += fold(grad * normed)
        acc[1] += fold(grad)
        acc[2] += fold(second)

    send_out = pltpu.make_async_copy(k.out_stage, k.out, k.local.at[2])
    send_out.start()
    swap_d = swap(3, k.base.at[own, :], k.base.at[own, :])
    swap_d.start()
    acc_up = k.acc_up
    acc_up[...] = jnp.zeros_like(acc_up)

    def fall(start):
        rows = pl.ds(start, half)

        @pl.loop(0, blocks)
        def _(i):
            cols = pl.ds(pl.multiple_of(i * chunk, chunk), chunk)
            grad = mul(k.base[rows, :], k.full3[:, cols]) * k.slope[rows, cols].astype(f32)
            k.slope[rows, cols] = grad.astype(bf16)
            acc_up[:, cols] += fold(grad)

    descend = Descend(
        place, k.grad0, k.total0, high_half, k.deep, k.deep_far, k.deep_near, k.r_send, k.r_recv, 0
    )
    sum_down, sum_up, sum_out, *sum_pairs = [
        Reduce(
            place, many(k, "grad", g), many(k, "total", g), part,
            many(k, "near", g), many(k, "ring", g), many(k, "high", g), k.r_send, k.r_recv, 1 + g,
        )
        for g, part in enumerate(
            [low_half, slice(0, hidden_width), slice(0, pairs * PAIR)] + [slice(0, 3 * PAIR)] * pairs
        )
    ]

    def weight_grad(dest, left_t, right, source_col, dest_col, count, step):
        @pl.loop(0, count // step)
        def _(i):
            to = pl.ds(pl.multiple_of(dest_col + i * step, 128), step)
            source = pl.ds(pl.multiple_of(source_col + i * step, 128), step)
            dest[:, to] = mul(left_t[...], right[:, source]).astype(bf16)

    fall(own0)
    swap_c.wait_send()
    swap_d.wait_recv()
    transpose(k.base, k.grad_t)
    middle = hidden_width // 2
    weight_grad(k.grad0, k.grad_t, k.act, middle, middle, middle, 256)
    descend.begin()
    weight_grad(k.grad0, k.grad_t, k.act, 0, 0, middle, 256)
    sum_down.begin()
    fall(far0)

    @pl.loop(0, half // block)
    def _(i):
        rows = pl.ds(pl.multiple_of(far0 + i * block, block), block)
        k.half_send[pl.ds(pl.multiple_of(i * block, block), block), :] = mul_t(
            k.slope[rows, :], k.full2[...]
        ).astype(bf16)

    swap_e = swap(4, k.half_send, k.half_recv)
    swap_e.start()

    @pl.loop(0, half // block)
    def _(i):
        here = pl.ds(pl.multiple_of(i * block, block), block)
        rows = pl.ds(pl.multiple_of(own0 + i * block, block), block)
        own_sum[here, :] += mul_t(k.slope[rows, :], k.full2[...])

    swap_e.wait_recv()

    @pl.loop(0, half // small)
    def _(i):
        here = pl.ds(pl.multiple_of(i * small, small), small)
        grad = own_sum[here, :] + k.half_recv[here, :].astype(f32)
        normed = normed_one[here, :]
        scaled = grad * vector(2)
        r1 = inv_one[here, 0:1] * (scaled - mean(scaled) - normed * mean(scaled * normed))
        k.first[pl.ds(pl.multiple_of(own0 + i * small, small), small), :] = r1.astype(bf16)
        acc[3] += fold(grad * normed)
        acc[4] += fold(grad)
        acc[5] += fold(r1)

    swap_f = swap(5, k.first.at[own, :], k.first.at[own, :])
    swap_f.start()
    sum_down.join()
    weight_grad(k.grad1, k.first_t, k.slope, 0, 0, hidden_width, 512)
    sum_up.begin()
    descend.pass_in()
    swap_f.wait_recv()

    @pl.loop(0, total_rows // 512)
    def _(i):
        rows = pl.ds(pl.multiple_of(i * 512, 512), 512)
        k.grad_mixed[rows, :] = mul(k.first[rows, :], k.full1[...]).astype(bf16)

    transpose(k.first, k.grad_t)
    weight_grad(k.grad2, k.grad_t, k.mixed, 0, 0, pairs * PAIR, pairs * PAIR)
    sum_out.begin()

    grad_qkv = k.grad_qkv
    acc_qkv = k.acc_qkv

    def attend_back(j, midway):
        mixed_cut = slice(j * PAIR, (j + 1) * PAIR)
        for h in (0, 1):
            k.keys[h] = with_mask(qkv[:, cut_of(j, 0)], k.mask_q[...], h)
        product = k.grad_mixed[:, mixed_cut].astype(f32) * k.mixed[:, mixed_cut].astype(f32)
        flipped = product.T
        k.inner[0:1, :] = jnp.sum(flipped[:HD], axis=0, keepdims=True)
        k.inner[1:2, :] = jnp.sum(flipped[HD:], axis=0, keepdims=True)
        k.keys_t[...] = qkv[:, cut_of(j, 1)].T
        k.query_t[...] = jnp.zeros_like(k.query_t)

        steps = total_rows // rows_at_once

        def one_block(i):
            start = pl.multiple_of(i * rows_at_once, rows_at_once)
            rows = pl.ds(start, rows_at_once)
            grads_v, grads_k, query_t = [], [], []
            for h in (0, 1):
                key = with_mask(qkv[rows, cut_of(j, 1)], k.mask_k[rows, :], h)
                prob = jnp.exp(mul_t(key, k.keys[h]) - k.lse_t[j, h : h + 1, :])
                value = jnp.where(in_head(h), qkv[rows, cut_of(j, 2)].astype(f32), 0.0).astype(bf16)
                grad_prob = mul_t(value, k.grad_mixed[:, mixed_cut])
                grad_score = (prob * (grad_prob - k.inner[h : h + 1, :])).astype(bf16)
                grads_v.append(mul(prob.astype(bf16), k.grad_mixed[:, mixed_cut]))
                grads_k.append(mul(grad_score, qkv[:, cut_of(j, 0)]))
                query_t.append(mul(k.keys_t[h * HD : (h + 1) * HD, rows], grad_score))
            grad_k = jnp.where(lower, grads_k[0], grads_k[1]).astype(bf16)
            grad_v = jnp.where(lower, grads_v[0], grads_v[1]).astype(bf16)
            grad_qkv[rows, cut_of(j, 1)] = grad_k
            grad_qkv[rows, cut_of(j, 2)] = grad_v
            k.query_t[...] += jnp.concatenate(query_t, axis=0)

        pl.loop(0, steps // 2)(one_block)
        midway()
        pl.loop(steps // 2, steps)(one_block)
        grad_qkv[:, cut_of(j, 0)] = (k.query_t[...].T * HD**-0.5).astype(bf16)
        cols = slice(3 * j * PAIR, 3 * (j + 1) * PAIR)
        acc_qkv[:, cols] = fold(grad_qkv[:, cols].astype(f32))
        weight_grad(many(k, "grad", 3 + j), k.base_t, grad_qkv, 3 * j * PAIR, 0, 3 * PAIR, 3 * PAIR)
        sum_pairs[j].begin()

    attend_back(0, sum_down.cross)
    sum_up.join()
    descend.pass_out()
    attend_back(1, sum_out.join)
    descend.arrive()
    sum_up.cross()
    for j in range(2, pairs):
        attend_back(j, sum_pairs[j - 2].join)
    descend.join()
    sum_out.cross()

    in_send, in_recv = k.act.at[:, :width], k.act.at[:, width : 2 * width]

    @pl.loop(0, total_rows // block)
    def _(i):
        rows = pl.ds(pl.multiple_of(i * block, block), block)
        in_send[rows, :] = mul_t(grad_qkv[rows, :], k.full0[...]).astype(bf16)

    swap_g = swap(6, in_send, in_recv)
    swap_g.start()
    for j in range(pairs - 2, pairs - 1):
        sum_pairs[j].join()
    sum_down.finish()
    sum_pairs[0].cross()
    swap_g.wait_recv()
    ge = k.acc_ge
    ge[...] = jnp.zeros_like(ge)

    def settle(stage, base):
        @pl.loop(0, half // small)
        def _(i):
            start = pl.multiple_of(base + i * small, small)
            rows = pl.ds(start, small)
            grad = (in_send[rows, :].astype(f32) + in_recv[rows, :].astype(f32)) + k.first[
                rows, :
            ].astype(f32)
            stage[pl.ds(pl.multiple_of(i * small, small), small), :] = grad
            seg = segment(start, small)
            ge[0] += fold(jnp.where(seg == 0, grad, 0.0))
            ge[1] += fold(jnp.where(seg == 1, grad, 0.0))

    send_in = []
    for n, stage in enumerate((first_own, normed_one)):
        settle(stage, n * half)
        send_in.append(
            pltpu.make_async_copy(stage, k.grad_in.at[pl.ds(n * half, half), :], k.local.at[3 + n])
        )
        send_in[n].start()

    def row_of(x):
        return jnp.sum(x, axis=0, keepdims=True)

    sums = k.part.at[0]
    sums[...] = jnp.zeros_like(sums)
    for row, n in enumerate((5, 3, 4, 2, 0, 1)):
        sums[row : row + 1, :] = row_of(acc[n])
    up_row = row_of(acc_up[...])
    for n in range(hidden_width // width):
        sums[8 + n : 9 + n, :] = up_row[:, n * width : (n + 1) * width]
    qkv_row = row_of(acc_qkv[...])
    at = 8 + hidden_width // width
    sums[at : at + 1, :] = qkv_row[:, :width]
    sums[at + 1 : at + 2, : qkv_row.shape[1] - width] = qkv_row[:, width:]
    sums[16:, :] = jnp.where(
        seq_row == at_row, row_of(ge[0]), jnp.where(seq_row == at_row + 1, row_of(ge[1]), 0.0)
    )
    pair_sums = Spread(place, "tp", [sums], k.part_tp, small_send, small_recv, 13)
    pair_sums.start()
    sum_pairs[pairs - 1].join()
    pair_sums.wait()
    row = lax.broadcasted_iota(jnp.int32, sums.shape, 0)
    k.part_sum[...] = sums[...] + jnp.where(row < 8, k.part_tp[...], 0.0)
    sums_z = Spread(place, "z", [k.part_sum] * 3, k.part_z, small_send, small_recv, 14)
    sums_z.start()
    for j in range(1, pairs - 1):
        sum_pairs[j].cross()
    sums_z.wait()
    k.part_zsum[...] = k.part_sum[...] + k.part_z[0] + k.part_z[1] + k.part_z[2]
    sums_r = Spread(place, "r", [k.part_zsum] * 3, k.part_in, small_send, small_recv, 17)
    sums_r.start()
    descend.finish()
    sum_up.finish()
    sum_out.finish()
    sums_r.wait()
    k.all_sums[...] = (
        k.part_zsum[:16] + k.part_in[0, :16] + k.part_in[1, :16] + k.part_in[2, :16]
    )
    k.all_embed[0] = k.part_zsum[16:]
    for d in (1, 2, 3):
        k.all_embed[d] = k.part_in[d - 1, 16:]
    sum_pairs[pairs - 1].cross()
    for one in sum_pairs:
        one.finish()
    for one in (
        gather_a, gather_b, gather_c, gather_d, climb, descend, sum_down, sum_up, sum_out,
        *sum_pairs, pair_sums, sums_z, sums_r,
    ):
        one.drain()
    send_out.wait()
    for copy in send_in:
        copy.wait()
    for copy in (swap_d, swap_e, swap_f, swap_g):
        copy.wait_send()


def call_layer(sub, operands):
    rows, width = operands["x"].shape
    half = rows // 2
    mine, heads = operands["wo"].shape
    hidden = operands["bu"].shape[0]
    pairs = heads // PAIR
    seqs = 8 * sub
    count = operands["v0"].shape[1]
    tall = seqs + 16
    columns = [hidden, hidden, heads] + [3 * PAIR] * pairs
    shape = jax.ShapeDtypeStruct
    results = dict(
        out=shape((half, width), bf16),
        grad_in=shape((rows, width), f32),
        all_feats=shape((4, seqs, TE), f32),
        all_sums=shape((16, width), f32),
        all_embed=shape((4, seqs, width), f32),
    )
    for g, wide in enumerate(columns):
        results["total" + str(g)] = shape((mine, wide), f32)
    vm = pltpu.VMEM
    sem = pltpu.SemaphoreType.DMA
    scratch = dict(
        rows_in=vm((rows, width), bf16),
        cot_in=vm((half, width), bf16),
        out_stage=vm((half, width), bf16),
        w0=vm((mine, 3 * heads), bf16),
        w1=vm((mine, heads), bf16),
        w2=vm((mine, hidden), bf16),
        w3=vm((mine, hidden), bf16),
        bqkv=vm((1, 3 * heads), f32),
        bup=vm((1, hidden), f32),
        feats=vm((seqs, TE), f32),
        given=vm((8, count), f32),
        deep=vm((5, 4 * mine, hidden // 2), bf16),
        deep_far=vm((mine, hidden // 2), bf16),
        deep_near=vm((2, mine, hidden // 2), bf16),
        local=sem((5,)),
        full0=vm((width, 3 * heads), bf16),
        full1=vm((width, heads), bf16),
        full2=vm((width, hidden), bf16),
        full3=vm((width, hidden), bf16),
        feat_z=vm((3, seqs, TE), f32),
        feat_sum=vm((seqs, TE), f32),
        feat_in=vm((3, seqs, TE), f32),
        part=vm((4, tall, width), f32),
        part_in=vm((3, tall, width), f32),
        part_sum=vm((tall, width), f32),
        part_z=vm((3, tall, width), f32),
        part_zsum=vm((tall, width), f32),
        part_tp=vm((tall, width), f32),
        shared=vm((8, width), f32),
        embed=vm((8, width), f32),
        base=vm((rows, width), bf16),
        base_t=vm((width, rows), bf16),
        mask_q=vm((rows, PAIR), bf16),
        mask_k=vm((rows, PAIR), bf16),
        keys=vm((2, rows, PAIR), bf16),
        qkv=vm((rows, 3 * heads), bf16),
        mixed=vm((rows, heads), bf16),
        lse=vm((rows, PAIR), f32),
        lse_t=vm((pairs, 8, rows), f32),
        half_send=vm((half, width), bf16),
        half_recv=vm((half, width), bf16),
        first_own=vm((half, width), f32),
        normed_one=vm((half, width), f32),
        inv_one=vm((half, 128), f32),
        first=vm((rows, width), bf16),
        first_t=vm((width, rows), bf16),
        act=vm((rows, hidden), bf16),
        slope=vm((rows, hidden), bf16),
        acc=vm((6, 8, width), f32),
        acc_up=vm((8, hidden), f32),
        acc_qkv=vm((8, 3 * heads), f32),
        acc_ge=vm((2, 8, width), f32),
        grad_t=vm((width, rows), bf16),
        grad_mixed=vm((rows, heads), bf16),
        inner=vm((8, rows), f32),
        keys_t=vm((PAIR, rows), bf16),
        query_t=vm((PAIR, rows), f32),
        grad_qkv=vm((rows, 3 * heads), bf16),
        g_send=sem((5, 15)),
        g_recv=sem((5, 15)),
        r_send=sem((4 + pairs, 15)),
        r_recv=sem((4 + pairs, 15)),
        small_send=sem((20,)),
        small_recv=sem((20,)),
        tp_send=sem((7,)),
        tp_recv=sem((7,)),
    )
    for g, wide in enumerate(columns):
        scratch["grad" + str(g)] = vm((width, wide), bf16)
        part = wide // 2 if g == 0 else wide
        scratch["near" + str(g)] = vm((4, mine, part), bf16)
        scratch["ring" + str(g)] = vm((8, mine, part), bf16)
        scratch["high" + str(g)] = vm((3, mine, part), bf16)
    names = [*operands, *results, *scratch]
    spaces = dict(lengths=pltpu.SMEM, steps=pltpu.SMEM, x=pl.ANY, cot=pl.ANY, out=pl.ANY, grad_in=pl.ANY)
    spec = lambda n: pl.BlockSpec(memory_space=spaces.get(n, pltpu.VMEM))
    got = pl.pallas_call(
        functools.partial(layer_kernel, sub, names),
        out_shape=list(results.values()),
        in_specs=[spec(n) for n in operands],
        out_specs=[spec(n) for n in results],
        scratch_shapes=list(scratch.values()),
        compiler_params=pltpu.CompilerParams(
            collective_id=0, has_side_effects=True, vmem_limit_bytes=63_000 * 1024
        ),
        name="layer",
    )(*operands.values())
    return types.SimpleNamespace(**dict(zip(results, got, strict=True)))


def finish_kernel(dp_size, names, *refs):
    k = types.SimpleNamespace(**dict(zip(names, refs, strict=True)))
    moves = [
        pltpu.make_async_copy(k.out_from, k.out, k.local.at[0]),
        pltpu.make_async_copy(k.grad_from, k.grad_in, k.local.at[1]),
    ]
    for move in moves:
        move.start()
    feats, embeds = k.feats[...], k.embeds[...]
    before = mul_t(feats.astype(bf16), k.tw1t[...].astype(bf16)) + k.tb1[...]
    gate = jax.nn.sigmoid(before)
    hidden = (before * gate).astype(bf16).astype(f32)
    grad_hidden = exact(embeds, k.tw2[...].astype(bf16).astype(f32), 1, 1)
    grad_before = grad_hidden * (gate * (1.0 + before * (1.0 - gate)))
    k.g_tw2[...] = exact(hidden, embeds, 0, 0)
    k.g_tw1t[...] = exact(grad_before, feats, 0, 0)
    k.g_tb1[...] = jnp.sum(grad_before, axis=0, keepdims=True)
    sums = k.sums[...]
    width = sums.shape[1]
    row = lax.broadcasted_iota(jnp.int32, (8, 1), 0)
    vectors = jnp.where(row == 6, jnp.sum(embeds, axis=0, keepdims=True), sums[:8])
    count = k.tb1.shape[1]
    start = (lax.axis_index("dp") * lax.axis_size("tp") + lax.axis_index("tp")) * count
    entry = lax.broadcasted_iota(jnp.int32, (count, width), 0)
    column = lax.broadcasted_iota(jnp.int32, (count, width), 1)
    picked = exact(vectors, jnp.where(column == start + entry, 1.0, 0.0), 1, 1)
    for n, dest in enumerate((k.g_bout, k.g_g1, k.g_s1, k.g_bdown, k.g_g2, k.g_s2, k.g_tb2)):
        dest[...] = picked[n : n + 1, :]
    hidden_width = k.g_bup.shape[0]
    for n in range(hidden_width // width):
        k.g_bup[n * width : (n + 1) * width] = sums[8 + n, :]
    at = 8 + hidden_width // width
    pairs = k.g_bq.shape[0] // PAIR
    for j in range(pairs):
        here = slice(j * PAIR, (j + 1) * PAIR)
        source = many(k, "pair", j)
        for n, dest in enumerate((k.g_wq, k.g_wk, k.g_wv)):
            dest[:, here] = source[:, n * PAIR : (n + 1) * PAIR]
        for n, dest in ((0, k.g_bq), (2, k.g_bv)):
            first = (3 * j + n) * PAIR
            dest[here] = sums[at + first // width, first % width : first % width + PAIR]
    k.g_wo[...] = k.sum_out[...]
    k.g_wu[...] = k.sum_up[...]
    k.g_wd[...] = k.sum_down[...]
    for move in moves:
        move.wait()


def call_finish(dp_size, operands, hidden):
    shape = jax.ShapeDtypeStruct
    own = operands["tb1"].shape[1]
    width = operands["sums"].shape[1]
    mine, heads = operands["sum_out"].shape
    line = shape((1, own), f32)
    matrix = shape((mine, heads), f32)
    wide = shape((mine, hidden), f32)
    results = dict(
        out=shape(operands["out_from"].shape, bf16),
        grad_in=shape(operands["grad_from"].shape, f32),
        g_tw1t=shape((own, TE), f32),
        g_tb1=line,
        g_tw2=shape((own, width), f32),
        g_tb2=line,
        g_wq=matrix,
        g_bq=shape((heads,), f32),
        g_wk=matrix,
        g_wv=matrix,
        g_bv=shape((heads,), f32),
        g_wo=matrix,
        g_bout=line,
        g_g1=line,
        g_s1=line,
        g_wu=wide,
        g_bup=shape((hidden,), f32),
        g_wd=wide,
        g_bdown=line,
        g_g2=line,
        g_s2=line,
    )
    scratch = dict(local=pltpu.SemaphoreType.DMA((2,)))
    names = [*operands, *results, *scratch]
    spaces = dict(out_from=pl.ANY, grad_from=pl.ANY, out=pl.ANY, grad_in=pl.ANY)
    spec = lambda n: pl.BlockSpec(memory_space=spaces.get(n, pltpu.VMEM))
    got = pl.pallas_call(
        functools.partial(finish_kernel, dp_size, names),
        out_shape=list(results.values()),
        in_specs=[spec(n) for n in operands],
        out_specs=[spec(n) for n in results],
        scratch_shapes=list(scratch.values()),
        compiler_params=pltpu.CompilerParams(vmem_limit_bytes=61_000 * 1024),
        name="finish",
    )(*operands.values())
    return types.SimpleNamespace(**dict(zip(results, got, strict=True)))


def on_device(
    inputs, cotangent, seq_lengths, timesteps, time_w1, time_b1, time_w2, time_b2,
    w_query, b_query, w_key, w_value, b_value, w_out, b_out, norm1_gain, norm1_bias,
    w_up, b_up, w_down, b_down, norm2_gain, norm2_bias,
):
    dp = lax.axis_size("dp")
    sub = dp // SUPER
    low = [[q * sub + l for l in range(sub)] for q in range(SUPER)]
    head_width = w_query.shape[1]

    def near(value, axis=0):
        if sub == 1:
            return value
        return lax.all_gather(value, "dp", axis=axis, tiled=True, axis_index_groups=low)

    def line(value):
        return near(value)[None, :]

    steps = timesteps
    if sub > 1:
        steps = near(timesteps.astype(f32)).astype(jnp.int32).reshape(1, -1)
    got = call_layer(
        sub,
        dict(
            lengths=seq_lengths,
            steps=steps,
            x=inputs,
            cot=cotangent,
            wq=near(w_query),
            wk=near(w_key),
            wv=near(w_value),
            wo=near(w_out.T),
            wu=near(w_up),
            wd=near(w_down.T),
            bq=b_query,
            bv=b_value,
            bu=b_up,
            tw1t=near(time_w1.T),
            tb1=line(time_b1),
            tw2=near(time_w2),
            v0=line(time_b2),
            v1=line(b_out),
            v2=line(norm1_gain),
            v3=line(norm1_bias),
            v4=line(b_down),
            v5=line(norm2_gain),
            v6=line(norm2_bias),
        ),
    )
    sums, embeds, feats = got.all_sums, got.all_embed, got.all_feats
    pairs = head_width // PAIR
    totals = [many(got, "total", g) for g in range(3 + pairs)]
    if sub > 1:
        sums, embeds = lax.psum((sums, embeds), "dp", axis_index_groups=low)
        totals = [
            lax.psum_scatter(one, "dp", scatter_dimension=0, tiled=True, axis_index_groups=low)
            for one in totals
        ]
    operands = dict(
        out_from=got.out,
        grad_from=got.grad_in,
        sums=sums,
        embeds=embeds.reshape(-1, embeds.shape[-1]),
        feats=feats.reshape(-1, TE),
        tw1t=time_w1.T,
        tb1=time_b1[None, :],
        tw2=time_w2,
        sum_down=totals[0],
        sum_up=totals[1],
        sum_out=totals[2],
    )
    for j in range(pairs):
        operands["pair" + str(j)] = totals[3 + j]
    done = call_finish(dp, operands, b_up.shape[0])
    return (
        done.out,
        done.grad_in,
        done.g_tw1t.T,
        done.g_tb1[0],
        done.g_tw2,
        done.g_tb2[0],
        done.g_wq,
        done.g_bq,
        done.g_wk,
        done.g_wv,
        done.g_bv,
        done.g_wo.T,
        done.g_bout[0],
        done.g_g1[0],
        done.g_s1[0],
        done.g_wu,
        done.g_bup,
        done.g_wd.T,
        done.g_bdown[0],
        done.g_g2[0],
        done.g_s2[0],
    )


def solution(mesh):
    placed = (
        P("dp", None),
        P(("dp", "tp"), None),
        P("dp", None),
        P("dp", None),
        P(None, ("dp", "tp")),
        P(("dp", "tp")),
        P(("dp", "tp"), None),
        P(("dp", "tp")),
        P("dp", "tp"),
        P("tp"),
        P("dp", "tp"),
        P("dp", "tp"),
        P("tp"),
        P("tp", "dp"),
        P(("dp", "tp")),
        P(("dp", "tp")),
        P(("dp", "tp")),
        P("dp", "tp"),
        P("tp"),
        P("tp", "dp"),
        P(("dp", "tp")),
        P(("dp", "tp")),
        P(("dp", "tp")),
    )
    return jax.shard_map(
        on_device,
        mesh=mesh,
        in_specs=placed,
        out_specs=(
            P(("dp", "tp"), None),
            P("dp", None),
            P(None, ("dp", "tp")),
            P(("dp", "tp")),
            P(("dp", "tp"), None),
            P(("dp", "tp")),
            P("dp", "tp"),
            P("tp"),
            P("dp", "tp"),
            P("dp", "tp"),
            P("tp"),
            P("tp", "dp"),
            P(("dp", "tp")),
            P(("dp", "tp")),
            P(("dp", "tp")),
            P("dp", "tp"),
            P("tp"),
            P("tp", "dp"),
            P(("dp", "tp")),
            P(("dp", "tp")),
            P(("dp", "tp")),
        ),
        check_vma=False,
    )
```

```python
import functools
import math
import types

import jax
import jax.numpy as jnp
from jax import lax
from jax.experimental import pallas as pl
from jax.experimental.pallas import tpu as pltpu
from jax.sharding import PartitionSpec as P

HD = 64
TE = 128
SUPER = 16

epsilon = 1e-05
highest = lax.Precision.HIGHEST
f32 = jnp.float32
bf16 = jnp.bfloat16


class Place:
    def __init__(self, sub):
        self.sub = sub
        index = lax.axis_index("dp")
        self.low = lax.rem(index, sub)
        self.place = lax.div(index, sub)
        self.z = lax.div(self.place, 4)
        self.p = lax.rem(self.place, 4)
        self.r = self.ring(self.p)
        self.outer = (self.z == 0) | (self.z == 3)
        self.inner = (self.z == 1) | (self.z == 2)

    @staticmethod
    def ring(v):
        half = lax.div(v, 2)
        return 2 * half + lax.rem(lax.rem(v, 2) + half, 2)

    def spot(self, dz, dr):
        z = lax.rem(self.z + dz + 4, 4)
        p = self.ring(lax.rem(self.r + dr + 4, 4))
        return z * 4 + p

    def device(self, dz, dr):
        return {"dp": self.spot(dz, dr) * self.sub + self.low}

    def beside(self, step):
        plane = lax.rem(self.z + step + 4, 4)
        return {"dp": (plane * 4 + self.p) * self.sub + self.low}

    def other(self):
        return {"tp": 1 - lax.axis_index("tp")}

    def rows(self, dz, dr, count):
        return pl.ds(pl.multiple_of(self.spot(dz, dr) * count, 16), count)

    def enter(self):
        barrier = pltpu.get_barrier_semaphore()
        for peer in (
            [self.device(d, 0) for d in (1, 2, 3)]
            + [self.device(0, d) for d in (1, 2, 3)]
            + [self.other()]
        ):
            pl.semaphore_signal(barrier, inc=1, device_id=peer, device_id_type=pl.DeviceIdType.MESH)
        pl.semaphore_wait(barrier, 7)


def remote(src, dst, send, recv, device):
    return pltpu.make_async_remote_copy(
        src_ref=src,
        dst_ref=dst,
        send_sem=send,
        recv_sem=recv,
        device_id=device,
        device_id_type=pl.DeviceIdType.MESH,
    )


def many(k, name, g):
    return getattr(k, name + str(g))


class Gather:
    def __init__(self, place, shard, full, cols, send, recv, g):
        rows = shard.shape[0]
        at = lambda dz, dr: full.at[place.rows(dz, dr, rows), cols]
        self.place, self.shard, self.full, self.count = place, shard, full, rows
        self.cols = cols
        shard = shard.at[:, cols]
        self.to_planes = [
            remote(shard, at(0, 0), send.at[g, d - 1], recv.at[g, d - 1], place.device(d, 0))
            for d in (1, 2, 3)
        ]
        self.around = []
        self.relay = []
        for d in range(4):
            source = shard if d == 0 else at(-d, 0)
            self.around.append(
                [
                    remote(
                        source,
                        at(-d, 0),
                        send.at[g, 3 + 2 * d + k],
                        recv.at[g, 3 + 2 * d + k],
                        place.device(0, 1 - 2 * k),
                    )
                    for k in (0, 1)
                ]
            )
            k = d // 2
            self.relay.append(
                remote(
                    at(-d, 2 * k - 1),
                    at(-d, 2 * k - 1),
                    send.at[g, 11 + d],
                    recv.at[g, 11 + d],
                    place.device(0, 1 - 2 * k),
                )
            )

    def begin(self):
        for copy in self.to_planes:
            copy.start()
        self.full[self.place.rows(0, 0, self.count), self.cols] = self.shard[:, self.cols]

    def own(self):
        for copy in self.around[0]:
            copy.start()

    def turn(self, *which):
        for d in which or (1, 2, 3):
            self.to_planes[d - 1].wait_recv()
            for copy in self.around[d]:
                copy.start()

    def pass_on(self, *which):
        for d in which or (0, 1, 2, 3):
            self.around[d][d // 2].wait_recv()
            self.relay[d].start()

    def finish(self):
        for d in range(4):
            self.around[d][1 - d // 2].wait_recv()
            self.relay[d].wait_recv()

    def drain(self):
        for copy in self.to_planes + [c for pair in self.around for c in pair] + self.relay:
            copy.wait_send()


def halves(cols):
    middle = (cols.start + cols.stop) // 2
    return slice(cols.start, middle), slice(middle, cols.stop)


class Climb:
    def __init__(self, place, shard, full, cols, send, recv, g):
        rows = shard.shape[0]
        self.place, self.shard, self.full, self.count, self.cols = place, shard, full, rows, cols
        z = place.z
        at = lambda dr, part: full.at[place.rows(0, dr, rows), part]
        slab = lambda plane: full.at[pl.ds(pl.multiple_of(plane * 4 * rows, 16), 4 * rows), cols]
        self.around = [
            remote(shard.at[:, cols], at(0, cols), send.at[g, n], recv.at[g, n], place.device(0, 1 - 2 * n))
            for n in (0, 1)
        ]
        self.relay = [
            remote(at(2 * n - 1, part), at(2 * n - 1, part), send.at[g, 2 + n], recv.at[g, 2 + n], place.device(0, 1 - 2 * n))
            for n, part in enumerate(halves(cols))
        ]
        self.up, self.down = [
            remote(slab(z), slab(z), send.at[g, 4 + n], recv.at[g, 4 + z], place.beside(1 - 2 * n))
            for n in (0, 1)
        ]
        self.heard = []
        table = [
            jnp.where(z == 0, 1, z - 1),
            jnp.where(z == 3, 1, jnp.where(z == 2, 3, 2)),
            jnp.where(z < 2, 3, 0),
        ]
        for n, plane in enumerate(table):
            self.heard.append(
                remote(
                    slab(plane), slab(plane), send.at[g, 6 + n], recv.at[g, 4 + plane],
                    place.beside(jnp.where(plane < z, 1, -1)),
                )
            )

    def begin(self):
        for copy in self.around:
            copy.start()
        self.full[self.place.rows(0, 0, self.count), self.cols] = self.shard[:, self.cols]

    def pass_on(self):
        for n in (0, 1):
            self.around[n].wait_recv()
            self.relay[n].start()

    def rise(self):
        for n in (0, 1):
            self.relay[n].wait_recv()
        pl.when(self.place.z < 3)(self.up.start)
        pl.when(self.place.z > 0)(self.down.start)

    def hear(self, n):
        self.heard[n].wait_recv()
        pl.when(self.place.inner)(self.heard[n].start)

    def drain(self):
        for copy in self.around + self.relay:
            copy.wait_send()
        pl.when(self.place.z < 3)(self.up.wait_send)
        pl.when(self.place.z > 0)(self.down.wait_send)
        for copy in self.heard:
            pl.when(self.place.inner)(copy.wait_send)


class Reduce:
    def __init__(self, place, grads, total, cols, first, second, third, send, recv, g):
        rows = total.shape[0]
        at = lambda dz, dr: grads.at[place.rows(dz, dr, rows), cols]
        self.place, self.grads, self.total, self.rows, self.cols = place, grads, total, rows, cols
        self.first, self.second, self.third = first, second, third
        self.far, self.near, self.up = [], [], []
        for d in range(4):
            k = d // 2
            self.far.append(
                remote(
                    at(d, 2), first.at[d], send.at[g, d], recv.at[g, d], place.device(0, 1 - 2 * k)
                )
            )
            self.near.append(
                [
                    remote(
                        at(d, 1 - 2 * j),
                        second.at[j * 4 + d],
                        send.at[g, 4 + 2 * d + j],
                        recv.at[g, 4 + 2 * d + j],
                        place.device(0, 1 - 2 * j),
                    )
                    for j in (0, 1)
                ]
            )
        for d in (1, 2, 3):
            self.up.append(
                remote(
                    at(d, 0),
                    third.at[d - 1],
                    send.at[g, 11 + d],
                    recv.at[g, 11 + d],
                    place.device(d, 0),
                )
            )

    def begin(self):
        for d in range(4):
            self.far[d].start()
        for d in range(4):
            self.near[d][1 - d // 2].start()

    def join(self):
        for d in range(4):
            k = d // 2
            self.far[d].wait_recv()
            here = self.place.rows(d, 1 - 2 * k, self.rows), self.cols
            self.grads[here] = (self.grads[here].astype(f32) + self.first[d].astype(f32)).astype(bf16)
            self.near[d][k].start()

    def cross(self):
        for d in (1, 2, 3, 0):
            for j in (0, 1):
                self.near[d][j].wait_recv()
            here = self.place.rows(d, 0, self.rows), self.cols
            summed = (
                self.grads[here].astype(f32)
                + self.second[d].astype(f32)
                + self.second[4 + d].astype(f32)
            )
            if d:
                self.grads[here] = summed.astype(bf16)
                self.up[d - 1].start()
            else:
                self.total[:, self.cols] = summed

    def finish(self):
        for copy in self.up:
            copy.wait_recv()
        self.total[:, self.cols] += (
            self.third[0].astype(f32) + self.third[1].astype(f32) + self.third[2].astype(f32)
        )

    def drain(self):
        for copy in self.far + [c for pair in self.near for c in pair] + self.up:
            copy.wait_send()


class Descend:
    def __init__(self, place, grads, total, cols, deep, far, near, send, recv, g):
        rows = total.shape[0]
        self.place, self.grads, self.total, self.rows, self.cols = place, grads, total, rows, cols
        self.deep, self.far, self.near = deep, far, near
        lower = place.z < 2
        inward = jnp.where(lower, 1, -1)
        plane = lambda c: jnp.where(lower, c, 3 - c)
        self.slab = lambda c: (pl.ds(pl.multiple_of(plane(c) * 4 * rows, 16), 4 * rows), cols)
        part = halves(cols)
        self.part = part
        self.here = lambda dr, n: (place.rows(0, dr, rows), part[n])
        self.slot = [slice(p.start - cols.start, p.stop - cols.start) for p in part]

        def copy(source, dest, n, m, to):
            return remote(grads.at[source], dest, send.at[g, n], recv.at[g, m], to)

        ahead = place.beside(inward)
        self.enter = [copy(self.slab(3 - n), deep.at[n], n, n, ahead) for n in range(3)]
        self.between = [copy(self.slab(3 - n), deep.at[3 + n], 3 + n, 3 + n, ahead) for n in (0, 1)]
        self.leave = copy(self.slab(0), deep.at[0], 5, 5, place.beside(-inward))
        side = [place.device(0, 1), place.device(0, -1)]
        self.away = [
            copy(self.here(2, n), far.at[:, self.slot[n]], 6 + n, 6 + n, side[n]) for n in (0, 1)
        ]
        self.plain = [
            copy(self.here(1 - 2 * n, 1 - n), near.at[n, :, self.slot[1 - n]], 8 + n, 8 + n, side[n])
            for n in (0, 1)
        ]
        self.joined = [
            copy(self.here(1 - 2 * n, n), near.at[n, :, self.slot[n]], 10 + n, 10 + n, side[n])
            for n in (0, 1)
        ]

    def add(self, here, *terms):
        total = self.grads[here].astype(f32)
        for term in terms:
            total += term.astype(f32)
        self.grads[here] = total.astype(bf16)

    def begin(self):
        @pl.when(self.place.outer)
        def _():
            for copy in self.enter:
                copy.start()

    def pass_in(self):
        @pl.when(self.place.inner)
        def _():
            for n in (0, 1):
                self.enter[n].wait_recv()
                self.add(self.slab(3 - n), self.deep[n])
                self.between[n].start()

    def pass_out(self):
        @pl.when(self.place.inner)
        def _():
            self.between[0].wait_recv()
            self.add(self.slab(0), self.deep[3])
            self.leave.start()

    def arrive(self):
        @pl.when(self.place.inner)
        def _():
            self.enter[2].wait_recv()
            self.between[1].wait_recv()
            self.add(self.slab(1), self.deep[2], self.deep[4])

        @pl.when(self.place.outer)
        def _():
            self.leave.wait_recv()
            self.add(self.slab(0), self.deep[0])

        for copy in self.away + self.plain:
            copy.start()

    def join(self):
        for n in (0, 1):
            self.away[n].wait_recv()
            self.add(self.here(1 - 2 * n, n), self.far[:, self.slot[n]])
            self.joined[n].start()

    def finish(self):
        for copy in self.plain + self.joined:
            copy.wait_recv()
        own = self.place.rows(0, 0, self.rows), self.cols
        self.total[:, self.cols] = (
            self.grads[own].astype(f32) + self.near[0].astype(f32) + self.near[1].astype(f32)
        )

    def drain(self):
        for copy in self.away + self.plain + self.joined:
            copy.wait_send()

        @pl.when(self.place.outer)
        def _():
            for copy in self.enter:
                copy.wait_send()

        @pl.when(self.place.inner)
        def _():
            for copy in self.between + [self.leave]:
                copy.wait_send()


class Spread:
    def __init__(self, place, along, sources, slots, send, recv, base):
        rows = slice(0, sources[0].shape[0])
        if along == "tp":
            self.copies = [
                remote(sources[0], slots.at[rows], send.at[base], recv.at[base], place.other())
            ]
            return
        self.copies = [
            remote(
                sources[d - 1],
                slots.at[d - 1, rows],
                send.at[base + d - 1],
                recv.at[base + d - 1],
                place.device(d, 0) if along == "z" else place.device(0, d),
            )
            for d in (1, 2, 3)
        ]

    def start(self):
        for copy in self.copies:
            copy.start()

    def wait(self):
        for copy in self.copies:
            copy.wait_recv()

    def drain(self):
        for copy in self.copies:
            copy.wait_send()


def mul(a, b):
    return lax.dot_general(a, b, (((1,), (0,)), ((), ())), preferred_element_type=f32)


def mul_t(a, b):
    return lax.dot_general(a, b, (((1,), (1,)), ((), ())), preferred_element_type=f32)


def fold(x):
    return jnp.sum(x.reshape(x.shape[0] // 8, 8, x.shape[1]), axis=0)


def mean(x):
    return jnp.mean(x, axis=-1, keepdims=True)


def exact(a, b, i, j):
    return lax.dot_general(
        a, b, (((i,), (j,)), ((), ())), precision=highest, preferred_element_type=f32
    )


def chosen(place, count, width):
    own = count // place.sub
    entry = lax.broadcasted_iota(jnp.int32, (count, width), 0)
    column = lax.broadcasted_iota(jnp.int32, (count, width), 1)
    low = lax.div(entry, own)
    home = (place.place * place.sub + low) * lax.axis_size("tp") + lax.axis_index("tp")
    return jnp.where(column == home * own + lax.rem(entry, own), 1.0, 0.0)


PAIR = 2 * HD
TOP = math.sqrt(2.0 / math.pi)


def layer_kernel(sub, names, *refs):
    k = types.SimpleNamespace(**dict(zip(names, refs, strict=True)))
    place = Place(sub)
    side = lax.axis_index("tp")
    x_ref = k.rows_in
    total_rows, width = x_ref.shape
    half = total_rows // 2
    tp_send, tp_recv = k.tp_send, k.tp_recv
    per = k.steps.shape[1]
    seqs = k.feats.shape[0]
    pairs = k.mixed.shape[1] // PAIR
    hidden_width = k.bup.shape[1]
    own0 = pl.multiple_of(side * half, half)
    far0 = pl.multiple_of((1 - side) * half, half)
    first_len = k.lengths[0, 0]
    both_len = first_len + k.lengths[0, 1]

    def segment(start, count):
        row = lax.broadcasted_iota(jnp.int32, (count, 1), 0) + start
        return jnp.where(row < first_len, 0, jnp.where(row < both_len, 1, 2))

    def swap(n, src, dst):
        return remote(src, dst, tp_send.at[n], tp_recv.at[n], place.other())

    def cut_of(j, part_index):
        return slice((3 * j + part_index) * PAIR, (3 * j + part_index + 1) * PAIR)

    def pair_of(j):
        return slice(j * PAIR, (j + 1) * PAIR)

    bring_x = pltpu.make_async_copy(k.x, x_ref, k.local.at[0])
    bring_cot = pltpu.make_async_copy(k.cot, k.cot_in, k.local.at[1])
    bring_x.start()
    bring_cot.start()
    for j in range(pairs):
        for n, source in enumerate((k.wq, k.wk, k.wv)):
            k.w0[:, cut_of(j, n)] = source[:, pair_of(j)].astype(bf16)
        k.bqkv[:, cut_of(j, 0)] = k.bq[pair_of(j)].reshape(1, PAIR)
        k.bqkv[:, cut_of(j, 1)] = jnp.zeros((1, PAIR), f32)
        k.bqkv[:, cut_of(j, 2)] = k.bv[pair_of(j)].reshape(1, PAIR)
    k.bup[...] = k.bu[...].reshape(1, hidden_width)
    k.w1[...] = k.wo[...].astype(bf16)
    k.w2[...] = k.wu[...].astype(bf16)
    k.w3[...] = k.wd[...].astype(bf16)
    at_row = (place.z * sub + place.low) * 2
    seq_row = lax.broadcasted_iota(jnp.int32, (seqs, 1), 0)
    step = jnp.zeros((seqs, 1), f32)
    for n in range(per):
        step = jnp.where(seq_row == place.z * per + n, k.steps[0, n].astype(f32), step)
    column = lax.broadcasted_iota(jnp.int32, (1, TE), 1)
    number = jnp.where(column < TE // 2, column, column - TE // 2).astype(f32)
    angle = step * jnp.exp(-math.log(10000.0) * number / (TE // 2))
    wave = jnp.where(column < TE // 2, jnp.cos(angle), jnp.sin(angle)).astype(bf16).astype(f32)
    mine = (seq_row >= place.z * per) & (seq_row < (place.z + 1) * per)
    k.feats[...] = jnp.where(mine, wave, 0.0)
    given = (k.v0, k.v1, k.v2, k.v3, k.v4, k.v5, k.v6)
    count = k.v0.shape[1]
    for n, source in enumerate(given):
        k.given[n : n + 1, :] = source[...]
    k.given[7:8, :] = jnp.zeros((1, count), f32)
    vectors = exact(k.given[...], chosen(place, count, width), 1, 0)

    place.enter()
    small_send, small_recv = k.small_send, k.small_recv
    spread_z = Spread(place, "z", [k.feats] * 3, k.feat_z, small_send, small_recv, 0)
    spread_z.start()
    low_half, high_half = halves(slice(0, hidden_width))
    gather_a, gather_b, gather_c, gather_d = [
        Gather(place, shard, full, part, k.g_send, k.g_recv, g)
        for g, (shard, full, part) in enumerate(
            (
                (k.w0, k.full0, slice(0, k.w0.shape[1])),
                (k.w1, k.full1, slice(0, k.w1.shape[1])),
                (k.w2, k.full2, slice(0, hidden_width)),
                (k.w3, k.full3, low_half),
            )
        )
    ]
    climb = Climb(place, k.w3, k.full3, high_half, k.g_send, k.g_recv, 4)
    gather_a.begin()
    gather_a.own()
    spread_z.wait()
    k.feat_sum[...] = k.feats[...] + k.feat_z[0] + k.feat_z[1] + k.feat_z[2]
    spread_r = Spread(place, "r", [k.feat_sum] * 3, k.feat_in, small_send, small_recv, 3)
    spread_r.start()
    climb.begin()
    gather_b.own()
    k.all_feats[0] = k.feat_sum[...]

    @pl.loop(0, total_rows // 128)
    def _(i):
        start = pl.multiple_of(i * 128, 128)
        seg = segment(start, 128)
        lane = lax.rem(lax.broadcasted_iota(jnp.int32, (1, PAIR), 1), HD)
        k.mask_k[pl.ds(start, 128), :] = jnp.where(lane == seg, 1.0, 0.0).astype(bf16)
        k.mask_q[pl.ds(start, 128), :] = jnp.where((lane < 3) & (lane != seg), -1e30, 0.0).astype(
            bf16
        )

    spread_r.wait()
    for d in (1, 2, 3):
        k.all_feats[d] = k.feat_in[d - 1]
    every = k.all_feats[...].reshape(4 * seqs, TE)
    before = mul_t(every.astype(bf16), k.tw1t[...].astype(bf16)) + k.tb1[...]
    hidden = jax.nn.silu(before).astype(bf16)
    share = mul(hidden, k.tw2[...].astype(bf16))
    part = k.part
    for d in range(4):
        part[d, :seqs, :] = share[d * seqs : (d + 1) * seqs, :]
        part[d, seqs : seqs + 8, :] = vectors
    top = slice(0, seqs + 8)
    back = Spread(
        place, "r", [part.at[n, top] for n in (3, 2, 1)], k.part_in, small_send, small_recv, 6
    )
    back.start()
    gather_c.own()
    gather_b.begin()
    gather_a.turn()
    back.wait()
    in_plane = k.part_in
    k.part_sum[top] = part[0, top] + in_plane[0, top] + in_plane[1, top] + in_plane[2, top]
    over_z = Spread(place, "z", [k.part_sum.at[top]] * 3, k.part_z, small_send, small_recv, 9)
    over_z.start()
    gather_c.begin()
    gather_d.begin()
    gather_d.own()
    climb.pass_on()
    gather_a.pass_on(0)
    bring_x.wait()
    over_z.wait()
    from_z = k.part_z
    k.part_zsum[top] = k.part_sum[top] + from_z[0, top] + from_z[1, top] + from_z[2, top]
    pair = Spread(place, "tp", [k.part_zsum.at[top]], k.part_tp, small_send, small_recv, 12)
    pair.start()
    gather_b.turn()
    pair.wait()
    both = k.part_zsum[top] + k.part_tp[top]
    shared = k.shared
    shared[...] = both[seqs:]
    embed = both[:seqs] + shared[0:1, :]
    for s in (0, 1):
        k.embed[s : s + 1, :] = jnp.sum(
            jnp.where(seq_row == at_row + s, embed, 0.0), axis=0, keepdims=True
        )
    for one in (spread_z, spread_r, back, over_z, pair):
        one.drain()

    def vector(n):
        return shared[n : n + 1, :]

    def base_of(start, count):
        seg = segment(start, count)
        added = jnp.where(
            seg == 0, k.embed[0:1, :], jnp.where(seg == 1, k.embed[1:2, :], 0.0)
        )
        return x_ref[pl.ds(start, count), :].astype(f32) + added

    @pl.loop(0, total_rows // 128)
    def _(i):
        start = pl.multiple_of(i * 128, 128)
        k.base[pl.ds(start, 128), :] = base_of(start, 128).astype(bf16)

    def transpose(source, dest):
        @pl.loop(0, width // 128)
        def _(i):
            cut = pl.ds(pl.multiple_of(i * 128, 128), 128)
            dest[cut, :] = source[:, cut].T

    transpose(k.base, k.base_t)
    gather_a.pass_on(1, 2, 3)
    climb.rise()
    gather_a.finish()

    lane = lax.broadcasted_iota(jnp.int32, (1, PAIR), 1)
    lower = lane < HD
    scale = jnp.where(lax.broadcasted_iota(jnp.int32, (1, 3 * PAIR), 1) < PAIR, HD**-0.5, 1.0)
    qkv = k.qkv
    rows_at_once = 256

    def projection(j):
        cols = slice(3 * j * PAIR, 3 * (j + 1) * PAIR)

        @pl.loop(0, total_rows // 512)
        def _(i):
            rows = pl.ds(pl.multiple_of(i * 512, 512), 512)
            got = (mul(k.base[rows, :], k.full0[:, cols]) + k.bqkv[:, cols]) * scale
            qkv[rows, cols] = got.astype(bf16)

    def in_head(h):
        return lower if h == 0 else jnp.logical_not(lower)

    def with_mask(value, mask, h):
        return jnp.where(in_head(h), value.astype(f32), mask.astype(f32)).astype(bf16)

    def attend(j):
        for h in (0, 1):
            k.keys[h] = with_mask(qkv[:, cut_of(j, 1)], k.mask_k[...], h)

        @pl.loop(0, total_rows // rows_at_once)
        def _(i):
            rows = pl.ds(pl.multiple_of(i * rows_at_once, rows_at_once), rows_at_once)
            outs, logs = [], []
            for h in (0, 1):
                query = with_mask(qkv[rows, cut_of(j, 0)], k.mask_q[rows, :], h)
                scores = mul_t(query, k.keys[h])
                top = jnp.max(scores, axis=-1, keepdims=True)
                weight = jnp.exp(scores - top)
                total = jnp.sum(weight, axis=-1, keepdims=True)
                outs.append(mul(weight.astype(bf16), qkv[:, cut_of(j, 2)]) / total)
                logs.append(top + jnp.log(total))
            k.mixed[rows, j * PAIR : (j + 1) * PAIR] = jnp.where(lower, outs[0], outs[1]).astype(bf16)
            k.lse[rows, :] = jnp.where(lower, logs[0], logs[1])

        flipped = k.lse[...].T
        k.lse_t[j, 0:1, :] = flipped[0:1, :]
        k.lse_t[j, 1:2, :] = flipped[HD : HD + 1, :]

    projection(0)
    gather_c.turn()
    gather_b.pass_on()
    for j in range(1, pairs):
        projection(j)
    attend(0)
    gather_d.turn()
    gather_c.pass_on(0, 1)
    attend(1)
    gather_c.pass_on(2, 3)
    climb.hear(0)
    gather_d.pass_on()
    for j in range(2, pairs):
        attend(j)
    gather_b.finish()

    block = 256

    @pl.loop(0, half // block)
    def _(i):
        rows = pl.ds(pl.multiple_of(far0 + i * block, block), block)
        k.half_send[pl.ds(pl.multiple_of(i * block, block), block), :] = mul_t(
            k.mixed[rows, :], k.full1[...]
        ).astype(bf16)

    swap_a = swap(0, k.half_send, k.half_recv)
    swap_a.start()
    first_own, normed_one, inv_one = k.first_own, k.normed_one, k.inv_one

    @pl.loop(0, half // block)
    def _(i):
        here = pl.ds(pl.multiple_of(i * block, block), block)
        start = pl.multiple_of(own0 + i * block, block)
        first_own[here, :] = (
            base_of(start, block) + vector(1) + mul_t(k.mixed[pl.ds(start, block), :], k.full1[...])
        )

    climb.hear(1)
    swap_a.wait_recv()
    small = 128

    @pl.loop(0, half // small)
    def _(i):
        here = pl.ds(pl.multiple_of(i * small, small), small)
        summed = first_own[here, :] + k.half_recv[here, :].astype(f32)
        centered = summed - mean(summed)
        inv = lax.rsqrt(mean(centered * centered) + epsilon)
        normed = centered * inv
        first = normed * vector(2) + vector(3)
        first_own[here, :] = first
        normed_one[here, :] = normed
        inv_one[here, :] = jnp.broadcast_to(inv, (small, 128))
        k.first[pl.ds(pl.multiple_of(own0 + i * small, small), small), :] = first.astype(bf16)

    own = pl.ds(own0, half)
    far = pl.ds(far0, half)
    swap_b = swap(1, k.first.at[own, :], k.first.at[own, :])
    swap_b.start()
    gather_c.finish()
    chunk = 512
    blocks = hidden_width // chunk

    def rise(start):
        rows = pl.ds(start, half)

        @pl.loop(0, blocks)
        def _(i):
            cols = pl.ds(pl.multiple_of(i * chunk, chunk), chunk)
            up = mul(k.first[rows, :], k.full2[:, cols]) + k.bup[:, cols]
            square = up * up
            inner = up * (TOP + (TOP * 0.044715) * square)
            gate = 0.5 + 0.5 * jnp.tanh(inner)
            act = up * gate
            slope = gate + act * (1.0 - gate) * (2.0 * TOP + (6.0 * TOP * 0.044715) * square)
            k.act[rows, cols] = act.astype(bf16)
            k.slope[rows, cols] = slope.astype(bf16)

    rise(own0)
    swap_a.wait_send()
    swap_b.wait_recv()
    rise(far0)
    transpose(k.first, k.first_t)
    gather_d.finish()
    climb.hear(2)
    bring_cot.wait()

    @pl.loop(0, half // block)
    def _(i):
        rows = pl.ds(pl.multiple_of(far0 + i * block, block), block)
        k.half_send[pl.ds(pl.multiple_of(i * block, block), block), :] = mul_t(
            k.act[rows, :], k.full3[...]
        ).astype(bf16)

    swap_c = swap(2, k.half_send, k.half_recv)
    swap_c.start()
    own_sum = first_own

    @pl.loop(0, half // block)
    def _(i):
        here = pl.ds(pl.multiple_of(i * block, block), block)
        rows = pl.ds(pl.multiple_of(own0 + i * block, block), block)
        own_sum[here, :] = mul_t(k.act[rows, :], k.full3[...]) + first_own[here, :] + vector(4)

    swap_c.wait_recv()
    swap_b.wait_send()
    acc = k.acc
    acc[...] = jnp.zeros_like(acc)

    @pl.loop(0, half // small)
    def _(i):
        here = pl.ds(pl.multiple_of(i * small, small), small)
        summed = own_sum[here, :] + k.half_recv[here, :].astype(f32)
        centered = summed - mean(summed)
        inv = lax.rsqrt(mean(centered * centered) + epsilon)
        normed = centered * inv
        k.out_stage[here, :] = (normed * vector(5) + vector(6)).astype(bf16)
        start = pl.multiple_of(own0 + i * small, small)
        grad = jnp.where(segment(start, small) < 2, k.cot_in[here, :].astype(f32), 0.0)
        scaled = grad * vector(5)
        second = inv * (scaled - mean(scaled) - normed * mean(scaled * normed))
        own_sum[here, :] = second
        k.base[pl.ds(start, small), :] = second.astype(bf16)
        acc[0] += fold(grad * normed)
        acc[1] += fold(grad)
        acc[2] += fold(second)

    send_out = pltpu.make_async_copy(k.out_stage, k.out, k.local.at[2])
    send_out.start()
    swap_d = swap(3, k.base.at[own, :], k.base.at[own, :])
    swap_d.start()
    acc_up = k.acc_up
    acc_up[...] = jnp.zeros_like(acc_up)

    def fall(start):
        rows = pl.ds(start, half)

        @pl.loop(0, blocks)
        def _(i):
            cols = pl.ds(pl.multiple_of(i * chunk, chunk), chunk)
            grad = mul(k.base[rows, :], k.full3[:, cols]) * k.slope[rows, cols].astype(f32)
            k.slope[rows, cols] = grad.astype(bf16)
            acc_up[:, cols] += fold(grad)

    descend = Descend(
        place, k.grad0, k.total0, high_half, k.deep, k.deep_far, k.deep_near, k.r_send, k.r_recv, 0
    )
    sum_down, sum_up, sum_out, *sum_pairs = [
        Reduce(
            place, many(k, "grad", g), many(k, "total", g), part,
            many(k, "near", g), many(k, "ring", g), many(k, "high", g), k.r_send, k.r_recv, 1 + g,
        )
        for g, part in enumerate(
            [low_half, slice(0, hidden_width), slice(0, pairs * PAIR)] + [slice(0, 3 * PAIR)] * pairs
        )
    ]

    def weight_grad(dest, left_t, right, source_col, dest_col, count, step):
        @pl.loop(0, count // step)
        def _(i):
            to = pl.ds(pl.multiple_of(dest_col + i * step, 128), step)
            source = pl.ds(pl.multiple_of(source_col + i * step, 128), step)
            dest[:, to] = mul(left_t[...], right[:, source]).astype(bf16)

    fall(own0)
    swap_c.wait_send()
    swap_d.wait_recv()
    transpose(k.base, k.grad_t)
    middle = hidden_width // 2
    weight_grad(k.grad0, k.grad_t, k.act, middle, middle, middle, 256)
    descend.begin()
    weight_grad(k.grad0, k.grad_t, k.act, 0, 0, middle, 256)
    sum_down.begin()
    fall(far0)

    @pl.loop(0, half // block)
    def _(i):
        rows = pl.ds(pl.multiple_of(far0 + i * block, block), block)
        k.half_send[pl.ds(pl.multiple_of(i * block, block), block), :] = mul_t(
            k.slope[rows, :], k.full2[...]
        ).astype(bf16)

    swap_e = swap(4, k.half_send, k.half_recv)
    swap_e.start()

    @pl.loop(0, half // block)
    def _(i):
        here = pl.ds(pl.multiple_of(i * block, block), block)
        rows = pl.ds(pl.multiple_of(own0 + i * block, block), block)
        own_sum[here, :] += mul_t(k.slope[rows, :], k.full2[...])

    swap_e.wait_recv()

    @pl.loop(0, half // small)
    def _(i):
        here = pl.ds(pl.multiple_of(i * small, small), small)
        grad = own_sum[here, :] + k.half_recv[here, :].astype(f32)
        normed = normed_one[here, :]
        scaled = grad * vector(2)
        r1 = inv_one[here, 0:1] * (scaled - mean(scaled) - normed * mean(scaled * normed))
        k.first[pl.ds(pl.multiple_of(own0 + i * small, small), small), :] = r1.astype(bf16)
        acc[3] += fold(grad * normed)
        acc[4] += fold(grad)
        acc[5] += fold(r1)

    swap_f = swap(5, k.first.at[own, :], k.first.at[own, :])
    swap_f.start()
    sum_down.join()
    weight_grad(k.grad1, k.first_t, k.slope, 0, 0, hidden_width, 512)
    sum_up.begin()
    descend.pass_in()
    swap_f.wait_recv()

    @pl.loop(0, total_rows // 512)
    def _(i):
        rows = pl.ds(pl.multiple_of(i * 512, 512), 512)
        k.grad_mixed[rows, :] = mul(k.first[rows, :], k.full1[...]).astype(bf16)

    transpose(k.first, k.grad_t)
    weight_grad(k.grad2, k.grad_t, k.mixed, 0, 0, pairs * PAIR, pairs * PAIR)
    sum_out.begin()

    grad_qkv = k.grad_qkv
    acc_qkv = k.acc_qkv

    def attend_back(j, midway):
        mixed_cut = slice(j * PAIR, (j + 1) * PAIR)
        for h in (0, 1):
            k.keys[h] = with_mask(qkv[:, cut_of(j, 0)], k.mask_q[...], h)
        product = k.grad_mixed[:, mixed_cut].astype(f32) * k.mixed[:, mixed_cut].astype(f32)
        flipped = product.T
        k.inner[0:1, :] = jnp.sum(flipped[:HD], axis=0, keepdims=True)
        k.inner[1:2, :] = jnp.sum(flipped[HD:], axis=0, keepdims=True)
        k.keys_t[...] = qkv[:, cut_of(j, 1)].T
        k.query_t[...] = jnp.zeros_like(k.query_t)

        steps = total_rows // rows_at_once

        def one_block(i):
            start = pl.multiple_of(i * rows_at_once, rows_at_once)
            rows = pl.ds(start, rows_at_once)
            grads_v, grads_k, query_t = [], [], []
            for h in (0, 1):
                key = with_mask(qkv[rows, cut_of(j, 1)], k.mask_k[rows, :], h)
                prob = jnp.exp(mul_t(key, k.keys[h]) - k.lse_t[j, h : h + 1, :])
                value = jnp.where(in_head(h), qkv[rows, cut_of(j, 2)].astype(f32), 0.0).astype(bf16)
                grad_prob = mul_t(value, k.grad_mixed[:, mixed_cut])
                grad_score = (prob * (grad_prob - k.inner[h : h + 1, :])).astype(bf16)
                grads_v.append(mul(prob.astype(bf16), k.grad_mixed[:, mixed_cut]))
                grads_k.append(mul(grad_score, qkv[:, cut_of(j, 0)]))
                query_t.append(mul(k.keys_t[h * HD : (h + 1) * HD, rows], grad_score))
            grad_k = jnp.where(lower, grads_k[0], grads_k[1]).astype(bf16)
            grad_v = jnp.where(lower, grads_v[0], grads_v[1]).astype(bf16)
            grad_qkv[rows, cut_of(j, 1)] = grad_k
            grad_qkv[rows, cut_of(j, 2)] = grad_v
            k.query_t[...] += jnp.concatenate(query_t, axis=0)

        pl.loop(0, steps // 2)(one_block)
        midway()
        pl.loop(steps // 2, steps)(one_block)
        grad_qkv[:, cut_of(j, 0)] = (k.query_t[...].T * HD**-0.5).astype(bf16)
        cols = slice(3 * j * PAIR, 3 * (j + 1) * PAIR)
        acc_qkv[:, cols] = fold(grad_qkv[:, cols].astype(f32))
        weight_grad(many(k, "grad", 3 + j), k.base_t, grad_qkv, 3 * j * PAIR, 0, 3 * PAIR, 3 * PAIR)
        sum_pairs[j].begin()

    attend_back(0, sum_down.cross)
    sum_up.join()
    descend.pass_out()
    attend_back(1, sum_out.join)
    descend.arrive()
    sum_up.cross()
    for j in range(2, pairs):
        attend_back(j, sum_pairs[j - 2].join)
    descend.join()
    sum_out.cross()

    in_send, in_recv = k.act.at[:, :width], k.act.at[:, width : 2 * width]

    @pl.loop(0, total_rows // block)
    def _(i):
        rows = pl.ds(pl.multiple_of(i * block, block), block)
        in_send[rows, :] = mul_t(grad_qkv[rows, :], k.full0[...]).astype(bf16)

    swap_g = swap(6, in_send, in_recv)
    swap_g.start()
    for j in range(pairs - 2, pairs - 1):
        sum_pairs[j].join()
    sum_down.finish()
    sum_pairs[0].cross()
    swap_g.wait_recv()
    ge = k.acc_ge
    ge[...] = jnp.zeros_like(ge)

    def settle(stage, base):
        @pl.loop(0, half // small)
        def _(i):
            start = pl.multiple_of(base + i * small, small)
            rows = pl.ds(start, small)
            grad = (in_send[rows, :].astype(f32) + in_recv[rows, :].astype(f32)) + k.first[
                rows, :
            ].astype(f32)
            stage[pl.ds(pl.multiple_of(i * small, small), small), :] = grad
            seg = segment(start, small)
            ge[0] += fold(jnp.where(seg == 0, grad, 0.0))
            ge[1] += fold(jnp.where(seg == 1, grad, 0.0))

    send_in = []
    for n, stage in enumerate((first_own, normed_one)):
        settle(stage, n * half)
        send_in.append(
            pltpu.make_async_copy(stage, k.grad_in.at[pl.ds(n * half, half), :], k.local.at[3 + n])
        )
        send_in[n].start()

    def row_of(x):
        return jnp.sum(x, axis=0, keepdims=True)

    sums = k.part.at[0]
    sums[...] = jnp.zeros_like(sums)
    for row, n in enumerate((5, 3, 4, 2, 0, 1)):
        sums[row : row + 1, :] = row_of(acc[n])
    up_row = row_of(acc_up[...])
    for n in range(hidden_width // width):
        sums[8 + n : 9 + n, :] = up_row[:, n * width : (n + 1) * width]
    qkv_row = row_of(acc_qkv[...])
    at = 8 + hidden_width // width
    sums[at : at + 1, :] = qkv_row[:, :width]
    sums[at + 1 : at + 2, : qkv_row.shape[1] - width] = qkv_row[:, width:]
    sums[16:, :] = jnp.where(
        seq_row == at_row, row_of(ge[0]), jnp.where(seq_row == at_row + 1, row_of(ge[1]), 0.0)
    )
    pair_sums = Spread(place, "tp", [sums], k.part_tp, small_send, small_recv, 13)
    pair_sums.start()
    sum_pairs[pairs - 1].join()
    pair_sums.wait()
    row = lax.broadcasted_iota(jnp.int32, sums.shape, 0)
    k.part_sum[...] = sums[...] + jnp.where(row < 8, k.part_tp[...], 0.0)
    sums_z = Spread(place, "z", [k.part_sum] * 3, k.part_z, small_send, small_recv, 14)
    sums_z.start()
    for j in range(1, pairs - 1):
        sum_pairs[j].cross()
    sums_z.wait()
    k.part_zsum[...] = k.part_sum[...] + k.part_z[0] + k.part_z[1] + k.part_z[2]
    sums_r = Spread(place, "r", [k.part_zsum] * 3, k.part_in, small_send, small_recv, 17)
    sums_r.start()
    descend.finish()
    sum_up.finish()
    sum_out.finish()
    sums_r.wait()
    k.all_sums[...] = (
        k.part_zsum[:16] + k.part_in[0, :16] + k.part_in[1, :16] + k.part_in[2, :16]
    )
    k.all_embed[0] = k.part_zsum[16:]
    for d in (1, 2, 3):
        k.all_embed[d] = k.part_in[d - 1, 16:]
    sum_pairs[pairs - 1].cross()
    for one in sum_pairs:
        one.finish()
    for one in (
        gather_a, gather_b, gather_c, gather_d, climb, descend, sum_down, sum_up, sum_out,
        *sum_pairs, pair_sums, sums_z, sums_r,
    ):
        one.drain()
    send_out.wait()
    for copy in send_in:
        copy.wait()
    for copy in (swap_d, swap_e, swap_f, swap_g):
        copy.wait_send()


def call_layer(sub, operands):
    rows, width = operands["x"].shape
    half = rows // 2
    mine, heads = operands["wo"].shape
    hidden = operands["bu"].shape[0]
    pairs = heads // PAIR
    seqs = 8 * sub
    count = operands["v0"].shape[1]
    tall = seqs + 16
    columns = [hidden, hidden, heads] + [3 * PAIR] * pairs
    shape = jax.ShapeDtypeStruct
    results = dict(
        out=shape((half, width), bf16),
        grad_in=shape((rows, width), f32),
        all_feats=shape((4, seqs, TE), f32),
        all_sums=shape((16, width), f32),
        all_embed=shape((4, seqs, width), f32),
    )
    for g, wide in enumerate(columns):
        results["total" + str(g)] = shape((mine, wide), f32)
    vm = pltpu.VMEM
    sem = pltpu.SemaphoreType.DMA
    scratch = dict(
        rows_in=vm((rows, width), bf16),
        cot_in=vm((half, width), bf16),
        out_stage=vm((half, width), bf16),
        w0=vm((mine, 3 * heads), bf16),
        w1=vm((mine, heads), bf16),
        w2=vm((mine, hidden), bf16),
        w3=vm((mine, hidden), bf16),
        bqkv=vm((1, 3 * heads), f32),
        bup=vm((1, hidden), f32),
        feats=vm((seqs, TE), f32),
        given=vm((8, count), f32),
        deep=vm((5, 4 * mine, hidden // 2), bf16),
        deep_far=vm((mine, hidden // 2), bf16),
        deep_near=vm((2, mine, hidden // 2), bf16),
        local=sem((5,)),
        full0=vm((width, 3 * heads), bf16),
        full1=vm((width, heads), bf16),
        full2=vm((width, hidden), bf16),
        full3=vm((width, hidden), bf16),
        feat_z=vm((3, seqs, TE), f32),
        feat_sum=vm((seqs, TE), f32),
        feat_in=vm((3, seqs, TE), f32),
        part=vm((4, tall, width), f32),
        part_in=vm((3, tall, width), f32),
        part_sum=vm((tall, width), f32),
        part_z=vm((3, tall, width), f32),
        part_zsum=vm((tall, width), f32),
        part_tp=vm((tall, width), f32),
        shared=vm((8, width), f32),
        embed=vm((8, width), f32),
        base=vm((rows, width), bf16),
        base_t=vm((width, rows), bf16),
        mask_q=vm((rows, PAIR), bf16),
        mask_k=vm((rows, PAIR), bf16),
        keys=vm((2, rows, PAIR), bf16),
        qkv=vm((rows, 3 * heads), bf16),
        mixed=vm((rows, heads), bf16),
        lse=vm((rows, PAIR), f32),
        lse_t=vm((pairs, 8, rows), f32),
        half_send=vm((half, width), bf16),
        half_recv=vm((half, width), bf16),
        first_own=vm((half, width), f32),
        normed_one=vm((half, width), f32),
        inv_one=vm((half, 128), f32),
        first=vm((rows, width), bf16),
        first_t=vm((width, rows), bf16),
        act=vm((rows, hidden), bf16),
        slope=vm((rows, hidden), bf16),
        acc=vm((6, 8, width), f32),
        acc_up=vm((8, hidden), f32),
        acc_qkv=vm((8, 3 * heads), f32),
        acc_ge=vm((2, 8, width), f32),
        grad_t=vm((width, rows), bf16),
        grad_mixed=vm((rows, heads), bf16),
        inner=vm((8, rows), f32),
        keys_t=vm((PAIR, rows), bf16),
        query_t=vm((PAIR, rows), f32),
        grad_qkv=vm((rows, 3 * heads), bf16),
        g_send=sem((5, 15)),
        g_recv=sem((5, 15)),
        r_send=sem((4 + pairs, 15)),
        r_recv=sem((4 + pairs, 15)),
        small_send=sem((20,)),
        small_recv=sem((20,)),
        tp_send=sem((7,)),
        tp_recv=sem((7,)),
    )
    for g, wide in enumerate(columns):
        scratch["grad" + str(g)] = vm((width, wide), bf16)
        part = wide // 2 if g == 0 else wide
        scratch["near" + str(g)] = vm((4, mine, part), bf16)
        scratch["ring" + str(g)] = vm((8, mine, part), bf16)
        scratch["high" + str(g)] = vm((3, mine, part), bf16)
    names = [*operands, *results, *scratch]
    spaces = dict(lengths=pltpu.SMEM, steps=pltpu.SMEM, x=pl.ANY, cot=pl.ANY, out=pl.ANY, grad_in=pl.ANY)
    spec = lambda n: pl.BlockSpec(memory_space=spaces.get(n, pltpu.VMEM))
    got = pl.pallas_call(
        functools.partial(layer_kernel, sub, names),
        out_shape=list(results.values()),
        in_specs=[spec(n) for n in operands],
        out_specs=[spec(n) for n in results],
        scratch_shapes=list(scratch.values()),
        compiler_params=pltpu.CompilerParams(
            collective_id=0, has_side_effects=True, vmem_limit_bytes=63_000 * 1024
        ),
        name="layer",
    )(*operands.values())
    return types.SimpleNamespace(**dict(zip(results, got, strict=True)))


def finish_kernel(dp_size, names, *refs):
    k = types.SimpleNamespace(**dict(zip(names, refs, strict=True)))
    rows = k.grad_from.shape[0] // 4
    moves = [(k.out_from, k.out_held, k.out)]
    for n in range(4):
        here = slice(n * rows, (n + 1) * rows)
        moves.append((k.grad_from.at[here], k.grad_held.at[here], k.grad_in.at[here]))
    fetch = [pltpu.make_async_copy(a, b, k.local.at[n]) for n, (a, b, _) in enumerate(moves)]
    store = [pltpu.make_async_copy(b, c, k.local.at[5 + n]) for n, (_, b, c) in enumerate(moves)]
    for copy in fetch:
        copy.start()
    feats, embeds = k.feats[...], k.embeds[...]
    before = mul_t(feats.astype(bf16), k.tw1t[...].astype(bf16)) + k.tb1[...]
    gate = jax.nn.sigmoid(before)
    hidden = (before * gate).astype(bf16).astype(f32)
    grad_hidden = exact(embeds, k.tw2[...].astype(bf16).astype(f32), 1, 1)
    for first, then in zip(fetch, store, strict=True):
        first.wait()
        then.start()
    grad_before = grad_hidden * (gate * (1.0 + before * (1.0 - gate)))
    k.g_tw2[...] = exact(hidden, embeds, 0, 0)
    k.g_tw1t[...] = exact(grad_before, feats, 0, 0)
    k.g_tb1[...] = jnp.sum(grad_before, axis=0, keepdims=True)
    sums = k.sums[...]
    width = sums.shape[1]
    row = lax.broadcasted_iota(jnp.int32, (8, 1), 0)
    vectors = jnp.where(row == 6, jnp.sum(embeds, axis=0, keepdims=True), sums[:8])
    count = k.tb1.shape[1]
    start = (lax.axis_index("dp") * lax.axis_size("tp") + lax.axis_index("tp")) * count
    entry = lax.broadcasted_iota(jnp.int32, (count, width), 0)
    column = lax.broadcasted_iota(jnp.int32, (count, width), 1)
    picked = exact(vectors, jnp.where(column == start + entry, 1.0, 0.0), 1, 1)
    for n, dest in enumerate((k.g_bout, k.g_g1, k.g_s1, k.g_bdown, k.g_g2, k.g_s2, k.g_tb2)):
        dest[...] = picked[n : n + 1, :]
    hidden_width = k.g_bup.shape[0]
    for n in range(hidden_width // width):
        k.g_bup[n * width : (n + 1) * width] = sums[8 + n, :]
    at = 8 + hidden_width // width
    pairs = k.g_bq.shape[0] // PAIR
    for j in range(pairs):
        here = slice(j * PAIR, (j + 1) * PAIR)
        source = many(k, "pair", j)
        for n, dest in enumerate((k.g_wq, k.g_wk, k.g_wv)):
            dest[:, here] = source[:, n * PAIR : (n + 1) * PAIR]
        for n, dest in ((0, k.g_bq), (2, k.g_bv)):
            first = (3 * j + n) * PAIR
            dest[here] = sums[at + first // width, first % width : first % width + PAIR]
    k.g_wo[...] = k.sum_out[...]
    k.g_wu[...] = k.sum_up[...]
    k.g_wd[...] = k.sum_down[...]
    for copy in store:
        copy.wait()


def call_finish(dp_size, operands, hidden):
    shape = jax.ShapeDtypeStruct
    own = operands["tb1"].shape[1]
    width = operands["sums"].shape[1]
    mine, heads = operands["sum_out"].shape
    line = shape((1, own), f32)
    matrix = shape((mine, heads), f32)
    wide = shape((mine, hidden), f32)
    results = dict(
        out=shape(operands["out_from"].shape, bf16),
        grad_in=shape(operands["grad_from"].shape, f32),
        g_tw1t=shape((own, TE), f32),
        g_tb1=line,
        g_tw2=shape((own, width), f32),
        g_tb2=line,
        g_wq=matrix,
        g_bq=shape((heads,), f32),
        g_wk=matrix,
        g_wv=matrix,
        g_bv=shape((heads,), f32),
        g_wo=matrix,
        g_bout=line,
        g_g1=line,
        g_s1=line,
        g_wu=wide,
        g_bup=shape((hidden,), f32),
        g_wd=wide,
        g_bdown=line,
        g_g2=line,
        g_s2=line,
    )
    scratch = dict(
        out_held=pltpu.VMEM(operands["out_from"].shape, bf16),
        grad_held=pltpu.VMEM(operands["grad_from"].shape, f32),
        local=pltpu.SemaphoreType.DMA((10,)),
    )
    names = [*operands, *results, *scratch]
    spaces = dict(out_from=pl.ANY, grad_from=pl.ANY, out=pl.ANY, grad_in=pl.ANY)
    spec = lambda n: pl.BlockSpec(memory_space=spaces.get(n, pltpu.VMEM))
    got = pl.pallas_call(
        functools.partial(finish_kernel, dp_size, names),
        out_shape=list(results.values()),
        in_specs=[spec(n) for n in operands],
        out_specs=[spec(n) for n in results],
        scratch_shapes=list(scratch.values()),
        compiler_params=pltpu.CompilerParams(vmem_limit_bytes=61_000 * 1024),
        name="finish",
    )(*operands.values())
    return types.SimpleNamespace(**dict(zip(results, got, strict=True)))


def on_device(
    inputs, cotangent, seq_lengths, timesteps, time_w1, time_b1, time_w2, time_b2,
    w_query, b_query, w_key, w_value, b_value, w_out, b_out, norm1_gain, norm1_bias,
    w_up, b_up, w_down, b_down, norm2_gain, norm2_bias,
):
    dp = lax.axis_size("dp")
    sub = dp // SUPER
    low = [[q * sub + l for l in range(sub)] for q in range(SUPER)]
    head_width = w_query.shape[1]

    def near(value, axis=0):
        if sub == 1:
            return value
        return lax.all_gather(value, "dp", axis=axis, tiled=True, axis_index_groups=low)

    def line(value):
        return near(value)[None, :]

    steps = timesteps
    if sub > 1:
        steps = near(timesteps.astype(f32)).astype(jnp.int32).reshape(1, -1)
    got = call_layer(
        sub,
        dict(
            lengths=seq_lengths,
            steps=steps,
            x=inputs,
            cot=cotangent,
            wq=near(w_query),
            wk=near(w_key),
            wv=near(w_value),
            wo=near(w_out.T),
            wu=near(w_up),
            wd=near(w_down.T),
            bq=b_query,
            bv=b_value,
            bu=b_up,
            tw1t=near(time_w1.T),
            tb1=line(time_b1),
            tw2=near(time_w2),
            v0=line(time_b2),
            v1=line(b_out),
            v2=line(norm1_gain),
            v3=line(norm1_bias),
            v4=line(b_down),
            v5=line(norm2_gain),
            v6=line(norm2_bias),
        ),
    )
    sums, embeds, feats = got.all_sums, got.all_embed, got.all_feats
    pairs = head_width // PAIR
    totals = [many(got, "total", g) for g in range(3 + pairs)]
    if sub > 1:
        sums, embeds = lax.psum((sums, embeds), "dp", axis_index_groups=low)
        totals = [
            lax.psum_scatter(one, "dp", scatter_dimension=0, tiled=True, axis_index_groups=low)
            for one in totals
        ]
    operands = dict(
        out_from=got.out,
        grad_from=got.grad_in,
        sums=sums,
        embeds=embeds.reshape(-1, embeds.shape[-1]),
        feats=feats.reshape(-1, TE),
        tw1t=time_w1.T,
        tb1=time_b1[None, :],
        tw2=time_w2,
        sum_down=totals[0],
        sum_up=totals[1],
        sum_out=totals[2],
    )
    for j in range(pairs):
        operands["pair" + str(j)] = totals[3 + j]
    done = call_finish(dp, operands, b_up.shape[0])
    return (
        done.out,
        done.grad_in,
        done.g_tw1t.T,
        done.g_tb1[0],
        done.g_tw2,
        done.g_tb2[0],
        done.g_wq,
        done.g_bq,
        done.g_wk,
        done.g_wv,
        done.g_bv,
        done.g_wo.T,
        done.g_bout[0],
        done.g_g1[0],
        done.g_s1[0],
        done.g_wu,
        done.g_bup,
        done.g_wd.T,
        done.g_bdown[0],
        done.g_g2[0],
        done.g_s2[0],
    )


def solution(mesh):
    placed = (
        P("dp", None),
        P(("dp", "tp"), None),
        P("dp", None),
        P("dp", None),
        P(None, ("dp", "tp")),
        P(("dp", "tp")),
        P(("dp", "tp"), None),
        P(("dp", "tp")),
        P("dp", "tp"),
        P("tp"),
        P("dp", "tp"),
        P("dp", "tp"),
        P("tp"),
        P("tp", "dp"),
        P(("dp", "tp")),
        P(("dp", "tp")),
        P(("dp", "tp")),
        P("dp", "tp"),
        P("tp"),
        P("tp", "dp"),
        P(("dp", "tp")),
        P(("dp", "tp")),
        P(("dp", "tp")),
    )
    return jax.shard_map(
        on_device,
        mesh=mesh,
        in_specs=placed,
        out_specs=(
            P(("dp", "tp"), None),
            P("dp", None),
            P(None, ("dp", "tp")),
            P(("dp", "tp")),
            P(("dp", "tp"), None),
            P(("dp", "tp")),
            P("dp", "tp"),
            P("tp"),
            P("dp", "tp"),
            P("dp", "tp"),
            P("tp"),
            P("tp", "dp"),
            P(("dp", "tp")),
            P(("dp", "tp")),
            P(("dp", "tp")),
            P("dp", "tp"),
            P("tp"),
            P("tp", "dp"),
            P(("dp", "tp")),
            P(("dp", "tp")),
            P(("dp", "tp")),
        ),
        check_vma=False,
    )
```

```python
import functools
import math
import types

import jax
import jax.numpy as jnp
from jax import lax
from jax.experimental import pallas as pl
from jax.experimental.pallas import tpu as pltpu
from jax.sharding import PartitionSpec as P

HD = 64
TE = 128
SUPER = 16

epsilon = 1e-05
highest = lax.Precision.HIGHEST
f32 = jnp.float32
bf16 = jnp.bfloat16


class Place:
    def __init__(self, sub):
        self.sub = sub
        index = lax.axis_index("dp")
        self.low = lax.rem(index, sub)
        self.place = lax.div(index, sub)
        self.z = lax.div(self.place, 4)
        self.p = lax.rem(self.place, 4)
        self.r = self.ring(self.p)

    @staticmethod
    def ring(v):
        half = lax.div(v, 2)
        return 2 * half + lax.rem(lax.rem(v, 2) + half, 2)

    def plane(self, m):
        z = self.z
        if m == 0:
            return z
        if m == 1:
            return jnp.where(z == 0, 1, z - 1)
        if m == 2:
            return jnp.where(z == 3, 1, jnp.where(z == 2, 3, 2))
        return jnp.where(z < 2, 3, 0)

    def spot(self, plane, dr):
        return plane * 4 + self.ring(lax.rem(self.r + dr + 4, 4))

    def device(self, plane, dr):
        return {"dp": self.spot(plane, dr) * self.sub + self.low}

    def rows(self, plane, dr, count):
        return pl.ds(pl.multiple_of(self.spot(plane, dr) * count, 16), count)

    def slab(self, plane, count):
        return pl.ds(pl.multiple_of(plane * 4 * count, 16), 4 * count)

    def other(self):
        return {"tp": 1 - lax.axis_index("tp")}

    def rows(self, dz, dr, count):
        return pl.ds(pl.multiple_of(self.spot(dz, dr) * count, 16), count)

    def enter(self):
        barrier = pltpu.get_barrier_semaphore()
        for peer in (
            [self.device(self.plane(m), 0) for m in (1, 2, 3)]
            + [self.device(self.z, d) for d in (1, 2, 3)]
            + [self.other()]
        ):
            pl.semaphore_signal(barrier, inc=1, device_id=peer, device_id_type=pl.DeviceIdType.MESH)
        pl.semaphore_wait(barrier, 7)


def remote(src, dst, send, recv, device):
    return pltpu.make_async_remote_copy(
        src_ref=src,
        dst_ref=dst,
        send_sem=send,
        recv_sem=recv,
        device_id=device,
        device_id_type=pl.DeviceIdType.MESH,
    )


def many(k, name, g):
    return getattr(k, name + str(g))


class Gather:
    def __init__(self, place, shard, full, cols, send, recv, g):
        count = shard.shape[0]
        at = lambda plane, dr: full.at[place.rows(plane, dr, count), cols]
        self.place, self.shard, self.full, self.count, self.cols = place, shard, full, count, cols
        z = place.z
        shard = shard.at[:, cols]
        self.over, self.heard, self.around, self.relay = [], [], [], []
        for m in range(4):
            plane = place.plane(m)
            if m:
                self.over.append(
                    remote(shard, at(z, 0), send.at[g, m - 1], recv.at[g, z], place.device(plane, 0))
                )
                self.heard.append(
                    remote(shard, at(plane, 0), send.at[g, m - 1], recv.at[g, plane], place.device(plane, 0))
                )
            source = at(plane, 0) if m else shard
            self.around.append(
                [
                    remote(
                        source,
                        at(plane, 0),
                        send.at[g, 4 + 2 * m + n],
                        recv.at[g, 4 + 2 * m + n],
                        place.device(z, 1 - 2 * n),
                    )
                    for n in (0, 1)
                ]
            )
            n = m // 2
            self.relay.append(
                remote(
                    at(plane, 2 * n - 1),
                    at(plane, 2 * n - 1),
                    send.at[g, 12 + m],
                    recv.at[g, 12 + m],
                    place.device(z, 1 - 2 * n),
                )
            )

    def begin(self):
        for copy in self.over:
            copy.start()
        self.full[self.place.rows(self.place.z, 0, self.count), self.cols] = self.shard[:, self.cols]

    def own(self):
        for copy in self.around[0]:
            copy.start()

    def turn(self, m):
        self.heard[m - 1].wait_recv()
        for copy in self.around[m]:
            copy.start()

    def pass_on(self, m):
        self.around[m][m // 2].wait_recv()
        self.relay[m].start()

    def finish(self):
        for m in range(4):
            self.around[m][1 - m // 2].wait_recv()
            self.relay[m].wait_recv()

    def drain(self):
        for copy in self.over + [c for pair in self.around for c in pair] + self.relay:
            copy.wait_send()


def halves(cols):
    middle = (cols.start + cols.stop) // 2
    return slice(cols.start, middle), slice(middle, cols.stop)


class Climb:
    def __init__(self, place, shard, full, cols, send, recv, g):
        count = shard.shape[0]
        self.place, self.shard, self.full, self.count, self.cols = place, shard, full, count, cols
        z = place.z
        at = lambda dr, part: full.at[place.rows(z, dr, count), part]
        slab = lambda plane: full.at[place.slab(plane, count), cols]
        self.around = [
            remote(shard.at[:, cols], at(0, cols), send.at[g, n], recv.at[g, n], place.device(z, 1 - 2 * n))
            for n in (0, 1)
        ]
        self.relay = [
            remote(
                at(2 * n - 1, part), at(2 * n - 1, part), send.at[g, 2 + n], recv.at[g, 2 + n],
                place.device(z, 1 - 2 * n),
            )
            for n, part in enumerate(halves(cols))
        ]
        self.over, self.heard = [], []
        for m in (1, 2, 3):
            plane = place.plane(m)
            self.over.append(
                remote(slab(z), slab(z), send.at[g, 3 + m], recv.at[g, 4 + z], place.device(plane, 0))
            )
            self.heard.append(
                remote(slab(plane), slab(plane), send.at[g, 3 + m], recv.at[g, 4 + plane], place.device(plane, 0))
            )

    def begin(self):
        for copy in self.around:
            copy.start()
        self.full[self.place.rows(self.place.z, 0, self.count), self.cols] = self.shard[:, self.cols]

    def pass_on(self):
        for n in (0, 1):
            self.around[n].wait_recv()
            self.relay[n].start()

    def rise(self):
        for n in (0, 1):
            self.relay[n].wait_recv()
        for copy in self.over:
            copy.start()

    def finish(self):
        for copy in self.heard:
            copy.wait_recv()

    def drain(self):
        for copy in self.around + self.relay + self.over:
            copy.wait_send()


class Reduce:
    def __init__(self, place, grads, total, cols, first, second, third, send, recv, g):
        count = total.shape[0]
        at = lambda plane, dr: grads.at[place.rows(plane, dr, count), cols]
        self.place, self.grads, self.total, self.count, self.cols = place, grads, total, count, cols
        self.first, self.second, self.third = first, second, third
        self.far_copies, self.near, self.up, self.heard = [], [], [], []
        z = place.z
        for m in range(4):
            n = m // 2
            plane = place.plane(m)
            self.far_copies.append(
                remote(at(plane, 2), first.at[m], send.at[g, m], recv.at[g, m], place.device(z, 1 - 2 * n))
            )
            self.near.append(
                [
                    remote(
                        at(plane, 1 - 2 * j),
                        second.at[j * 4 + m],
                        send.at[g, 4 + 2 * m + j],
                        recv.at[g, 4 + 2 * m + j],
                        place.device(z, 1 - 2 * j),
                    )
                    for j in (0, 1)
                ]
            )
            if m:
                self.up.append(
                    remote(at(plane, 0), third.at[z], send.at[g, 11 + m], recv.at[g, 12 + z], place.device(plane, 0))
                )
                self.heard.append(
                    remote(at(plane, 0), third.at[plane], send.at[g, 11 + m], recv.at[g, 12 + plane], place.device(plane, 0))
                )

    def far(self):
        for copy in self.far_copies:
            copy.start()

    def raw(self):
        for m in range(4):
            self.near[m][1 - m // 2].start()

    def join(self):
        for m in range(4):
            n = m // 2
            self.far_copies[m].wait_recv()
            here = self.place.rows(self.place.plane(m), 1 - 2 * n, self.count), self.cols
            self.grads[here] = (self.grads[here].astype(f32) + self.first[m].astype(f32)).astype(bf16)
            self.near[m][n].start()

    def cross(self):
        for m in (1, 2, 3, 0):
            for j in (0, 1):
                self.near[m][j].wait_recv()
            here = self.place.rows(self.place.plane(m), 0, self.count), self.cols
            summed = (
                self.grads[here].astype(f32)
                + self.second[m].astype(f32)
                + self.second[4 + m].astype(f32)
            )
            if m:
                self.grads[here] = summed.astype(bf16)
                self.up[m - 1].start()
            else:
                self.total[:, self.cols] = summed

    def finish(self):
        for copy in self.heard:
            copy.wait_recv()
        held = [self.third[self.place.plane(m)].astype(f32) for m in (1, 2, 3)]
        self.total[:, self.cols] += held[0] + held[1] + held[2]

    def drain(self):
        for copy in self.far_copies + [c for pair in self.near for c in pair] + self.up:
            copy.wait_send()


class Descend:
    def __init__(self, place, grads, total, cols, deep, far, near, send, recv, g):
        count = total.shape[0]
        self.place, self.grads, self.total, self.count, self.cols = place, grads, total, count, cols
        self.deep, self.far, self.near = deep, far, near
        z = place.z
        part = halves(cols)
        self.here = lambda dr, n: (place.rows(z, dr, count), part[n])
        self.slot = [slice(p.start - cols.start, p.stop - cols.start) for p in part]

        def copy(source, dest, n, m, to):
            return remote(grads.at[source], dest, send.at[g, n], recv.at[g, m], to)

        self.over, self.heard = [], []
        for m in (1, 2, 3):
            plane = place.plane(m)
            source = place.slab(plane, count), cols
            self.over.append(copy(source, deep.at[z], m - 1, z, place.device(plane, 0)))
            self.heard.append(copy(source, deep.at[plane], m - 1, plane, place.device(plane, 0)))
        side = [place.device(z, 1), place.device(z, -1)]
        self.away = [
            copy(self.here(2, n), far.at[:, self.slot[n]], 4 + n, 4 + n, side[n]) for n in (0, 1)
        ]
        self.plain = [
            copy(self.here(1 - 2 * n, 1 - n), near.at[n, :, self.slot[1 - n]], 6 + n, 6 + n, side[n])
            for n in (0, 1)
        ]
        self.joined = [
            copy(self.here(1 - 2 * n, n), near.at[n, :, self.slot[n]], 8 + n, 8 + n, side[n])
            for n in (0, 1)
        ]

    def begin(self):
        for copy in self.over:
            copy.start()

    def arrive(self):
        here = self.place.slab(self.place.z, self.count), self.cols
        total = self.grads[here].astype(f32)
        for m in (1, 2, 3):
            self.heard[m - 1].wait_recv()
            total += self.deep[self.place.plane(m)].astype(f32)
        self.grads[here] = total.astype(bf16)
        for copy in self.away + self.plain:
            copy.start()

    def join(self):
        for n in (0, 1):
            self.away[n].wait_recv()
            here = self.here(1 - 2 * n, n)
            self.grads[here] = (
                self.grads[here].astype(f32) + self.far[:, self.slot[n]].astype(f32)
            ).astype(bf16)
            self.joined[n].start()

    def finish(self):
        for copy in self.plain + self.joined:
            copy.wait_recv()
        own = self.place.rows(self.place.z, 0, self.count), self.cols
        self.total[:, self.cols] = (
            self.grads[own].astype(f32) + self.near[0].astype(f32) + self.near[1].astype(f32)
        )

    def drain(self):
        for copy in self.over + self.away + self.plain + self.joined:
            copy.wait_send()


class Spread:
    def __init__(self, place, along, sources, slots, send, recv, base):
        rows = slice(0, sources[0].shape[0])
        if along == "tp":
            self.copies = [
                remote(sources[0], slots.at[rows], send.at[base], recv.at[base], place.other())
            ]
            return
        self.copies = [
            remote(
                sources[d - 1],
                slots.at[d - 1, rows],
                send.at[base + d - 1],
                recv.at[base + d - 1],
                place.device(lax.rem(place.z + d, 4), 0) if along == "z" else place.device(place.z, d),
            )
            for d in (1, 2, 3)
        ]

    def start(self):
        for copy in self.copies:
            copy.start()

    def wait(self):
        for copy in self.copies:
            copy.wait_recv()

    def drain(self):
        for copy in self.copies:
            copy.wait_send()


def mul(a, b):
    return lax.dot_general(a, b, (((1,), (0,)), ((), ())), preferred_element_type=f32)


def mul_t(a, b):
    return lax.dot_general(a, b, (((1,), (1,)), ((), ())), preferred_element_type=f32)


def fold(x):
    return jnp.sum(x.reshape(x.shape[0] // 8, 8, x.shape[1]), axis=0)


def mean(x):
    return jnp.mean(x, axis=-1, keepdims=True)


def exact(a, b, i, j):
    return lax.dot_general(
        a, b, (((i,), (j,)), ((), ())), precision=highest, preferred_element_type=f32
    )


def chosen(place, count, width):
    own = count // place.sub
    entry = lax.broadcasted_iota(jnp.int32, (count, width), 0)
    column = lax.broadcasted_iota(jnp.int32, (count, width), 1)
    low = lax.div(entry, own)
    home = (place.place * place.sub + low) * lax.axis_size("tp") + lax.axis_index("tp")
    return jnp.where(column == home * own + lax.rem(entry, own), 1.0, 0.0)


PAIR = 2 * HD
TOP = math.sqrt(2.0 / math.pi)


def layer_kernel(sub, names, *refs):
    k = types.SimpleNamespace(**dict(zip(names, refs, strict=True)))
    place = Place(sub)
    side = lax.axis_index("tp")
    x_ref = k.rows_in
    total_rows, width = x_ref.shape
    half = total_rows // 2
    tp_send, tp_recv = k.tp_send, k.tp_recv
    per = k.steps.shape[1]
    seqs = k.feats.shape[0]
    pairs = k.mixed.shape[1] // PAIR
    hidden_width = k.bup.shape[1]
    own0 = pl.multiple_of(side * half, half)
    far0 = pl.multiple_of((1 - side) * half, half)
    first_len = k.lengths[0, 0]
    both_len = first_len + k.lengths[0, 1]

    def segment(start, count):
        row = lax.broadcasted_iota(jnp.int32, (count, 1), 0) + start
        return jnp.where(row < first_len, 0, jnp.where(row < both_len, 1, 2))

    def swap(n, src, dst):
        return remote(src, dst, tp_send.at[n], tp_recv.at[n], place.other())

    def cut_of(j, part_index):
        return slice((3 * j + part_index) * PAIR, (3 * j + part_index + 1) * PAIR)

    def pair_of(j):
        return slice(j * PAIR, (j + 1) * PAIR)

    bring_x = pltpu.make_async_copy(k.x, x_ref, k.local.at[0])
    bring_cot = pltpu.make_async_copy(k.cot, k.cot_in, k.local.at[1])
    bring_x.start()
    bring_cot.start()
    for j in range(pairs):
        for n, source in enumerate((k.wq, k.wk, k.wv)):
            k.w0[:, cut_of(j, n)] = source[:, pair_of(j)].astype(bf16)
        k.bqkv[:, cut_of(j, 0)] = k.bq[pair_of(j)].reshape(1, PAIR)
        k.bqkv[:, cut_of(j, 1)] = jnp.zeros((1, PAIR), f32)
        k.bqkv[:, cut_of(j, 2)] = k.bv[pair_of(j)].reshape(1, PAIR)
    k.bup[...] = k.bu[...].reshape(1, hidden_width)
    k.w1[...] = k.wo[...].astype(bf16)
    k.w2[...] = k.wu[...].astype(bf16)
    k.w3[...] = k.wd[...].astype(bf16)
    at_row = (place.z * sub + place.low) * 2
    seq_row = lax.broadcasted_iota(jnp.int32, (seqs, 1), 0)
    step = jnp.zeros((seqs, 1), f32)
    for n in range(per):
        step = jnp.where(seq_row == place.z * per + n, k.steps[0, n].astype(f32), step)
    column = lax.broadcasted_iota(jnp.int32, (1, TE), 1)
    number = jnp.where(column < TE // 2, column, column - TE // 2).astype(f32)
    angle = step * jnp.exp(-math.log(10000.0) * number / (TE // 2))
    wave = jnp.where(column < TE // 2, jnp.cos(angle), jnp.sin(angle)).astype(bf16).astype(f32)
    mine = (seq_row >= place.z * per) & (seq_row < (place.z + 1) * per)
    k.feats[...] = jnp.where(mine, wave, 0.0)
    given = (k.v0, k.v1, k.v2, k.v3, k.v4, k.v5, k.v6)
    count = k.v0.shape[1]
    for n, source in enumerate(given):
        k.given[n : n + 1, :] = source[...]
    k.given[7:8, :] = jnp.zeros((1, count), f32)
    vectors = exact(k.given[...], chosen(place, count, width), 1, 0)

    place.enter()
    small_send, small_recv = k.small_send, k.small_recv
    low_part, high_part = slice(0, hidden_width - 512), slice(hidden_width - 512, hidden_width)
    gather_a, gather_b, gather_c, gather_d = [
        Gather(place, shard, full, part, k.g_send, k.g_recv, g)
        for g, (shard, full, part) in enumerate(
            (
                (k.w0, k.full0, slice(0, k.w0.shape[1])),
                (k.w1, k.full1, slice(0, k.w1.shape[1])),
                (k.w2, k.full2, slice(0, hidden_width)),
                (k.w3, k.full3, low_part),
            )
        )
    ]
    climb = Climb(place, k.w3, k.full3, high_part, k.g_send, k.g_recv, 4)
    top = slice(0, seqs + 8)
    part, in_plane, from_z = k.part, k.part_in, k.part_z
    shared = k.shared
    spread_z = Spread(place, "z", [k.feats] * 3, k.feat_z, small_send, small_recv, 0)
    spread_r = Spread(place, "r", [k.feat_sum] * 3, k.feat_in, small_send, small_recv, 3)
    back = Spread(
        place, "r", [part.at[n, top] for n in (3, 2, 1)], in_plane, small_send, small_recv, 6
    )
    over_z = Spread(place, "z", [k.part_sum.at[top]] * 3, from_z, small_send, small_recv, 9)
    pair = Spread(place, "tp", [k.part_zsum.at[top]], k.part_tp, small_send, small_recv, 12)

    def vector(n):
        return shared[n : n + 1, :]

    def base_of(start, count):
        seg = segment(start, count)
        added = jnp.where(
            seg == 0, k.embed[0:1, :], jnp.where(seg == 1, k.embed[1:2, :], 0.0)
        )
        return x_ref[pl.ds(start, count), :].astype(f32) + added

    def transpose(source, dest, first=0, last=width // 128):
        @pl.loop(first, last)
        def _(i):
            cut = pl.ds(pl.multiple_of(i * 128, 128), 128)
            dest[cut, :] = source[:, cut].T

    lane = lax.broadcasted_iota(jnp.int32, (1, PAIR), 1)
    lower = lane < HD
    scale = jnp.where(lax.broadcasted_iota(jnp.int32, (1, 3 * PAIR), 1) < PAIR, HD**-0.5, 1.0)
    qkv = k.qkv
    rows_at_once = 256

    def projection(j):
        cols = slice(3 * j * PAIR, 3 * (j + 1) * PAIR)

        @pl.loop(0, total_rows // 512)
        def _(i):
            rows = pl.ds(pl.multiple_of(i * 512, 512), 512)
            got = (mul(k.base[rows, :], k.full0[:, cols]) + k.bqkv[:, cols]) * scale
            qkv[rows, cols] = got.astype(bf16)

    def in_head(h):
        return lower if h == 0 else jnp.logical_not(lower)

    def with_mask(value, mask, h):
        return jnp.where(in_head(h), value.astype(f32), mask.astype(f32)).astype(bf16)

    def attend_start(j):
        for h in (0, 1):
            k.keys[h] = with_mask(qkv[:, cut_of(j, 1)], k.mask_k[...], h)

    def attend(j, first, last):
        @pl.loop(first, last)
        def _(i):
            rows = pl.ds(pl.multiple_of(i * rows_at_once, rows_at_once), rows_at_once)
            outs, logs = [], []
            for h in (0, 1):
                query = with_mask(qkv[rows, cut_of(j, 0)], k.mask_q[rows, :], h)
                scores = mul_t(query, k.keys[h])
                top = jnp.max(scores, axis=-1, keepdims=True)
                weight = jnp.exp(scores - top)
                total = jnp.sum(weight, axis=-1, keepdims=True)
                outs.append(mul(weight.astype(bf16), qkv[:, cut_of(j, 2)]) / total)
                logs.append(top + jnp.log(total))
            k.mixed[rows, j * PAIR : (j + 1) * PAIR] = jnp.where(lower, outs[0], outs[1]).astype(bf16)
            flipped = jnp.where(lower, logs[0], logs[1]).T
            k.lse_t[j, 0:1, rows] = flipped[0:1, :]
            k.lse_t[j, 1:2, rows] = flipped[HD : HD + 1, :]

    block = 256
    small = 128
    chunk = 512
    blocks = hidden_width // chunk
    own = pl.ds(own0, half)
    far = pl.ds(far0, half)
    first_own, normed_one, inv_one = k.first_own, k.normed_one, k.inv_one

    def rise(start, first, last):
        rows = pl.ds(start, half)

        @pl.loop(first, last)
        def _(i):
            cols = pl.ds(pl.multiple_of(i * chunk, chunk), chunk)
            up = mul(k.first[rows, :], k.full2[:, cols]) + k.bup[:, cols]
            square = up * up
            inner = up * (TOP + (TOP * 0.044715) * square)
            gate = 0.5 + 0.5 * jnp.tanh(inner)
            act = up * gate
            slope = gate + act * (1.0 - gate) * (2.0 * TOP + (6.0 * TOP * 0.044715) * square)
            k.act[rows, cols] = act.astype(bf16)
            k.slope[rows, cols] = slope.astype(bf16)

    spread_z.start()
    gather_c.own()
    gather_d.own()
    gather_b.begin()
    spread_z.wait()
    k.feat_sum[...] = k.feats[...] + k.feat_z[0] + k.feat_z[1] + k.feat_z[2]
    gather_b.turn(1)
    spread_r.start()
    k.all_feats[0] = k.feat_sum[...]
    gather_b.turn(2)
    gather_a.own()
    gather_a.begin()

    @pl.loop(0, total_rows // 128)
    def _(i):
        start = pl.multiple_of(i * 128, 128)
        seg = segment(start, 128)
        lane = lax.rem(lax.broadcasted_iota(jnp.int32, (1, PAIR), 1), HD)
        k.mask_k[pl.ds(start, 128), :] = jnp.where(lane == seg, 1.0, 0.0).astype(bf16)
        k.mask_q[pl.ds(start, 128), :] = jnp.where((lane < 3) & (lane != seg), -1e30, 0.0).astype(
            bf16
        )

    gather_b.pass_on(1)
    spread_r.wait()
    climb.begin()
    gather_b.pass_on(2)
    for d in (1, 2, 3):
        k.all_feats[d] = k.feat_in[d - 1]
    every = k.all_feats[...].reshape(4 * seqs, TE)
    before = mul_t(every.astype(bf16), k.tw1t[...].astype(bf16)) + k.tb1[...]
    hidden = jax.nn.silu(before).astype(bf16)
    share = mul(hidden, k.tw2[...].astype(bf16))
    for d in range(4):
        part[d, :seqs, :] = share[d * seqs : (d + 1) * seqs, :]
        part[d, seqs : seqs + 8, :] = vectors
    back.start()
    gather_b.own()
    gather_b.turn(3)
    back.wait()
    k.part_sum[top] = part[0, top] + in_plane[0, top] + in_plane[1, top] + in_plane[2, top]
    over_z.start()
    climb.pass_on()
    gather_a.turn(1)
    gather_a.turn(2)
    gather_a.turn(3)
    gather_c.begin()
    over_z.wait()
    k.part_zsum[top] = k.part_sum[top] + from_z[0, top] + from_z[1, top] + from_z[2, top]
    pair.start()
    gather_d.begin()
    pair.wait()
    both = k.part_zsum[top] + k.part_tp[top]
    shared[...] = both[seqs:]
    embed = both[:seqs] + shared[0:1, :]
    for s in (0, 1):
        k.embed[s : s + 1, :] = jnp.sum(
            jnp.where(seq_row == at_row + s, embed, 0.0), axis=0, keepdims=True
        )
    bring_x.wait()
    for one in (spread_z, spread_r, back, over_z, pair):
        one.drain()
    gather_a.pass_on(0)
    gather_a.pass_on(1)

    @pl.loop(0, total_rows // 128)
    def _(i):
        start = pl.multiple_of(i * 128, 128)
        k.base[pl.ds(start, 128), :] = base_of(start, 128).astype(bf16)

    transpose(k.base, k.base_t)
    gather_a.pass_on(2)
    gather_a.pass_on(3)
    gather_c.turn(1)
    gather_c.turn(2)
    gather_a.finish()
    projection(0)
    projection(1)
    projection(2)
    attend_start(0)
    attend(0, 0, 2)
    gather_c.turn(3)
    climb.rise()
    attend(0, 2, 4)
    gather_c.pass_on(2)
    attend_start(1)
    attend(1, 0, 1)
    gather_c.pass_on(1)
    attend(1, 1, 2)
    gather_b.pass_on(0)
    attend(1, 2, 3)
    gather_d.turn(1)
    attend(1, 3, 4)
    gather_b.pass_on(3)
    gather_d.turn(2)
    gather_c.pass_on(0)
    attend_start(2)
    attend(2, 0, 3)
    gather_d.pass_on(0)
    attend(2, 3, 4)
    gather_b.finish()
    gather_c.pass_on(3)
    gather_d.turn(3)

    @pl.loop(0, half // block)
    def _(i):
        rows = pl.ds(pl.multiple_of(far0 + i * block, block), block)
        k.half_send[pl.ds(pl.multiple_of(i * block, block), block), :] = mul_t(
            k.mixed[rows, :], k.full1[...]
        ).astype(bf16)

    swap_a = swap(0, k.half_send, k.half_recv)
    swap_a.start()

    @pl.loop(0, half // block)
    def _(i):
        here = pl.ds(pl.multiple_of(i * block, block), block)
        start = pl.multiple_of(own0 + i * block, block)
        first_own[here, :] = (
            base_of(start, block) + vector(1) + mul_t(k.mixed[pl.ds(start, block), :], k.full1[...])
        )

    swap_a.wait_recv()

    @pl.loop(0, half // small)
    def _(i):
        here = pl.ds(pl.multiple_of(i * small, small), small)
        summed = first_own[here, :] + k.half_recv[here, :].astype(f32)
        centered = summed - mean(summed)
        inv = lax.rsqrt(mean(centered * centered) + epsilon)
        normed = centered * inv
        first = normed * vector(2) + vector(3)
        first_own[here, :] = first
        normed_one[here, :] = normed
        inv_one[here, :] = jnp.broadcast_to(inv, (small, 128))
        k.first[pl.ds(pl.multiple_of(own0 + i * small, small), small), :] = first.astype(bf16)

    swap_b = swap(1, k.first.at[own, :], k.first.at[own, :])
    swap_b.start()
    gather_d.pass_on(1)
    gather_c.finish()
    rise(own0, 0, 1)
    gather_d.pass_on(2)
    rise(own0, 1, 2)
    gather_d.pass_on(3)
    rise(own0, 2, 3)
    swap_a.wait_send()
    swap_b.wait_recv()
    rise(far0, 0, 3)
    transpose(k.first, k.first_t, 0, 3)
    transpose(k.first, k.first_t, 3)
    gather_d.finish()
    climb.finish()
    bring_cot.wait()

    @pl.loop(0, half // block)
    def _(i):
        rows = pl.ds(pl.multiple_of(far0 + i * block, block), block)
        k.half_send[pl.ds(pl.multiple_of(i * block, block), block), :] = mul_t(
            k.act[rows, :], k.full3[...]
        ).astype(bf16)

    swap_c = swap(2, k.half_send, k.half_recv)
    swap_c.start()
    own_sum = first_own

    @pl.loop(0, half // block)
    def _(i):
        here = pl.ds(pl.multiple_of(i * block, block), block)
        rows = pl.ds(pl.multiple_of(own0 + i * block, block), block)
        own_sum[here, :] = mul_t(k.act[rows, :], k.full3[...]) + first_own[here, :] + vector(4)

    swap_c.wait_recv()
    swap_b.wait_send()
    acc = k.acc
    acc[...] = jnp.zeros_like(acc)

    @pl.loop(0, half // small)
    def _(i):
        here = pl.ds(pl.multiple_of(i * small, small), small)
        summed = own_sum[here, :] + k.half_recv[here, :].astype(f32)
        centered = summed - mean(summed)
        inv = lax.rsqrt(mean(centered * centered) + epsilon)
        normed = centered * inv
        k.out_stage[here, :] = (normed * vector(5) + vector(6)).astype(bf16)
        start = pl.multiple_of(own0 + i * small, small)
        grad = jnp.where(segment(start, small) < 2, k.cot_in[here, :].astype(f32), 0.0)
        scaled = grad * vector(5)
        second = inv * (scaled - mean(scaled) - normed * mean(scaled * normed))
        own_sum[here, :] = second
        k.base[pl.ds(start, small), :] = second.astype(bf16)
        acc[0] += fold(grad * normed)
        acc[1] += fold(grad)
        acc[2] += fold(second)

    send_out = pltpu.make_async_copy(k.out_stage, k.out, k.local.at[2])
    send_out.start()
    swap_d = swap(3, k.base.at[own, :], k.base.at[own, :])
    swap_d.start()
    acc_up = k.acc_up
    acc_up[...] = jnp.zeros_like(acc_up)

    def fall(start, first=0, last=blocks):
        rows = pl.ds(start, half)

        @pl.loop(first, last)
        def _(i):
            cols = pl.ds(pl.multiple_of(i * chunk, chunk), chunk)
            grad = mul(k.base[rows, :], k.full3[:, cols]) * k.slope[rows, cols].astype(f32)
            k.slope[rows, cols] = grad.astype(bf16)
            acc_up[:, cols] += fold(grad)

    descend = Descend(
        place, k.grad0, k.total0, slice(hidden_width - 512, hidden_width), k.deep, k.deep_far, k.deep_near,
        k.r_send, k.r_recv, 0,
    )
    summed_parts = [
        (0, slice(0, hidden_width - 512)),
        (1, slice(0, hidden_width // 2)),
        (1, slice(hidden_width // 2, hidden_width)),
        (2, slice(0, pairs * PAIR)),
    ] + [(3 + j, slice(0, 3 * PAIR)) for j in range(pairs)]
    sum_down, sum_up0, sum_up1, sum_out, *sum_pairs = [
        Reduce(
            place, many(k, "grad", g), many(k, "total", g), part,
            many(k, "near", n), many(k, "ring", n), many(k, "high", n), k.r_send, k.r_recv, 1 + n,
        )
        for n, (g, part) in enumerate(summed_parts)
    ]

    def weight_grad(dest, left_t, right, source_col, dest_col, count, step):
        @pl.loop(0, count // step)
        def _(i):
            to = pl.ds(pl.multiple_of(dest_col + i * step, 128), step)
            source = pl.ds(pl.multiple_of(source_col + i * step, 128), step)
            dest[:, to] = mul(left_t[...], right[:, source]).astype(bf16)

    fall(own0)
    swap_c.wait_send()
    swap_d.wait_recv()
    transpose(k.base, k.grad_t)
    grad_qkv = k.grad_qkv
    acc_qkv = k.acc_qkv
    split = hidden_width - 512

    def attend_back_start(j):
        mixed_cut = pair_of(j)
        for h in (0, 1):
            k.keys[h] = with_mask(qkv[:, cut_of(j, 0)], k.mask_q[...], h)
        product = k.grad_mixed[:, mixed_cut].astype(f32) * k.mixed[:, mixed_cut].astype(f32)
        flipped = product.T
        k.inner[0:1, :] = jnp.sum(flipped[:HD], axis=0, keepdims=True)
        k.inner[1:2, :] = jnp.sum(flipped[HD:], axis=0, keepdims=True)
        k.keys_t[...] = qkv[:, cut_of(j, 1)].T
        k.query_t[...] = jnp.zeros_like(k.query_t)

    def attend_back(j, first, last):
        mixed_cut = pair_of(j)

        @pl.loop(first, last)
        def one_block(i):
            start = pl.multiple_of(i * rows_at_once, rows_at_once)
            rows = pl.ds(start, rows_at_once)
            grads_v, grads_k, query_t = [], [], []
            for h in (0, 1):
                key = with_mask(qkv[rows, cut_of(j, 1)], k.mask_k[rows, :], h)
                prob = jnp.exp(mul_t(key, k.keys[h]) - k.lse_t[j, h : h + 1, :])
                value = jnp.where(in_head(h), qkv[rows, cut_of(j, 2)].astype(f32), 0.0).astype(bf16)
                grad_prob = mul_t(value, k.grad_mixed[:, mixed_cut])
                grad_score = (prob * (grad_prob - k.inner[h : h + 1, :])).astype(bf16)
                grads_v.append(mul(prob.astype(bf16), k.grad_mixed[:, mixed_cut]))
                grads_k.append(mul(grad_score, qkv[:, cut_of(j, 0)]))
                query_t.append(mul(k.keys_t[h * HD : (h + 1) * HD, rows], grad_score))
            grad_k = jnp.where(lower, grads_k[0], grads_k[1]).astype(bf16)
            grad_v = jnp.where(lower, grads_v[0], grads_v[1]).astype(bf16)
            grad_qkv[rows, cut_of(j, 1)] = grad_k
            grad_qkv[rows, cut_of(j, 2)] = grad_v
            k.query_t[...] += jnp.concatenate(query_t, axis=0)

    def attend_back_end(j):
        grad_qkv[:, cut_of(j, 0)] = (k.query_t[...].T * HD**-0.5).astype(bf16)
        cols = slice(3 * j * PAIR, 3 * (j + 1) * PAIR)
        acc_qkv[:, cols] = fold(grad_qkv[:, cols].astype(f32))
        weight_grad(many(k, "grad", 3 + j), k.base_t, grad_qkv, 3 * j * PAIR, 0, 3 * PAIR, 3 * PAIR)

    def row_of(x):
        return jnp.sum(x, axis=0, keepdims=True)

    early = slice(0, 16)
    late, late_sum = part.at[1, top], part.at[2, top]
    sums = part.at[0]
    pair_sums = Spread(place, "tp", [sums.at[early]], k.part_tp, small_send, small_recv, 13)
    sums_z = Spread(place, "z", [k.part_sum.at[early]] * 3, from_z, small_send, small_recv, 14)
    sums_r = Spread(place, "r", [k.part_zsum.at[early]] * 3, in_plane, small_send, small_recv, 17)
    late_z = Spread(place, "z", [late] * 3, k.late_z, small_send, small_recv, 20)
    late_r = Spread(place, "r", [late_sum] * 3, k.late_r, small_send, small_recv, 23)

    def early_sums():
        sums[early] = jnp.zeros((16, width), f32)
        for row, n in enumerate((5, 3, 4, 2, 0, 1)):
            sums[row : row + 1, :] = row_of(acc[n])
        up_row = row_of(acc_up[...])
        for n in range(hidden_width // width):
            sums[8 + n : 9 + n, :] = up_row[:, n * width : (n + 1) * width]
        pair_sums.start()

    def early_planes():
        pair_sums.wait()
        row = lax.broadcasted_iota(jnp.int32, (16, width), 0)
        k.part_sum[early] = sums[early] + jnp.where(row < 8, k.part_tp[early], 0.0)
        sums_z.start()

    def early_ring():
        sums_z.wait()
        k.part_zsum[early] = k.part_sum[early] + from_z[0, early] + from_z[1, early] + from_z[2, early]
        sums_r.start()

    def early_done():
        sums_r.wait()
        k.all_sums[early] = (
            k.part_zsum[early] + in_plane[0, early] + in_plane[1, early] + in_plane[2, early]
        )

    ge = k.acc_ge

    def late_planes():
        qkv_row = row_of(acc_qkv[...])
        late[:8] = jnp.zeros((8, width), f32)
        late[0:1, :] = qkv_row[:, :width]
        late[1:2, : qkv_row.shape[1] - width] = qkv_row[:, width:]
        late[8:, :] = jnp.where(
            seq_row == at_row, row_of(ge[0]), jnp.where(seq_row == at_row + 1, row_of(ge[1]), 0.0)
        )
        late_z.start()

    def late_ring():
        late_z.wait()
        late_sum[...] = late[...] + k.late_z[0] + k.late_z[1] + k.late_z[2]
        late_r.start()
        k.all_embed[0] = late_sum[8:]

    def late_done():
        late_r.wait()
        k.all_sums[16:] = late_sum[:8] + k.late_r[0, :8] + k.late_r[1, :8] + k.late_r[2, :8]
        for d in (1, 2, 3):
            k.all_embed[d] = k.late_r[d - 1, 8:]

    in_send, in_recv = k.act.at[:, :width], k.act.at[:, width : 2 * width]

    def back_far(first, last):
        @pl.loop(first, last)
        def _(i):
            rows = pl.ds(pl.multiple_of(far0 + i * block, block), block)
            k.half_send[pl.ds(pl.multiple_of(i * block, block), block), :] = mul_t(
                k.slope[rows, :], k.full2[...]
            ).astype(bf16)

    def back_own(first, last):
        @pl.loop(first, last)
        def _(i):
            here = pl.ds(pl.multiple_of(i * block, block), block)
            rows = pl.ds(pl.multiple_of(own0 + i * block, block), block)
            own_sum[here, :] += mul_t(k.slope[rows, :], k.full2[...])

    def in_grad(base):
        @pl.loop(0, half // block)
        def _(i):
            rows = pl.ds(pl.multiple_of(base + i * block, block), block)
            in_send[rows, :] = mul_t(grad_qkv[rows, :], k.full0[...]).astype(bf16)

    def settle(stage, base):
        @pl.loop(0, half // small)
        def _(i):
            start = pl.multiple_of(base + i * small, small)
            rows = pl.ds(start, small)
            grad = (in_send[rows, :].astype(f32) + in_recv[rows, :].astype(f32)) + k.first[
                rows, :
            ].astype(f32)
            stage[pl.ds(pl.multiple_of(i * small, small), small), :] = grad
            seg = segment(start, small)
            ge[0] += fold(jnp.where(seg == 0, grad, 0.0))
            ge[1] += fold(jnp.where(seg == 1, grad, 0.0))

    def swap_in(n):
        rows = pl.ds(n * half, half)
        return swap(6 + n, in_send.at[rows, :], in_recv.at[rows, :])

    def keep_in(n, stage):
        return pltpu.make_async_copy(stage, k.grad_in.at[pl.ds(n * half, half), :], k.local.at[3 + n])

    ge[...] = jnp.zeros_like(ge)
    weight_grad(k.grad0, k.grad_t, k.act, split, split, 512, 256)
    descend.begin()
    weight_grad(k.grad0, k.grad_t, k.act, 0, 0, split, 256)
    sum_down.far()
    fall(far0, 0, 3)
    back_far(0, 1)
    back_far(1, 2)
    swap_e = swap(4, k.half_send, k.half_recv)
    swap_e.start()
    back_own(0, 1)
    sum_down.raw()
    back_own(1, 2)
    sum_down.join()
    swap_e.wait_recv()

    @pl.loop(0, half // small)
    def _(i):
        here = pl.ds(pl.multiple_of(i * small, small), small)
        grad = own_sum[here, :] + k.half_recv[here, :].astype(f32)
        normed = normed_one[here, :]
        scaled = grad * vector(2)
        r1 = inv_one[here, 0:1] * (scaled - mean(scaled) - normed * mean(scaled * normed))
        k.first[pl.ds(pl.multiple_of(own0 + i * small, small), small), :] = r1.astype(bf16)
        acc[3] += fold(grad * normed)
        acc[4] += fold(grad)
        acc[5] += fold(r1)

    swap_f = swap(5, k.first.at[own, :], k.first.at[own, :])
    swap_f.start()
    weight_grad(k.grad1, k.first_t, k.slope, 0, 0, hidden_width // 2, 256)
    sum_up0.far()
    sum_up0.raw()
    weight_grad(k.grad1, k.first_t, k.slope, hidden_width // 2, hidden_width // 2, hidden_width // 2, 256)
    swap_f.wait_recv()
    sum_up1.far()

    @pl.loop(0, total_rows // 512)
    def _(i):
        rows = pl.ds(pl.multiple_of(i * 512, 512), 512)
        k.grad_mixed[rows, :] = mul(k.first[rows, :], k.full1[...]).astype(bf16)

    transpose(k.first, k.grad_t)
    weight_grad(k.grad2, k.grad_t, k.mixed, 0, 0, pairs * PAIR, pairs * PAIR)
    attend_back_start(0)
    attend_back(0, 0, 1)
    sum_down.cross()
    attend_back(0, 1, 2)
    early_sums()
    attend_back(0, 2, 4)
    early_planes()
    attend_back_end(0)
    sum_up0.join()
    sum_up1.raw()
    attend_back_start(1)
    attend_back(1, 0, 2)
    sum_pairs[0].far()
    sum_up1.join()
    attend_back(1, 2, 3)
    sum_up0.cross()
    attend_back(1, 3, 4)
    attend_back_end(1)
    sum_pairs[1].far()
    attend_back_start(2)
    attend_back(2, 0, 1)
    sum_pairs[1].raw()
    attend_back(2, 1, 3)
    sum_up1.cross()
    attend_back(2, 3, 4)
    attend_back_end(2)
    sum_pairs[2].far()
    sum_pairs[2].raw()
    sum_pairs[2].join()
    sum_pairs[0].join()
    sum_pairs[0].raw()
    in_grad(0)
    swap_g = swap_in(0)
    swap_g.start()
    sum_pairs[1].join()
    in_grad(half)
    sum_pairs[2].cross()
    swap_h = swap_in(1)
    swap_h.start()
    sum_down.finish()
    descend.arrive()
    swap_g.wait_recv()
    sum_out.far()
    sum_out.raw()
    settle(first_own, 0)
    keep_g = keep_in(0, first_own)
    keep_g.start()
    sum_pairs[0].cross()
    sum_pairs[1].cross()
    swap_h.wait_recv()
    descend.join()
    settle(normed_one, half)
    keep_h = keep_in(1, normed_one)
    keep_h.start()
    sum_up0.finish()
    late_planes()
    sum_pairs[2].finish()
    sum_up1.finish()
    sum_out.join()
    sum_pairs[1].finish()
    descend.finish()
    sum_out.cross()
    sum_pairs[0].finish()
    early_ring()
    late_ring()
    sum_out.finish()
    early_done()
    late_done()
    for one in (
        gather_a, gather_b, gather_c, gather_d, climb, descend, sum_down, sum_up0, sum_up1, sum_out,
        *sum_pairs, pair_sums, sums_z, sums_r, late_z, late_r,
    ):
        one.drain()
    send_out.wait()
    keep_g.wait()
    keep_h.wait()
    for copy in (swap_d, swap_e, swap_f, swap_g, swap_h):
        copy.wait_send()


def call_layer(sub, operands):
    rows, width = operands["x"].shape
    half = rows // 2
    mine, heads = operands["wo"].shape
    hidden = operands["bu"].shape[0]
    pairs = heads // PAIR
    seqs = 8 * sub
    count = operands["v0"].shape[1]
    tall = seqs + 16
    columns = [hidden, hidden, heads] + [3 * PAIR] * pairs
    shape = jax.ShapeDtypeStruct
    results = dict(
        out=shape((half, width), bf16),
        grad_in=shape((rows, width), f32),
        all_feats=shape((4, seqs, TE), f32),
        all_sums=shape((24, width), f32),
        all_embed=shape((4, seqs, width), f32),
    )
    for g, wide in enumerate(columns):
        results["total" + str(g)] = shape((mine, wide), f32)
    vm = pltpu.VMEM
    sem = pltpu.SemaphoreType.DMA
    scratch = dict(
        rows_in=vm((rows, width), bf16),
        cot_in=vm((half, width), bf16),
        out_stage=vm((half, width), bf16),
        w0=vm((mine, 3 * heads), bf16),
        w1=vm((mine, heads), bf16),
        w2=vm((mine, hidden), bf16),
        w3=vm((mine, hidden), bf16),
        bqkv=vm((1, 3 * heads), f32),
        bup=vm((1, hidden), f32),
        feats=vm((seqs, TE), f32),
        given=vm((8, count), f32),
        deep=vm((4, 4 * mine, 512), bf16),
        deep_far=vm((mine, 512), bf16),
        deep_near=vm((2, mine, 512), bf16),
        late_z=vm((3, seqs + 8, width), f32),
        late_r=vm((3, seqs + 8, width), f32),
        local=sem((5,)),
        full0=vm((width, 3 * heads), bf16),
        full1=vm((width, heads), bf16),
        full2=vm((width, hidden), bf16),
        full3=vm((width, hidden), bf16),
        feat_z=vm((3, seqs, TE), f32),
        feat_sum=vm((seqs, TE), f32),
        feat_in=vm((3, seqs, TE), f32),
        part=vm((4, tall, width), f32),
        part_in=vm((3, tall, width), f32),
        part_sum=vm((tall, width), f32),
        part_z=vm((3, tall, width), f32),
        part_zsum=vm((tall, width), f32),
        part_tp=vm((tall, width), f32),
        shared=vm((8, width), f32),
        embed=vm((8, width), f32),
        base=vm((rows, width), bf16),
        base_t=vm((width, rows), bf16),
        mask_q=vm((rows, PAIR), bf16),
        mask_k=vm((rows, PAIR), bf16),
        keys=vm((2, rows, PAIR), bf16),
        qkv=vm((rows, 3 * heads), bf16),
        mixed=vm((rows, heads), bf16),
        lse_t=vm((pairs, 8, rows), f32),
        half_send=vm((half, width), bf16),
        half_recv=vm((half, width), bf16),
        first_own=vm((half, width), f32),
        normed_one=vm((half, width), f32),
        inv_one=vm((half, 128), f32),
        first=vm((rows, width), bf16),
        first_t=vm((width, rows), bf16),
        act=vm((rows, hidden), bf16),
        slope=vm((rows, hidden), bf16),
        acc=vm((6, 8, width), f32),
        acc_up=vm((8, hidden), f32),
        acc_qkv=vm((8, 3 * heads), f32),
        acc_ge=vm((2, 8, width), f32),
        grad_t=vm((width, rows), bf16),
        grad_mixed=vm((rows, heads), bf16),
        inner=vm((8, rows), f32),
        keys_t=vm((PAIR, rows), bf16),
        query_t=vm((PAIR, rows), f32),
        grad_qkv=vm((rows, 3 * heads), bf16),
        g_send=sem((5, 16)),
        g_recv=sem((5, 16)),
        r_send=sem((5 + pairs, 16)),
        r_recv=sem((5 + pairs, 16)),
        small_send=sem((26,)),
        small_recv=sem((26,)),
        tp_send=sem((8,)),
        tp_recv=sem((8,)),
    )
    for g, wide in enumerate(columns):
        scratch["grad" + str(g)] = vm((width, wide), bf16)
    parts = [hidden - 512, hidden // 2, hidden // 2, heads] + [3 * PAIR] * pairs
    for n, wide in enumerate(parts):
        scratch["near" + str(n)] = vm((4, mine, wide), bf16)
        scratch["ring" + str(n)] = vm((8, mine, wide), bf16)
        scratch["high" + str(n)] = vm((4, mine, wide), bf16)
    names = [*operands, *results, *scratch]
    spaces = dict(lengths=pltpu.SMEM, steps=pltpu.SMEM, x=pl.ANY, cot=pl.ANY, out=pl.ANY, grad_in=pl.ANY)
    spec = lambda n: pl.BlockSpec(memory_space=spaces.get(n, pltpu.VMEM))
    got = pl.pallas_call(
        functools.partial(layer_kernel, sub, names),
        out_shape=list(results.values()),
        in_specs=[spec(n) for n in operands],
        out_specs=[spec(n) for n in results],
        scratch_shapes=list(scratch.values()),
        compiler_params=pltpu.CompilerParams(
            collective_id=0, has_side_effects=True, vmem_limit_bytes=63_000 * 1024
        ),
        name="layer",
    )(*operands.values())
    return types.SimpleNamespace(**dict(zip(results, got, strict=True)))


def finish_kernel(dp_size, names, *refs):
    k = types.SimpleNamespace(**dict(zip(names, refs, strict=True)))
    rows = k.grad_from.shape[0] // 4
    moves = [(k.out_from, k.out_held, k.out)]
    for n in range(4):
        here = slice(n * rows, (n + 1) * rows)
        moves.append((k.grad_from.at[here], k.grad_held.at[here], k.grad_in.at[here]))
    fetch = [pltpu.make_async_copy(a, b, k.local.at[n]) for n, (a, b, _) in enumerate(moves)]
    store = [pltpu.make_async_copy(b, c, k.local.at[5 + n]) for n, (_, b, c) in enumerate(moves)]
    for copy in fetch:
        copy.start()
    feats, embeds = k.feats[...], k.embeds[...]
    before = mul_t(feats.astype(bf16), k.tw1t[...].astype(bf16)) + k.tb1[...]
    gate = jax.nn.sigmoid(before)
    hidden = (before * gate).astype(bf16).astype(f32)
    grad_hidden = exact(embeds, k.tw2[...].astype(bf16).astype(f32), 1, 1)
    for first, then in zip(fetch, store, strict=True):
        first.wait()
        then.start()
    grad_before = grad_hidden * (gate * (1.0 + before * (1.0 - gate)))
    k.g_tw2[...] = exact(hidden, embeds, 0, 0)
    k.g_tw1t[...] = exact(grad_before, feats, 0, 0)
    k.g_tb1[...] = jnp.sum(grad_before, axis=0, keepdims=True)
    sums = k.sums[...]
    width = sums.shape[1]
    row = lax.broadcasted_iota(jnp.int32, (8, 1), 0)
    vectors = jnp.where(row == 6, jnp.sum(embeds, axis=0, keepdims=True), sums[:8])
    count = k.tb1.shape[1]
    start = (lax.axis_index("dp") * lax.axis_size("tp") + lax.axis_index("tp")) * count
    entry = lax.broadcasted_iota(jnp.int32, (count, width), 0)
    column = lax.broadcasted_iota(jnp.int32, (count, width), 1)
    picked = exact(vectors, jnp.where(column == start + entry, 1.0, 0.0), 1, 1)
    for n, dest in enumerate((k.g_bout, k.g_g1, k.g_s1, k.g_bdown, k.g_g2, k.g_s2, k.g_tb2)):
        dest[...] = picked[n : n + 1, :]
    hidden_width = k.g_bup.shape[0]
    for n in range(hidden_width // width):
        k.g_bup[n * width : (n + 1) * width] = sums[8 + n, :]
    at = 16
    pairs = k.g_bq.shape[0] // PAIR
    for j in range(pairs):
        here = slice(j * PAIR, (j + 1) * PAIR)
        source = many(k, "pair", j)
        for n, dest in enumerate((k.g_wq, k.g_wk, k.g_wv)):
            dest[:, here] = source[:, n * PAIR : (n + 1) * PAIR]
        for n, dest in ((0, k.g_bq), (2, k.g_bv)):
            first = (3 * j + n) * PAIR
            dest[here] = sums[at + first // width, first % width : first % width + PAIR]
    k.g_wo[...] = k.sum_out[...]
    k.g_wu[...] = k.sum_up[...]
    k.g_wd[...] = k.sum_down[...]
    for copy in store:
        copy.wait()


def call_finish(dp_size, operands, hidden):
    shape = jax.ShapeDtypeStruct
    own = operands["tb1"].shape[1]
    width = operands["sums"].shape[1]
    mine, heads = operands["sum_out"].shape
    line = shape((1, own), f32)
    matrix = shape((mine, heads), f32)
    wide = shape((mine, hidden), f32)
    results = dict(
        out=shape(operands["out_from"].shape, bf16),
        grad_in=shape(operands["grad_from"].shape, f32),
        g_tw1t=shape((own, TE), f32),
        g_tb1=line,
        g_tw2=shape((own, width), f32),
        g_tb2=line,
        g_wq=matrix,
        g_bq=shape((heads,), f32),
        g_wk=matrix,
        g_wv=matrix,
        g_bv=shape((heads,), f32),
        g_wo=matrix,
        g_bout=line,
        g_g1=line,
        g_s1=line,
        g_wu=wide,
        g_bup=shape((hidden,), f32),
        g_wd=wide,
        g_bdown=line,
        g_g2=line,
        g_s2=line,
    )
    scratch = dict(
        out_held=pltpu.VMEM(operands["out_from"].shape, bf16),
        grad_held=pltpu.VMEM(operands["grad_from"].shape, f32),
        local=pltpu.SemaphoreType.DMA((10,)),
    )
    names = [*operands, *results, *scratch]
    spaces = dict(out_from=pl.ANY, grad_from=pl.ANY, out=pl.ANY, grad_in=pl.ANY)
    spec = lambda n: pl.BlockSpec(memory_space=spaces.get(n, pltpu.VMEM))
    got = pl.pallas_call(
        functools.partial(finish_kernel, dp_size, names),
        out_shape=list(results.values()),
        in_specs=[spec(n) for n in operands],
        out_specs=[spec(n) for n in results],
        scratch_shapes=list(scratch.values()),
        compiler_params=pltpu.CompilerParams(vmem_limit_bytes=61_000 * 1024),
        name="finish",
    )(*operands.values())
    return types.SimpleNamespace(**dict(zip(results, got, strict=True)))


def on_device(
    inputs, cotangent, seq_lengths, timesteps, time_w1, time_b1, time_w2, time_b2,
    w_query, b_query, w_key, w_value, b_value, w_out, b_out, norm1_gain, norm1_bias,
    w_up, b_up, w_down, b_down, norm2_gain, norm2_bias,
):
    dp = lax.axis_size("dp")
    sub = dp // SUPER
    low = [[q * sub + l for l in range(sub)] for q in range(SUPER)]
    head_width = w_query.shape[1]

    def near(value, axis=0):
        if sub == 1:
            return value
        return lax.all_gather(value, "dp", axis=axis, tiled=True, axis_index_groups=low)

    def line(value):
        return near(value)[None, :]

    steps = timesteps
    if sub > 1:
        steps = near(timesteps.astype(f32)).astype(jnp.int32).reshape(1, -1)
    got = call_layer(
        sub,
        dict(
            lengths=seq_lengths,
            steps=steps,
            x=inputs,
            cot=cotangent,
            wq=near(w_query),
            wk=near(w_key),
            wv=near(w_value),
            wo=near(w_out.T),
            wu=near(w_up),
            wd=near(w_down.T),
            bq=b_query,
            bv=b_value,
            bu=b_up,
            tw1t=near(time_w1.T),
            tb1=line(time_b1),
            tw2=near(time_w2),
            v0=line(time_b2),
            v1=line(b_out),
            v2=line(norm1_gain),
            v3=line(norm1_bias),
            v4=line(b_down),
            v5=line(norm2_gain),
            v6=line(norm2_bias),
        ),
    )
    sums, embeds, feats = got.all_sums, got.all_embed, got.all_feats
    pairs = head_width // PAIR
    totals = [many(got, "total", g) for g in range(3 + pairs)]
    if sub > 1:
        sums, embeds = lax.psum((sums, embeds), "dp", axis_index_groups=low)
        totals = [
            lax.psum_scatter(one, "dp", scatter_dimension=0, tiled=True, axis_index_groups=low)
            for one in totals
        ]
    operands = dict(
        out_from=got.out,
        grad_from=got.grad_in,
        sums=sums,
        embeds=embeds.reshape(-1, embeds.shape[-1]),
        feats=feats.reshape(-1, TE),
        tw1t=time_w1.T,
        tb1=time_b1[None, :],
        tw2=time_w2,
        sum_down=totals[0],
        sum_up=totals[1],
        sum_out=totals[2],
    )
    for j in range(pairs):
        operands["pair" + str(j)] = totals[3 + j]
    done = call_finish(dp, operands, b_up.shape[0])
    return (
        done.out,
        done.grad_in,
        done.g_tw1t.T,
        done.g_tb1[0],
        done.g_tw2,
        done.g_tb2[0],
        done.g_wq,
        done.g_bq,
        done.g_wk,
        done.g_wv,
        done.g_bv,
        done.g_wo.T,
        done.g_bout[0],
        done.g_g1[0],
        done.g_s1[0],
        done.g_wu,
        done.g_bup,
        done.g_wd.T,
        done.g_bdown[0],
        done.g_g2[0],
        done.g_s2[0],
    )


def solution(mesh):
    placed = (
        P("dp", None),
        P(("dp", "tp"), None),
        P("dp", None),
        P("dp", None),
        P(None, ("dp", "tp")),
        P(("dp", "tp")),
        P(("dp", "tp"), None),
        P(("dp", "tp")),
        P("dp", "tp"),
        P("tp"),
        P("dp", "tp"),
        P("dp", "tp"),
        P("tp"),
        P("tp", "dp"),
        P(("dp", "tp")),
        P(("dp", "tp")),
        P(("dp", "tp")),
        P("dp", "tp"),
        P("tp"),
        P("tp", "dp"),
        P(("dp", "tp")),
        P(("dp", "tp")),
        P(("dp", "tp")),
    )
    return jax.shard_map(
        on_device,
        mesh=mesh,
        in_specs=placed,
        out_specs=(
            P(("dp", "tp"), None),
            P("dp", None),
            P(None, ("dp", "tp")),
            P(("dp", "tp")),
            P(("dp", "tp"), None),
            P(("dp", "tp")),
            P("dp", "tp"),
            P("tp"),
            P("dp", "tp"),
            P("dp", "tp"),
            P("tp"),
            P("tp", "dp"),
            P(("dp", "tp")),
            P(("dp", "tp")),
            P(("dp", "tp")),
            P("dp", "tp"),
            P("tp"),
            P("tp", "dp"),
            P(("dp", "tp")),
            P(("dp", "tp")),
            P(("dp", "tp")),
        ),
        check_vma=False,
    )
```
